32 devices in a mesh: tiles: 4 (over y, core), coef: 8 (over z, x).
Axes of the slice: x: 2, y: 2, z: 4, core: 2. Of those that a mesh axis runs over, the one named last changes fastest.
Arguments:
- fields: bfloat16 [256, 2048], P('coef', 'tiles'), may hold values from -6 to 6
- adjoints: bfloat16 [256, 2048], P('coef', 'tiles'), may hold values from -6 to 6
- couple: bfloat16 [30, 256, 256], replicated, may hold values from -0.0625 to 0.0625
- tmatrices: bfloat16 [16, 256, 256], P('tiles', 'coef'), may hold values from -0.375 to 0.375
- neighbours: int32 [2048, 30], P('tiles'), may hold values from -1 to 2047, as said below
- classes: int32 [2048], P('tiles'), may hold values from 0 to 15
Outputs:
- forward_out: bfloat16 [256, 2048], P('coef', 'tiles')
- adjoint_out: bfloat16 [256, 2048], P('coef', 'tiles')
The draws below stay inside these ranges and needn't reach their ends.
Inputs may be any that keep to these rules, and one draw needn't show every extreme that they name: neighbours[i, m] is -1 or i + m - 15 for m < 15, or i + m - 14 for m >= 15; links are mutual: neighbours[i, m] = j >= 0 exactly when neighbours[j, 29 - m] = i; slots 15 - 1 and 15 are filled wherever the neighbouring pillar exists.
All inputs are finite; a program needn't handle non-finite values.
Results may differ from the reference program's by a relative error of at most 0.0037.
Values may be sent and summed in bfloat16 or wider, within the bound.
No kernel may reach another device: no remote copies, remote signals or barrier semaphores. Data moves between devices by JAX's collectives and lax.ppermute only.
A program may use at most 64 MiB of HBM per device.

```python
import jax
import jax.numpy as jnp
from jax import lax

KR = 256
SLOTS = 30
HW = 15
PILLARS = 2048
CLASSES = 16


def draw_neighbours(key, part):
    link_bits = jax.random.randint(key, (PILLARS, HW), 0, 5)
    keep_link = link_bits < 4
    keep_link = keep_link.at[:, 0].set(True)
    slot_ids = jnp.arange(SLOTS, dtype=jnp.int32)
    offsets = jnp.where(slot_ids < HW, slot_ids - HW, slot_ids - HW + 1)
    pillar_ids = jnp.arange(PILLARS, dtype=jnp.int32)[:, None]
    targets = pillar_ids + offsets[None, :]
    lower = jnp.clip(jnp.minimum(pillar_ids, targets), 0, PILLARS - 1)
    distance = jnp.abs(offsets)[None, :] - 1
    inside = (targets >= 0) & (targets < PILLARS)
    kept = keep_link[lower, distance]
    return jnp.where(inside & kept, targets, -1).astype(jnp.int32)


def set_ends(drawn, own_key, least, top_value):
    longest = drawn.shape.index(max(drawn.shape))
    spots = []
    for shift in (0, 1):
        where = [jax.random.randint(jax.random.fold_in(own_key, axis), (), 0, length) for axis, length in enumerate(drawn.shape)]
        where[longest] = (where[longest] + shift) % drawn.shape[longest]
        spots.append(tuple(where))
    return drawn.at[spots[0]].set(least).at[spots[1]].set(top_value)


def levels(own_key, dims, split, smallest, largest):
    factor_of, own = 1.0, jax.random.fold_in(own_key, 6)
    for axis_at, blocks in split:
        heights = jnp.exp(jax.random.uniform(jax.random.fold_in(own, axis_at), (blocks,), jnp.float32, smallest / len(split), largest / len(split)))
        factor_of = factor_of * jnp.repeat(heights, dims[axis_at] // blocks).reshape([-1 if axis == axis_at else 1 for axis in range(len(dims))])
    return factor_of


def normal_values(rng, shape, deviation, bound, split=(), held_as=jnp.bfloat16):
    array = deviation * jax.random.normal(rng, shape, jnp.float32)
    if split:
        array = array * levels(rng, shape, split, -0.22, 0.18)
    return jnp.clip(array, -bound, bound).astype(held_as)


def setup_inputs(seed: int = 0) -> dict:
    splits = jax.random.split(jax.random.key(seed), 7)
    return {
        "fields": normal_values(splits[0], (KR, PILLARS), 1.0, 6.0, ((0, 8), (1, 4))),
        "adjoints": normal_values(splits[1], (KR, PILLARS), 1.0, 6.0, ((0, 8), (1, 4))),
        "couple": normal_values(splits[2], (SLOTS, KR, KR), (SLOTS * KR) ** -0.5, 0.0625),
        "tmatrices": normal_values(splits[3], (CLASSES, KR, KR), KR ** -0.5, 0.375, ((0, 4), (1, 8))),
        "neighbours": draw_neighbours(jax.random.fold_in(splits[6], 71), 0),
        "classes": set_ends(jax.random.randint(splits[5], (PILLARS,), 0, CLASSES), jax.random.fold_in(splits[5], 1), 0, CLASSES - 1).astype(jnp.int32),
    }


def pair_sum(source, couple, slot_index, slot_weight, adjoint_mode):
    def accumulate(running, slot_id):
        selected = jnp.take(source, slot_index[:, slot_id], axis=1) * slot_weight[:, slot_id][None, :]
        if adjoint_mode:
            matrix = lax.dynamic_index_in_dim(couple, SLOTS - 1 - slot_id, 0, keepdims=False).T
        else:
            matrix = lax.dynamic_index_in_dim(couple, slot_id, 0, keepdims=False)
        return running + jnp.dot(matrix, selected, preferred_element_type=jnp.float32), None

    start_sum = jnp.zeros((KR, PILLARS), jnp.float32)
    result, unused = lax.scan(accumulate, start_sum, jnp.arange(SLOTS, dtype=jnp.int32))
    return result


def class_apply(vectors, tmatrices, classes, adjoint_mode):
    block_len = 32
    count_blocks = PILLARS // block_len
    shaped = vectors.astype(jnp.float32).reshape(KR, count_blocks, block_len).transpose(1, 0, 2)
    grouped = classes.reshape(count_blocks, block_len)

    def one_block(inputs):
        labels, values = inputs
        matrices = jnp.take(tmatrices, labels, axis=0).astype(jnp.float32)
        if adjoint_mode:
            return jnp.einsum("irk,ri->ki", matrices, values)
        return jnp.einsum("irk,ki->ri", matrices, values)

    output = lax.map(one_block, (grouped, shaped))
    return output.transpose(1, 0, 2).reshape(KR, PILLARS)


def reference(fields, adjoints, couple, tmatrices, neighbours, classes):
    is_valid = neighbours >= 0
    slot_index = jnp.where(is_valid, neighbours, 0).astype(jnp.int32)
    slot_weight = is_valid.astype(fields.dtype)
    coupled = pair_sum(fields, couple, slot_index, slot_weight, False).astype(jnp.bfloat16)
    forward_out = (fields.astype(jnp.float32) - class_apply(coupled, tmatrices, classes, False)).astype(jnp.bfloat16)
    scattered = class_apply(adjoints, tmatrices, classes, True).astype(jnp.bfloat16)
    adjoint_out = (adjoints.astype(jnp.float32) - pair_sum(scattered, couple, slot_index, slot_weight, True)).astype(jnp.bfloat16)
    return forward_out, adjoint_out
```

```python
import functools

import jax
import jax.numpy as jnp
from jax import lax
from jax.experimental import pallas as pl
from jax.experimental.pallas import tpu as pltpu
from jax.sharding import PartitionSpec as P

SLOTS = 30
HW = 15
EDGE = 128
CHUNK = 3
OFFSETS = [slot - HW + (1 if slot >= HW else 0) for slot in range(SLOTS)]
BF16 = jnp.bfloat16
F32 = jnp.float32
VMEM = pl.BlockSpec(memory_space=pltpu.VMEM)
SMEM = pl.BlockSpec(memory_space=pltpu.SMEM)
ANY = pl.BlockSpec(memory_space=pl.ANY)
PARAMS = pltpu.CompilerParams(vmem_limit_bytes=32 * 1024 * 1024)


def edges_of(cells):
    width = cells.shape[1]
    head, tail = cells[:, :EDGE], cells[:, width - EDGE :]
    lane = lax.broadcasted_iota(jnp.int32, head.shape, 1)
    return jnp.where(lane < EDGE // 2, head, tail)


def pack_kernel(t_ref, f_ref, a_ref, class_ref, near_ref, far_ref):
    count, rows, depth = t_ref.shape
    mats = count * rows
    width = f_ref.shape[1]
    fields, adjoints = f_ref[...], a_ref[...]
    class_edge = edges_of(class_ref[...]).astype(F32).astype(BF16)
    class_rows = jnp.broadcast_to(class_edge, (16, EDGE))
    for out_ref in (near_ref, far_ref):
        out_ref[:mats, :] = t_ref[...].reshape(mats, depth)
        out_ref[mats : mats + rows, :EDGE] = edges_of(fields)
        out_ref[mats : mats + rows, EDGE : 2 * EDGE] = edges_of(adjoints)
        out_ref[mats + rows : mats + rows + 16, :EDGE] = class_rows
        out_ref[mats + rows : mats + rows + 16, EDGE : 2 * EDGE] = class_rows
    base = mats + rows + 16
    for part in range(width // depth):
        lanes = slice(part * depth, (part + 1) * depth)
        far_ref[base + 2 * part * rows : base + (2 * part + 1) * rows, :] = fields[:, lanes]
        far_ref[base + (2 * part + 1) * rows : base + (2 * part + 2) * rows, :] = adjoints[:, lanes]


def pick_halo(place, piece_refs, masks, row_slice, lane_slice):
    tile = place[0]
    shape = (row_slice.stop - row_slice.start, EDGE)
    lane = lax.broadcasted_iota(jnp.int32, shape, 1)
    above = jnp.zeros(shape, F32)
    below = jnp.zeros(shape, F32)
    for piece_ref, mask in zip(piece_refs, masks):
        cells = piece_ref[row_slice, lane_slice].astype(F32)
        owner = tile ^ mask
        above = jnp.where(owner == tile + 1, cells, above)
        below = jnp.where(owner == tile - 1, cells, below)
    return jnp.where(lane < EDGE // 2, above, below)


def own_and_far(place, own, far):
    odd = place[1] == 1
    own32, far32 = own.astype(F32), far.astype(F32)
    return jnp.where(odd, far32, own32).astype(BF16), jnp.where(odd, own32, far32).astype(BF16)


def fields_kernel(masks, count, place, f_ref, far_ref, *refs):
    half = len(masks)
    near, across, out_ref = refs[:half], refs[half : 2 * half], refs[-1]
    rows, width = f_ref.shape
    depth = far_ref.shape[1]
    mats = count * rows
    base = mats + rows + 16
    edge_rows = slice(mats, mats + rows)
    lanes = slice(0, EDGE)
    first = pl.multiple_of(place[1] * rows, rows)
    second = pl.multiple_of((1 - place[1]) * rows, rows)
    out_ref[pl.ds(first, rows), :width] = f_ref[...]
    out_ref[pl.ds(first, rows), width:] = pick_halo(place, near, masks, edge_rows, lanes).astype(BF16)
    for part in range(width // depth):
        out_ref[pl.ds(second, rows), part * depth : (part + 1) * depth] = far_ref[
            base + 2 * part * rows : base + (2 * part + 1) * rows, :
        ]
    out_ref[pl.ds(second, rows), width:] = pick_halo(place, across, masks, edge_rows, lanes).astype(BF16)


def start_chunks(couple_ref, held, sems):
    for chunk in range(SLOTS // CHUNK):
        span = pl.ds(chunk * CHUNK, CHUNK)
        pltpu.make_async_copy(couple_ref.at[span], held.at[span], sems.at[chunk]).start()


def wait_chunk(couple_ref, held, sems, chunk):
    span = pl.ds(chunk * CHUNK, CHUNK)
    pltpu.make_async_copy(couple_ref.at[span], held.at[span], sems.at[chunk]).wait()


def couple_all(source, weight_ref, couple_ref, held, sems, adjoint_mode):
    span = source.shape[1]
    width = weight_ref.shape[1]
    total = None
    for chunk in range(SLOTS // CHUNK):
        wait_chunk(couple_ref, held, sems, chunk)
        for mat in range(chunk * CHUNK, (chunk + 1) * CHUNK):
            slot = SLOTS - 1 - mat if adjoint_mode else mat
            moved = pltpu.roll(source, (-OFFSETS[slot]) % span, 1)[:, :width]
            selected = moved * weight_ref[slot : slot + 1, :]
            dims = (((0 if adjoint_mode else 1,), (0,)), ((), ()))
            product = lax.dot_general(held[mat], selected, dims, preferred_element_type=F32)
            total = product if total is None else total + product
    return total


def adjoint_kernel(
    masks, place, ids_ref, a_ref, far_ref, class_ref, weight_ref, couple_ref, *refs
):
    half = len(masks)
    near, across = refs[:half], refs[half : 2 * half]
    send_ref, keep_ref, total_ref, expanded, stacked, held, sems = refs[2 * half :]
    start_chunks(couple_ref, held, sems)
    rows, width = a_ref.shape
    depth = far_ref.shape[1]
    count = ids_ref.shape[0] // half
    mats = count * rows
    base = mats + rows + 16
    edge_rows = slice(mats, mats + rows)
    lanes = slice(EDGE, 2 * EDGE)
    far_own = jnp.concatenate(
        [
            far_ref[base + (2 * part + 1) * rows : base + (2 * part + 2) * rows, :]
            for part in range(width // depth)
        ],
        axis=1,
    )
    padded = [
        jnp.concatenate([own, pick_halo(place, pieces, masks, edge_rows, lanes).astype(BF16)], axis=1)
        for own, pieces in ((a_ref[...], near), (far_own, across))
    ]
    class_halo = pick_halo(place, near, masks, slice(mats + rows, mats + rows + 16), slice(0, EDGE))
    labels = jnp.concatenate(
        [class_ref[...], class_halo[0:1, :].astype(jnp.int32)], axis=1
    )
    zero = jnp.zeros((), BF16)
    at = 0
    for piece in range(half):
        for which, pieces in ((0, near), (1, across)):
            stacked[at : at + mats, :] = pieces[piece][:mats, :]
            for local_class in range(count):
                hit = labels == ids_ref[piece * count + local_class]
                factor = jnp.where(hit, 1.0, 0.0).astype(BF16)
                expanded[at : at + rows, :] = padded[which] * factor
                at += rows
    scattered = lax.dot_general(
        stacked[...], expanded[...], (((0,), (0,)), ((), ())), preferred_element_type=F32
    ).astype(BF16)
    total_ref[...] = couple_all(scattered, weight_ref, couple_ref, held, sems, True)
    steps = keep_ref.shape[0]
    for rel in range(steps):
        start = pl.multiple_of(((place[2] ^ rel) * 2 + place[1]) * rows, rows)
        keep_ref[rel] = total_ref[pl.ds(start, rows), :]
        start = pl.multiple_of(((place[2] ^ (rel + steps)) * 2 + place[1]) * rows, rows)
        send_ref[rel] = total_ref[pl.ds(start, rows), :].astype(BF16)


def forward_kernel(
    masks, rels, place, ids_ref, f_ref, class_ref, weight_ref, couple_ref, *refs
):
    half, parts = len(masks), len(rels)
    near, pieces = refs[:half], refs[half : half + parts]
    out_ref, padded, held, sems = refs[half + parts :]
    start_chunks(couple_ref, held, sems)
    rows, width = f_ref.shape
    count = ids_ref.shape[0] // half
    mats = count * rows
    block = 2 * rows
    for rel, piece_ref in zip(rels, pieces):
        start = pl.multiple_of((place[2] ^ rel) * block, block)
        padded[pl.ds(start, block), :] = piece_ref[...]
    coupled = couple_all(padded[...], weight_ref, couple_ref, held, sems, False).astype(BF16)
    applied = jnp.zeros((rows, width), F32)
    labels = class_ref[...]
    for piece in range(half):
        product = jnp.dot(near[piece][:mats, :], coupled, preferred_element_type=F32)
        for local_class in range(count):
            hit = labels == ids_ref[piece * count + local_class]
            applied = jnp.where(hit, product[local_class * rows : (local_class + 1) * rows, :], applied)
    out_ref[...] = (f_ref[...].astype(F32) - applied).astype(BF16)


def local(fields, adjoints, couple, tmatrices, neighbours, classes):
    tiles, coefs = lax.axis_size("tiles"), lax.axis_size("coef")
    tile, coef = lax.axis_index("tiles"), lax.axis_index("coef")
    rows, width = fields.shape
    count, unused, depth = tmatrices.shape
    place = jnp.stack([tile, coef % 2, coef // 2]).astype(jnp.int32)

    def swap(cells, tile_mask, coef_mask):
        pairs = [
            (i * coefs + j, (i ^ tile_mask) * coefs + (j ^ coef_mask))
            for i in range(tiles)
            for j in range(coefs)
        ]
        return lax.ppermute(cells, ("tiles", "coef"), pairs)

    weights = (neighbours >= 0).astype(BF16).T
    labels = classes.reshape(1, width)
    mats = count * rows
    near_rows = mats + rows + 16
    far_rows = near_rows + 2 * rows * (width // depth)
    near_own, far_own = pl.pallas_call(
        pack_kernel,
        out_shape=(
            jax.ShapeDtypeStruct((near_rows, depth), BF16),
            jax.ShapeDtypeStruct((far_rows, depth), BF16),
        ),
        in_specs=[VMEM] * 4,
        out_specs=(VMEM, VMEM),
        compiler_params=PARAMS,
    )(tmatrices, fields, adjoints, labels)

    top = tiles // 2
    far = swap(far_own, 0, 1)
    near = {0: near_own, top: swap(near_own, top, 0)}
    across = {0: far, top: swap(near_own, top, 1)}
    bit = top // 2
    while bit >= 1:
        for group in (near, across):
            for mask, piece in list(group.items()):
                source = piece[:near_rows] if group is across else piece
                group[mask ^ bit] = swap(source, bit, 0)
        bit //= 2
    masks = sorted(near)
    near_list = [near[mask] for mask in masks]
    across_list = [across[mask] for mask in masks]
    ids = (
        (tile ^ jnp.array(masks, jnp.int32))[:, None] * count + jnp.arange(count, dtype=jnp.int32)
    ).reshape(-1).astype(jnp.int32)

    padded_fields = pl.pallas_call(
        functools.partial(fields_kernel, masks, count),
        out_shape=jax.ShapeDtypeStruct((2 * rows, width + EDGE), BF16),
        in_specs=[SMEM] + [VMEM] * (2 + 2 * len(masks)),
        out_specs=VMEM,
        compiler_params=PARAMS,
    )(place, fields, far, *near_list, *across_list)

    groups = coefs // 2
    gathered = {0: padded_fields}
    bit = groups // 2
    while bit >= 1:
        for rel, piece in list(gathered.items()):
            gathered[rel ^ bit] = swap(piece, 0, 2 * bit)
        bit //= 2
    rels = sorted(gathered)

    held = pltpu.VMEM((SLOTS,) + couple.shape[1:], BF16)
    sems = pltpu.SemaphoreType.DMA((SLOTS // CHUNK,))
    steps = groups // 2
    total_rows = couple.shape[1]
    send, keep = pl.pallas_call(
        functools.partial(adjoint_kernel, masks),
        out_shape=(
            jax.ShapeDtypeStruct((steps, rows, width), BF16),
            jax.ShapeDtypeStruct((steps, rows, width), F32),
        ),
        in_specs=[SMEM, SMEM] + [VMEM] * 4 + [ANY] + [VMEM] * (2 * len(masks)),
        out_specs=(VMEM, VMEM),
        scratch_shapes=[
            pltpu.VMEM((total_rows, width), F32),
            pltpu.VMEM((2 * len(masks) * mats, width + EDGE), BF16),
            pltpu.VMEM((2 * len(masks) * mats, depth), BF16),
            held,
            sems,
        ],
        compiler_params=PARAMS,
    )(place, ids, adjoints, far, labels, weights, couple, *near_list, *across_list)

    bit = groups // 2
    while bit >= 1:
        arrived = swap(send, 0, 2 * bit)
        merged = keep + arrived.astype(F32)
        bit //= 2
        if bit >= 1:
            keep, send = merged[:bit], merged[bit:].astype(BF16)
    adjoint_out = (adjoints.astype(F32) - merged[0]).astype(BF16)

    forward_out = pl.pallas_call(
        functools.partial(forward_kernel, masks, rels),
        out_shape=jax.ShapeDtypeStruct((rows, width), BF16),
        in_specs=[SMEM, SMEM] + [VMEM] * 3 + [ANY] + [VMEM] * (len(masks) + len(rels)),
        out_specs=VMEM,
        scratch_shapes=[pltpu.VMEM((total_rows, width + EDGE), BF16), held, sems],
        compiler_params=PARAMS,
    )(place, ids, fields, labels, weights, couple, *near_list, *[gathered[rel] for rel in rels])
    return (forward_out, adjoint_out)


def solution(mesh):
    placed = (
        P("coef", "tiles"),
        P("coef", "tiles"),
        P(),
        P("tiles", "coef", None),
        P("tiles", None),
        P("tiles"),
    )
    return jax.shard_map(
        local,
        mesh=mesh,
        in_specs=placed,
        out_specs=(P("coef", "tiles"), P("coef", "tiles")),
        check_vma=False,
    )
```

```python
import functools

import jax
import jax.numpy as jnp
from jax import lax
from jax.experimental import pallas as pl
from jax.experimental.pallas import tpu as pltpu
from jax.sharding import PartitionSpec as P

SLOTS = 30
HW = 15
EDGE = 128
CHUNK = 5
OFFSETS = [slot - HW + (1 if slot >= HW else 0) for slot in range(SLOTS)]
BF16 = jnp.bfloat16
F32 = jnp.float32
VMEM = pl.BlockSpec(memory_space=pltpu.VMEM)
SMEM = pl.BlockSpec(memory_space=pltpu.SMEM)
ANY = pl.BlockSpec(memory_space=pl.ANY)
HBM = pl.BlockSpec(memory_space=pltpu.HBM)
PARAMS = pltpu.CompilerParams(vmem_limit_bytes=24 * 1024 * 1024)
FULL = pltpu.CompilerParams(vmem_limit_bytes=58 * 1024 * 1024)


def edges_of(cells):
    width = cells.shape[1]
    head, tail = cells[:, :EDGE], cells[:, width - EDGE :]
    lane = lax.broadcasted_iota(jnp.int32, head.shape, 1)
    return jnp.where(lane < EDGE // 2, head, tail)


def pack_kernel(t_any, f_any, a_any, class_any, near_ref, far_ref, f_ref, a_ref, class_ref, t_ref, sems):
    copies = [
        pltpu.make_async_copy(source, target, sems.at[at])
        for at, (source, target) in enumerate(
            ((t_any, t_ref), (f_any, f_ref), (a_any, a_ref), (class_any, class_ref))
        )
    ]
    for copy in copies:
        copy.start()
    for copy in copies:
        copy.wait()
    count, rows, depth = t_ref.shape
    mats = count * rows
    width = f_ref.shape[1]
    fields, adjoints = f_ref[...], a_ref[...]
    class_edge = edges_of(class_ref[...]).astype(F32).astype(BF16)
    class_rows = jnp.broadcast_to(class_edge, (16, EDGE))
    for out_ref in (near_ref, far_ref):
        out_ref[:mats, :] = t_ref[...].reshape(mats, depth)
        out_ref[mats : mats + rows, :EDGE] = edges_of(fields)
        out_ref[mats : mats + rows, EDGE : 2 * EDGE] = edges_of(adjoints)
        out_ref[mats + rows : mats + rows + 16, :EDGE] = class_rows
        out_ref[mats + rows : mats + rows + 16, EDGE : 2 * EDGE] = class_rows
    base = mats + rows + 16
    for part in range(width // depth):
        lanes = slice(part * depth, (part + 1) * depth)
        far_ref[base + 2 * part * rows : base + (2 * part + 1) * rows, :] = fields[:, lanes]
        far_ref[base + (2 * part + 1) * rows : base + (2 * part + 2) * rows, :] = adjoints[:, lanes]


def pick_halo(place, piece_refs, masks, row_slice, lane_slice):
    tile = place[0]
    shape = (row_slice.stop - row_slice.start, EDGE)
    lane = lax.broadcasted_iota(jnp.int32, shape, 1)
    above = jnp.zeros(shape, F32)
    below = jnp.zeros(shape, F32)
    for piece_ref, mask in zip(piece_refs, masks):
        cells = piece_ref[row_slice, lane_slice].astype(F32)
        owner = tile ^ mask
        above = jnp.where(owner == tile + 1, cells, above)
        below = jnp.where(owner == tile - 1, cells, below)
    return jnp.where(lane < EDGE // 2, above, below)


def own_and_far(place, own, far):
    odd = place[1] == 1
    own32, far32 = own.astype(F32), far.astype(F32)
    return jnp.where(odd, far32, own32).astype(BF16), jnp.where(odd, own32, far32).astype(BF16)


def fields_kernel(masks, count, place, f_ref, far_ref, *refs):
    half = len(masks)
    near, across, out_ref = refs[:half], refs[half : 2 * half], refs[-1]
    rows, width = f_ref.shape
    depth = far_ref.shape[1]
    mats = count * rows
    base = mats + rows + 16
    edge_rows = slice(mats, mats + rows)
    lanes = slice(0, EDGE)
    first = pl.multiple_of(place[1] * rows, rows)
    second = pl.multiple_of((1 - place[1]) * rows, rows)
    out_ref[pl.ds(first, rows), :width] = f_ref[...]
    out_ref[pl.ds(first, rows), width:] = pick_halo(place, near, masks, edge_rows, lanes).astype(BF16)
    for part in range(width // depth):
        out_ref[pl.ds(second, rows), part * depth : (part + 1) * depth] = far_ref[
            base + 2 * part * rows : base + (2 * part + 1) * rows, :
        ]
    out_ref[pl.ds(second, rows), width:] = pick_halo(place, across, masks, edge_rows, lanes).astype(BF16)


def prepare_kernel(couple_ref, after_ref, plain_ref, turned_ref, sems):
    copies = []
    for chunk in range(SLOTS // CHUNK):
        span = pl.ds(chunk * CHUNK, CHUNK)
        copies.append(
            pltpu.make_async_copy(couple_ref.at[span], plain_ref.at[span], sems.at[chunk])
        )
    for copy in copies:
        copy.start()
    for chunk, copy in enumerate(copies):
        copy.wait()
        for mat in range(chunk * CHUNK, (chunk + 1) * CHUNK):
            turned_ref[SLOTS - 1 - mat] = plain_ref[mat].T


def couple_all(source, weight_ref, mats_ref):
    span = source.shape[1]
    width = weight_ref.shape[1]
    total = None
    for slot in range(SLOTS):
        moved = pltpu.roll(source, (-OFFSETS[slot]) % span, 1)[:, :width]
        selected = moved * weight_ref[slot : slot + 1, :]
        product = jnp.dot(mats_ref[slot], selected, preferred_element_type=F32)
        total = product if total is None else total + product
    return total


def adjoint_kernel(
    masks, place, ids_ref, a_ref, far_ref, class_ref, weight_ref, mats_ref, after_ref, *refs
):
    half = len(masks)
    near, across = refs[:half], refs[half : 2 * half]
    send_ref, keep_ref, total_ref, expanded, stacked = refs[2 * half :]
    rows, width = a_ref.shape
    depth = far_ref.shape[1]
    count = ids_ref.shape[0] // half
    mats = count * rows
    base = mats + rows + 16
    edge_rows = slice(mats, mats + rows)
    lanes = slice(EDGE, 2 * EDGE)
    far_own = jnp.concatenate(
        [
            far_ref[base + (2 * part + 1) * rows : base + (2 * part + 2) * rows, :]
            for part in range(width // depth)
        ],
        axis=1,
    )
    padded = [
        jnp.concatenate([own, pick_halo(place, pieces, masks, edge_rows, lanes).astype(BF16)], axis=1)
        for own, pieces in ((a_ref[...], near), (far_own, across))
    ]
    class_halo = pick_halo(place, near, masks, slice(mats + rows, mats + rows + 16), slice(0, EDGE))
    labels = jnp.concatenate(
        [class_ref[...], class_halo[0:1, :].astype(jnp.int32)], axis=1
    )
    at = 0
    for piece in range(half):
        for which, pieces in ((0, near), (1, across)):
            stacked[at : at + mats, :] = pieces[piece][:mats, :]
            for local_class in range(count):
                hit = labels == ids_ref[piece * count + local_class]
                factor = jnp.where(hit, 1.0, 0.0).astype(BF16)
                expanded[at : at + rows, :] = padded[which] * factor
                at += rows
    scattered = lax.dot_general(
        stacked[...], expanded[...], (((0,), (0,)), ((), ())), preferred_element_type=F32
    ).astype(BF16)
    total_ref[...] = couple_all(scattered, weight_ref, mats_ref)
    steps = keep_ref.shape[0]
    for rel in range(steps):
        start = pl.multiple_of(((place[2] ^ rel) * 2 + place[1]) * rows, rows)
        keep_ref[rel] = total_ref[pl.ds(start, rows), :]
        start = pl.multiple_of(((place[2] ^ (rel + steps)) * 2 + place[1]) * rows, rows)
        send_ref[rel] = total_ref[pl.ds(start, rows), :].astype(BF16)


def forward_kernel(rels, place, weight_ref, mats_ref, *refs):
    pieces, out_ref, padded = refs[:-2], refs[-2], refs[-1]
    block = pieces[0].shape[0]
    for rel, piece_ref in zip(rels, pieces):
        start = pl.multiple_of((place[2] ^ rel) * block, block)
        padded[pl.ds(start, block), :] = piece_ref[...]
    out_ref[...] = couple_all(padded[...], weight_ref, mats_ref).astype(BF16)


def finish_kernel(masks, ids_ref, coupled_ref, f_ref, a_ref, class_ref, kept_ref, last_ref, *refs):
    near, forward_ref, adjoint_ref = refs[:-2], refs[-2], refs[-1]
    rows, width = f_ref.shape
    count = ids_ref.shape[0] // len(masks)
    mats = count * rows
    coupled = coupled_ref[...]
    applied = jnp.zeros((rows, width), F32)
    labels = class_ref[...]
    for piece in range(len(masks)):
        product = jnp.dot(near[piece][:mats, :], coupled, preferred_element_type=F32)
        for local_class in range(count):
            hit = labels == ids_ref[piece * count + local_class]
            applied = jnp.where(hit, product[local_class * rows : (local_class + 1) * rows, :], applied)
    forward_ref[...] = (f_ref[...].astype(F32) - applied).astype(BF16)
    returned = kept_ref[0] + last_ref[0].astype(F32)
    adjoint_ref[...] = (a_ref[...].astype(F32) - returned).astype(BF16)


def local(fields, adjoints, couple, tmatrices, neighbours, classes):
    tiles, coefs = lax.axis_size("tiles"), lax.axis_size("coef")
    tile, coef = lax.axis_index("tiles"), lax.axis_index("coef")
    rows, width = fields.shape
    count, unused, depth = tmatrices.shape
    place = jnp.stack([tile, coef % 2, coef // 2]).astype(jnp.int32)

    def swap(cells, tile_mask, coef_mask):
        pairs = [
            (i * coefs + j, (i ^ tile_mask) * coefs + (j ^ coef_mask))
            for i in range(tiles)
            for j in range(coefs)
        ]
        return lax.ppermute(cells, ("tiles", "coef"), pairs)

    weights = (neighbours >= 0).astype(BF16).T
    labels = classes.reshape(1, width)
    mats = count * rows
    near_rows = mats + rows + 16
    far_rows = near_rows + 2 * rows * (width // depth)
    near_own, far_own, fields, adjoints, labels = pl.pallas_call(
        pack_kernel,
        out_shape=(
            jax.ShapeDtypeStruct((near_rows, depth), BF16),
            jax.ShapeDtypeStruct((far_rows, depth), BF16),
            jax.ShapeDtypeStruct(fields.shape, BF16),
            jax.ShapeDtypeStruct(adjoints.shape, BF16),
            jax.ShapeDtypeStruct(labels.shape, jnp.int32),
        ),
        in_specs=[HBM] * 4,
        out_specs=(VMEM,) * 5,
        scratch_shapes=[pltpu.VMEM(tmatrices.shape, BF16), pltpu.SemaphoreType.DMA((4,))],
        compiler_params=FULL,
    )(tmatrices, fields, adjoints, labels)
    mats_plain, mats_turned = pl.pallas_call(
        prepare_kernel,
        out_shape=(jax.ShapeDtypeStruct(couple.shape, BF16),) * 2,
        in_specs=[HBM, ANY],
        out_specs=(VMEM, VMEM),
        scratch_shapes=[pltpu.SemaphoreType.DMA((SLOTS // CHUNK,))],
        cost_estimate=pl.CostEstimate(flops=0, bytes_accessed=4 * couple.size, transcendentals=0),
        compiler_params=PARAMS,
    )(couple, near_own)

    top = tiles // 2
    far = swap(far_own, 0, 1)
    near = {0: near_own, top: swap(near_own, top, 0)}
    across = {0: far, top: swap(near_own, top, 1)}
    bit = top // 2
    while bit >= 1:
        for group in (near, across):
            for mask, piece in list(group.items()):
                source = piece[:near_rows] if group is across else piece
                group[mask ^ bit] = swap(source, bit, 0)
        bit //= 2
    masks = sorted(near)
    near_list = [near[mask] for mask in masks]
    across_list = [across[mask] for mask in masks]
    ids = (
        (tile ^ jnp.array(masks, jnp.int32))[:, None] * count + jnp.arange(count, dtype=jnp.int32)
    ).reshape(-1).astype(jnp.int32)

    padded_fields = pl.pallas_call(
        functools.partial(fields_kernel, masks, count),
        out_shape=jax.ShapeDtypeStruct((2 * rows, width + EDGE), BF16),
        in_specs=[SMEM] + [VMEM] * (2 + 2 * len(masks)),
        out_specs=VMEM,
        compiler_params=PARAMS,
    )(place, fields, far, *near_list, *across_list)

    groups = coefs // 2
    gathered = {0: padded_fields}
    bit = groups // 2
    while bit >= 1:
        for rel, piece in list(gathered.items()):
            gathered[rel ^ bit] = swap(piece, 0, 2 * bit)
        bit //= 2
    rels = sorted(gathered)

    steps = groups // 2
    total_rows = couple.shape[1]
    work = pl.CostEstimate(flops=2 * couple.size * width, bytes_accessed=2 * couple.size, transcendentals=0)
    send, keep = pl.pallas_call(
        functools.partial(adjoint_kernel, masks),
        out_shape=(
            jax.ShapeDtypeStruct((steps, rows, width), BF16),
            jax.ShapeDtypeStruct((steps, rows, width), F32),
        ),
        in_specs=[SMEM, SMEM] + [VMEM] * 5 + [ANY] + [VMEM] * (2 * len(masks)),
        out_specs=(VMEM, VMEM),
        scratch_shapes=[
            pltpu.VMEM((total_rows, width), F32),
            pltpu.VMEM((2 * len(masks) * mats, width + EDGE), BF16),
            pltpu.VMEM((2 * len(masks) * mats, depth), BF16),
        ],
        cost_estimate=work,
        compiler_params=PARAMS,
    )(place, ids, adjoints, far, labels, weights, mats_turned, padded_fields, *near_list, *across_list)

    bit = groups // 2
    arrived = swap(send, 0, 2 * bit)
    while bit > 1:
        merged = keep + arrived.astype(F32)
        bit //= 2
        keep = merged[:bit]
        arrived = swap(merged[bit:].astype(BF16), 0, 2 * bit)

    coupled = pl.pallas_call(
        functools.partial(forward_kernel, rels),
        out_shape=jax.ShapeDtypeStruct((total_rows, width), BF16),
        in_specs=[SMEM] + [VMEM] * (2 + len(rels)),
        out_specs=VMEM,
        scratch_shapes=[pltpu.VMEM((total_rows, width + EDGE), BF16)],
        cost_estimate=work,
        compiler_params=PARAMS,
    )(place, weights, mats_plain, *[gathered[rel] for rel in rels])
    return pl.pallas_call(
        functools.partial(finish_kernel, masks),
        out_shape=(jax.ShapeDtypeStruct((rows, width), BF16),) * 2,
        in_specs=[SMEM] + [VMEM] * (6 + len(masks)),
        out_specs=(VMEM, VMEM),
        compiler_params=PARAMS,
    )(ids, coupled, fields, adjoints, labels, keep, arrived, *near_list)


def solution(mesh):
    placed = (
        P("coef", "tiles"),
        P("coef", "tiles"),
        P(),
        P("tiles", "coef", None),
        P("tiles", None),
        P("tiles"),
    )
    return jax.shard_map(
        local,
        mesh=mesh,
        in_specs=placed,
        out_specs=(P("coef", "tiles"), P("coef", "tiles")),
        check_vma=False,
    )
```

```python
import functools

import jax
import jax.numpy as jnp
from jax import lax
from jax.experimental import pallas as pl
from jax.experimental.pallas import tpu as pltpu
from jax.sharding import PartitionSpec as P

SLOTS = 30
HW = 15
EDGE = 128
CHUNK = 5
EARLY = 22
OFFSETS = [slot - HW + (1 if slot >= HW else 0) for slot in range(SLOTS)]
BF16 = jnp.bfloat16
F32 = jnp.float32
VMEM = pl.BlockSpec(memory_space=pltpu.VMEM)
SMEM = pl.BlockSpec(memory_space=pltpu.SMEM)
ANY = pl.BlockSpec(memory_space=pl.ANY)
HBM = pl.BlockSpec(memory_space=pltpu.HBM)
PARAMS = pltpu.CompilerParams(vmem_limit_bytes=24 * 1024 * 1024)
WIDE = pltpu.CompilerParams(vmem_limit_bytes=24 * 1024 * 1024)
FULL = pltpu.CompilerParams(vmem_limit_bytes=58 * 1024 * 1024)


def edges_of(cells):
    width = cells.shape[1]
    head, tail = cells[:, :EDGE], cells[:, width - EDGE :]
    lane = lax.broadcasted_iota(jnp.int32, head.shape, 1)
    return jnp.where(lane < EDGE // 2, head, tail)


def pack_kernel(
    spot, t_any, f_any, a_any, class_any, place, near_ref, far_ref, f_ref, a_ref, class_ref, t_ref, sems
):
    place[0] = spot[0]
    place[1] = spot[1] & 1
    place[2] = spot[1] >> 1
    copies = [
        pltpu.make_async_copy(source, target, sems.at[at])
        for at, (source, target) in enumerate(
            ((t_any, t_ref), (f_any, f_ref), (a_any, a_ref), (class_any, class_ref))
        )
    ]
    for copy in copies:
        copy.start()
    for copy in copies:
        copy.wait()
    count, rows, depth = t_ref.shape
    mats = count * rows
    width = f_ref.shape[1]
    fields, adjoints = f_ref[...], a_ref[...]
    class_edge = edges_of(class_ref[...]).astype(F32).astype(BF16)
    class_rows = jnp.broadcast_to(class_edge, (16, EDGE))
    for out_ref in (near_ref, far_ref):
        out_ref[:mats, :] = t_ref[...].reshape(mats, depth)
        out_ref[mats : mats + rows, :EDGE] = edges_of(fields)
        out_ref[mats : mats + rows, EDGE : 2 * EDGE] = edges_of(adjoints)
        out_ref[mats + rows : mats + rows + 16, :EDGE] = class_rows
        out_ref[mats + rows : mats + rows + 16, EDGE : 2 * EDGE] = class_rows
    base = mats + rows + 16
    for part in range(width // depth):
        lanes = slice(part * depth, (part + 1) * depth)
        far_ref[base + 2 * part * rows : base + (2 * part + 1) * rows, :] = fields[:, lanes]
        far_ref[base + (2 * part + 1) * rows : base + (2 * part + 2) * rows, :] = adjoints[:, lanes]


def relay_kernel(near_ref, top_ref, far_ref, cross_ref, after_ref, out_ref):
    rows = near_ref.shape[0]
    out_ref[0] = near_ref[...]
    out_ref[1] = top_ref[...]
    out_ref[2] = far_ref[:rows, :]
    out_ref[3] = cross_ref[...]


def merge_kernel(keep_ref, arrived_ref, after_ref, kept_ref, send_ref):
    half = kept_ref.shape[0]
    kept_ref[...] = keep_ref[:half] + arrived_ref[:half].astype(F32)
    send_ref[...] = (keep_ref[half:] + arrived_ref[half:].astype(F32)).astype(BF16)


def pick_halo(place, pieces, masks, row_slice, lane_slice):
    tile = place[0]
    shape = (row_slice.stop - row_slice.start, EDGE)
    lane = lax.broadcasted_iota(jnp.int32, shape, 1)
    above = jnp.zeros(shape, F32)
    below = jnp.zeros(shape, F32)
    for (piece_ref, at), mask in zip(pieces, masks):
        cells = piece_ref[at, row_slice, lane_slice].astype(F32)
        owner = tile ^ mask
        above = jnp.where(owner == tile + 1, cells, above)
        below = jnp.where(owner == tile - 1, cells, below)
    return jnp.where(lane < EDGE // 2, above, below)


def split_pieces(refs):
    near = [(ref, at) for ref in refs for at in (0, 1)]
    across = [(ref, at) for ref in refs for at in (2, 3)]
    return near, across


def fields_kernel(masks, count, place, f_ref, far_ref, *refs):
    (near, across), out_ref = split_pieces(refs[:-1]), refs[-1]
    rows, width = f_ref.shape
    depth = far_ref.shape[1]
    mats = count * rows
    base = mats + rows + 16
    edge_rows = slice(mats, mats + rows)
    lanes = slice(0, EDGE)
    first = pl.multiple_of(place[1] * rows, rows)
    second = pl.multiple_of((1 - place[1]) * rows, rows)
    out_ref[pl.ds(first, rows), :width] = f_ref[...]
    out_ref[pl.ds(first, rows), width:] = pick_halo(place, near, masks, edge_rows, lanes).astype(BF16)
    for part in range(width // depth):
        out_ref[pl.ds(second, rows), part * depth : (part + 1) * depth] = far_ref[
            base + 2 * part * rows : base + (2 * part + 1) * rows, :
        ]
    out_ref[pl.ds(second, rows), width:] = pick_halo(place, across, masks, edge_rows, lanes).astype(BF16)


def prepare_kernel(couple_ref, after_ref, plain_ref, turned_ref, sems):
    copies = []
    for chunk in range(SLOTS // CHUNK):
        span = pl.ds(chunk * CHUNK, CHUNK)
        copies.append(
            pltpu.make_async_copy(couple_ref.at[span], plain_ref.at[span], sems.at[chunk])
        )
    for copy in copies:
        copy.start()
    for chunk, copy in enumerate(copies):
        copy.wait()
        for mat in range(chunk * CHUNK, (chunk + 1) * CHUNK):
            turned_ref[SLOTS - 1 - mat] = plain_ref[mat].T


def couple_slots(source, weight_ref, mats_ref, slots, total=None):
    span = source.shape[1]
    width = weight_ref.shape[1]
    for slot in slots:
        moved = pltpu.roll(source, (-OFFSETS[slot]) % span, 1)[:, :width]
        selected = moved * weight_ref[slot : slot + 1, :]
        product = jnp.dot(mats_ref[slot], selected, preferred_element_type=F32)
        total = product if total is None else total + product
    return total


def adjoint_kernel(
    masks, count, place, a_ref, far_ref, class_ref, weight_ref, mats_ref, after_ref, *refs
):
    half = len(masks)
    near, across = split_pieces(refs[:-5])
    send_ref, keep_ref, total_ref, expanded, stacked = refs[-5:]
    rows, width = a_ref.shape
    depth = far_ref.shape[1]
    mats = count * rows
    base = mats + rows + 16
    edge_rows = slice(mats, mats + rows)
    lanes = slice(EDGE, 2 * EDGE)
    far_own = jnp.concatenate(
        [
            far_ref[base + (2 * part + 1) * rows : base + (2 * part + 2) * rows, :]
            for part in range(width // depth)
        ],
        axis=1,
    )
    padded = [
        jnp.concatenate([own, pick_halo(place, pieces, masks, edge_rows, lanes).astype(BF16)], axis=1)
        for own, pieces in ((a_ref[...], near), (far_own, across))
    ]
    class_halo = pick_halo(place, near, masks, slice(mats + rows, mats + rows + 16), slice(0, EDGE))
    labels = jnp.concatenate(
        [class_ref[...], class_halo[0:1, :].astype(jnp.int32)], axis=1
    )
    at = 0
    for piece in range(half):
        for which, pieces in ((0, near), (1, across)):
            ref, spot = pieces[piece]
            stacked[at : at + mats, :] = ref[spot, :mats, :]
            for local_class in range(count):
                hit = labels == (place[0] ^ masks[piece]) * count + local_class
                factor = jnp.where(hit, 1.0, 0.0).astype(BF16)
                expanded[at : at + rows, :] = padded[which] * factor
                at += rows
    scattered = lax.dot_general(
        stacked[...], expanded[...], (((0,), (0,)), ((), ())), preferred_element_type=F32
    ).astype(BF16)
    total_ref[...] = couple_slots(scattered, weight_ref, mats_ref, range(SLOTS))
    steps = keep_ref.shape[0]
    for rel in range(steps):
        start = pl.multiple_of(((place[2] ^ rel) * 2 + place[1]) * rows, rows)
        keep_ref[rel] = total_ref[pl.ds(start, rows), :]
        start = pl.multiple_of(((place[2] ^ (rel + steps)) * 2 + place[1]) * rows, rows)
        send_ref[rel] = total_ref[pl.ds(start, rows), :].astype(BF16)


def gather_kernel(rels, place, weight_ref, mats_ref, *refs):
    pieces, total_ref, padded = refs[:-2], refs[-2], refs[-1]
    block = pieces[0].shape[0]
    for rel, piece_ref in zip(rels, pieces):
        start = pl.multiple_of((place[2] ^ rel) * block, block)
        padded[pl.ds(start, block), :] = piece_ref[...]
    total_ref[...] = couple_slots(padded[...], weight_ref, mats_ref, range(EARLY))


def forward_kernel(masks, count, place, f_ref, class_ref, weight_ref, mats_ref, total_ref, padded, *refs):
    (near, across), out_ref = split_pieces(refs[:-1]), refs[-1]
    rows, width = f_ref.shape
    mats = count * rows
    coupled = couple_slots(
        padded[...], weight_ref, mats_ref, range(EARLY, SLOTS), total_ref[...]
    ).astype(BF16)
    applied = jnp.zeros((rows, width), F32)
    labels = class_ref[...]
    for piece in range(len(masks)):
        ref, spot = near[piece]
        product = jnp.dot(ref[spot, :mats, :], coupled, preferred_element_type=F32)
        for local_class in range(count):
            hit = labels == (place[0] ^ masks[piece]) * count + local_class
            applied = jnp.where(hit, product[local_class * rows : (local_class + 1) * rows, :], applied)
    out_ref[...] = (f_ref[...].astype(F32) - applied).astype(BF16)


def local(fields, adjoints, couple, tmatrices, neighbours, classes):
    tiles, coefs = lax.axis_size("tiles"), lax.axis_size("coef")
    tile, coef = lax.axis_index("tiles"), lax.axis_index("coef")
    rows, width = fields.shape
    count, unused, depth = tmatrices.shape
    spot = jnp.stack([tile, coef]).astype(jnp.int32)

    def swap(cells, tile_mask, coef_mask):
        pairs = [
            (i * coefs + j, (i ^ tile_mask) * coefs + (j ^ coef_mask))
            for i in range(tiles)
            for j in range(coefs)
        ]
        return lax.ppermute(cells, ("tiles", "coef"), pairs)

    weights = (neighbours >= 0).astype(BF16).T
    labels = classes.reshape(1, width)
    mats = count * rows
    near_rows = mats + rows + 16
    far_rows = near_rows + 2 * rows * (width // depth)
    place, near_own, far_own, fields, adjoints, labels = pl.pallas_call(
        pack_kernel,
        out_shape=(
            jax.ShapeDtypeStruct((3,), jnp.int32),
            jax.ShapeDtypeStruct((near_rows, depth), BF16),
            jax.ShapeDtypeStruct((far_rows, depth), BF16),
            jax.ShapeDtypeStruct(fields.shape, BF16),
            jax.ShapeDtypeStruct(adjoints.shape, BF16),
            jax.ShapeDtypeStruct(labels.shape, jnp.int32),
        ),
        in_specs=[SMEM] + [HBM] * 4,
        out_specs=(SMEM,) + (VMEM,) * 5,
        scratch_shapes=[pltpu.VMEM(tmatrices.shape, BF16), pltpu.SemaphoreType.DMA((4,))],
        compiler_params=FULL,
    )(spot, tmatrices, fields, adjoints, labels)
    mats_plain, mats_turned = pl.pallas_call(
        prepare_kernel,
        out_shape=(jax.ShapeDtypeStruct(couple.shape, BF16),) * 2,
        in_specs=[HBM, SMEM],
        out_specs=(VMEM, VMEM),
        scratch_shapes=[pltpu.SemaphoreType.DMA((SLOTS // CHUNK,))],
        cost_estimate=pl.CostEstimate(flops=0, bytes_accessed=4 * couple.size, transcendentals=0),
        compiler_params=WIDE,
    )(couple, place)

    top = tiles // 2
    far = swap(far_own, 0, 1)
    first = pl.pallas_call(
        relay_kernel,
        out_shape=jax.ShapeDtypeStruct((4, near_rows, depth), BF16),
        in_specs=[VMEM] * 5,
        out_specs=VMEM,
        compiler_params=PARAMS,
    )(near_own, swap(near_own, top, 0), far, swap(near_own, top, 1), mats_turned)
    held, lows = [first], [0]
    bit = top // 2
    while bit >= 1:
        held += [swap(block, bit, 0) for block in held]
        lows += [low ^ bit for low in lows]
        bit //= 2
    masks = [low ^ high for low in lows for high in (0, top)]

    padded_fields = pl.pallas_call(
        functools.partial(fields_kernel, masks, count),
        out_shape=jax.ShapeDtypeStruct((2 * rows, width + EDGE), BF16),
        in_specs=[SMEM] + [VMEM] * (2 + len(held)),
        out_specs=VMEM,
        compiler_params=PARAMS,
    )(place, fields, far, *held)

    groups = coefs // 2
    gathered = {0: padded_fields}
    for rel in range(1, groups):
        gathered[rel] = swap(padded_fields, 0, 2 * rel)
    rels = sorted(gathered)

    steps = groups // 2
    total_rows = couple.shape[1]

    def work(slots):
        size = slots * total_rows * total_rows
        return pl.CostEstimate(flops=2 * size * width, bytes_accessed=2 * size, transcendentals=0)

    send, keep = pl.pallas_call(
        functools.partial(adjoint_kernel, masks, count),
        out_shape=(
            jax.ShapeDtypeStruct((steps, rows, width), BF16),
            jax.ShapeDtypeStruct((steps, rows, width), F32),
        ),
        in_specs=[SMEM] + [VMEM] * 5 + [ANY] + [VMEM] * len(held),
        out_specs=(VMEM, VMEM),
        scratch_shapes=[
            pltpu.VMEM((total_rows, width), F32),
            pltpu.VMEM((2 * len(masks) * mats, width + EDGE), BF16),
            pltpu.VMEM((2 * len(masks) * mats, depth), BF16),
        ],
        cost_estimate=work(SLOTS + 8),
        compiler_params=PARAMS,
    )(place, adjoints, far, labels, weights, mats_turned, padded_fields, *held)

    partial, all_fields = pl.pallas_call(
        functools.partial(gather_kernel, rels),
        out_shape=(
            jax.ShapeDtypeStruct((total_rows, width), F32),
            jax.ShapeDtypeStruct((total_rows, width + EDGE), BF16),
        ),
        in_specs=[SMEM] + [VMEM] * (2 + len(rels)),
        out_specs=(VMEM, VMEM),
        cost_estimate=work(EARLY),
        compiler_params=PARAMS,
    )(place, weights, mats_plain, *[gathered[rel] for rel in rels])
    bit = groups // 2
    arrived = swap(send, 0, 2 * bit)
    while bit > 1:
        bit //= 2
        keep, send = pl.pallas_call(
            merge_kernel,
            out_shape=(
                jax.ShapeDtypeStruct((bit, rows, width), F32),
                jax.ShapeDtypeStruct((bit, rows, width), BF16),
            ),
            in_specs=[VMEM] * 3,
            out_specs=(VMEM, VMEM),
            compiler_params=PARAMS,
        )(keep, arrived, partial)
        arrived = swap(send, 0, 2 * bit)
    returned = keep[0] + arrived[0].astype(F32)
    adjoint_out = (adjoints.astype(F32) - returned).astype(BF16)

    forward_out = pl.pallas_call(
        functools.partial(forward_kernel, masks, count),
        out_shape=jax.ShapeDtypeStruct((rows, width), BF16),
        in_specs=[SMEM] + [VMEM] * (6 + len(held)),
        out_specs=VMEM,
        cost_estimate=work(SLOTS - EARLY + 8),
        compiler_params=PARAMS,
    )(place, fields, labels, weights, mats_plain, partial, all_fields, *held)
    return (forward_out, adjoint_out)


def solution(mesh):
    placed = (
        P("coef", "tiles"),
        P("coef", "tiles"),
        P(),
        P("tiles", "coef", None),
        P("tiles", None),
        P("tiles"),
    )
    return jax.shard_map(
        local,
        mesh=mesh,
        in_specs=placed,
        out_specs=(P("coef", "tiles"), P("coef", "tiles")),
        check_vma=False,
    )
```

```python
import functools

import jax
import jax.numpy as jnp
from jax import lax
from jax.experimental import pallas as pl
from jax.experimental.pallas import tpu as pltpu
from jax.sharding import PartitionSpec as P

SLOTS = 30
HW = 15
EDGE = 128
CHUNK = 5
EARLY = 22
OFFSETS = [slot - HW + (1 if slot >= HW else 0) for slot in range(SLOTS)]
BF16 = jnp.bfloat16
F32 = jnp.float32
VMEM = pl.BlockSpec(memory_space=pltpu.VMEM)
SMEM = pl.BlockSpec(memory_space=pltpu.SMEM)
ANY = pl.BlockSpec(memory_space=pl.ANY)
HBM = pl.BlockSpec(memory_space=pltpu.HBM)
PARAMS = pltpu.CompilerParams(vmem_limit_bytes=24 * 1024 * 1024)


def in_hbm(cells):
    return pltpu.with_memory_space_constraint(cells, pltpu.HBM)


def edges_of(cells):
    width = cells.shape[1]
    head, tail = cells[:, :EDGE], cells[:, width - EDGE :]
    lane = lax.broadcasted_iota(jnp.int32, head.shape, 1)
    return jnp.where(lane < EDGE // 2, head, tail)


def pack_kernel(
    t_any, f_any, a_any, class_any, place, near_ref, far_ref, f_ref, a_ref, class_ref, t_ref, sems
):
    coef = lax.axis_index("coef")
    place[0] = lax.axis_index("tiles")
    place[1] = coef & 1
    place[2] = coef >> 1
    copies = [
        pltpu.make_async_copy(source, target, sems.at[at])
        for at, (source, target) in enumerate(
            ((t_any, t_ref), (f_any, f_ref), (a_any, a_ref), (class_any, class_ref))
        )
    ]
    for copy in copies:
        copy.start()
    for copy in copies:
        copy.wait()
    count, rows, depth = t_ref.shape
    mats = count * rows
    width = f_ref.shape[1]
    fields, adjoints = f_ref[...], a_ref[...]
    class_edge = edges_of(class_ref[...]).astype(F32).astype(BF16)
    class_rows = jnp.broadcast_to(class_edge, (16, EDGE))
    for out_ref in (near_ref, far_ref):
        out_ref[:mats, :] = t_ref[...].reshape(mats, depth)
        out_ref[mats : mats + rows, :EDGE] = edges_of(fields)
        out_ref[mats : mats + rows, EDGE : 2 * EDGE] = edges_of(adjoints)
        out_ref[mats + rows : mats + rows + 16, :EDGE] = class_rows
        out_ref[mats + rows : mats + rows + 16, EDGE : 2 * EDGE] = class_rows
    base = mats + rows + 16
    for part in range(width // depth):
        lanes = slice(part * depth, (part + 1) * depth)
        far_ref[base + 2 * part * rows : base + (2 * part + 1) * rows, :] = fields[:, lanes]
        far_ref[base + (2 * part + 1) * rows : base + (2 * part + 2) * rows, :] = adjoints[:, lanes]


def relay_kernel(near_ref, top_ref, far_ref, cross_ref, after_ref, out_ref):
    rows = near_ref.shape[0]
    out_ref[0] = near_ref[...]
    out_ref[1] = top_ref[...]
    out_ref[2] = far_ref[:rows, :]
    out_ref[3] = cross_ref[...]


def merge_kernel(keep_ref, arrived_ref, after_ref, kept_ref, send_ref):
    half = kept_ref.shape[0]
    kept_ref[...] = keep_ref[:half] + arrived_ref[:half].astype(F32)
    send_ref[...] = (keep_ref[half:] + arrived_ref[half:].astype(F32)).astype(BF16)


def pick_halo(place, pieces, masks, row_slice, lane_slice):
    tile = place[0]
    shape = (row_slice.stop - row_slice.start, EDGE)
    lane = lax.broadcasted_iota(jnp.int32, shape, 1)
    above = jnp.zeros(shape, F32)
    below = jnp.zeros(shape, F32)
    for (piece_ref, at), mask in zip(pieces, masks):
        cells = piece_ref[at, row_slice, lane_slice].astype(F32)
        owner = tile ^ mask
        above = jnp.where(owner == tile + 1, cells, above)
        below = jnp.where(owner == tile - 1, cells, below)
    return jnp.where(lane < EDGE // 2, above, below)


def split_pieces(refs):
    near = [(ref, at) for ref in refs for at in (0, 1)]
    across = [(ref, at) for ref in refs for at in (2, 3)]
    return near, across


def fields_kernel(masks, count, place, f_ref, far_ref, *refs):
    (near, across), out_ref = split_pieces(refs[:-1]), refs[-1]
    rows, width = f_ref.shape
    depth = far_ref.shape[1]
    mats = count * rows
    base = mats + rows + 16
    edge_rows = slice(mats, mats + rows)
    lanes = slice(0, EDGE)
    first = pl.multiple_of(place[1] * rows, rows)
    second = pl.multiple_of((1 - place[1]) * rows, rows)
    out_ref[pl.ds(first, rows), :width] = f_ref[...]
    out_ref[pl.ds(first, rows), width:] = pick_halo(place, near, masks, edge_rows, lanes).astype(BF16)
    for part in range(width // depth):
        out_ref[pl.ds(second, rows), part * depth : (part + 1) * depth] = far_ref[
            base + 2 * part * rows : base + (2 * part + 1) * rows, :
        ]
    out_ref[pl.ds(second, rows), width:] = pick_halo(place, across, masks, edge_rows, lanes).astype(BF16)


def prepare_kernel(couple_ref, after_ref, plain_ref, turned_ref, sems):
    copies = []
    for chunk in range(SLOTS // CHUNK):
        span = pl.ds(chunk * CHUNK, CHUNK)
        copies.append(
            pltpu.make_async_copy(couple_ref.at[span], plain_ref.at[span], sems.at[chunk])
        )
    for copy in copies:
        copy.start()
    for chunk, copy in enumerate(copies):
        copy.wait()
        for mat in range(chunk * CHUNK, (chunk + 1) * CHUNK):
            turned_ref[SLOTS - 1 - mat] = plain_ref[mat].T


def couple_slots(source, weight_ref, mats_ref, slots, total=None):
    span = source.shape[1]
    width = weight_ref.shape[1]
    for slot in slots:
        moved = pltpu.roll(source, (-OFFSETS[slot]) % span, 1)[:, :width]
        selected = moved * weight_ref[slot : slot + 1, :]
        product = jnp.dot(mats_ref[slot], selected, preferred_element_type=F32)
        total = product if total is None else total + product
    return total


def adjoint_kernel(
    masks, count, place, a_ref, far_ref, class_ref, weight_ref, mats_ref, after_ref, *refs
):
    half = len(masks)
    near, across = split_pieces(refs[:-5])
    send_ref, keep_ref, total_ref, expanded, stacked = refs[-5:]
    rows, width = a_ref.shape
    depth = far_ref.shape[1]
    mats = count * rows
    base = mats + rows + 16
    edge_rows = slice(mats, mats + rows)
    lanes = slice(EDGE, 2 * EDGE)
    far_own = jnp.concatenate(
        [
            far_ref[base + (2 * part + 1) * rows : base + (2 * part + 2) * rows, :]
            for part in range(width // depth)
        ],
        axis=1,
    )
    padded = [
        jnp.concatenate([own, pick_halo(place, pieces, masks, edge_rows, lanes).astype(BF16)], axis=1)
        for own, pieces in ((a_ref[...], near), (far_own, across))
    ]
    class_halo = pick_halo(place, near, masks, slice(mats + rows, mats + rows + 16), slice(0, EDGE))
    labels = jnp.concatenate(
        [class_ref[...], class_halo[0:1, :].astype(jnp.int32)], axis=1
    )
    at = 0
    for piece in range(half):
        for which, pieces in ((0, near), (1, across)):
            ref, spot = pieces[piece]
            stacked[at : at + mats, :] = ref[spot, :mats, :]
            for local_class in range(count):
                hit = labels == (place[0] ^ masks[piece]) * count + local_class
                factor = jnp.where(hit, 1.0, 0.0).astype(BF16)
                expanded[at : at + rows, :] = padded[which] * factor
                at += rows
    scattered = lax.dot_general(
        stacked[...], expanded[...], (((0,), (0,)), ((), ())), preferred_element_type=F32
    ).astype(BF16)
    total_ref[...] = couple_slots(scattered, weight_ref, mats_ref, range(SLOTS))
    steps = keep_ref.shape[0]
    for rel in range(steps):
        start = pl.multiple_of(((place[2] ^ rel) * 2 + place[1]) * rows, rows)
        keep_ref[rel] = total_ref[pl.ds(start, rows), :]
        start = pl.multiple_of(((place[2] ^ (rel + steps)) * 2 + place[1]) * rows, rows)
        send_ref[rel] = total_ref[pl.ds(start, rows), :].astype(BF16)


def gather_kernel(rels, place, weight_ref, mats_ref, *refs):
    pieces, total_ref, padded = refs[:-2], refs[-2], refs[-1]
    block = pieces[0].shape[0]
    for rel, piece_ref in zip(rels, pieces):
        start = pl.multiple_of((place[2] ^ rel) * block, block)
        padded[pl.ds(start, block), :] = piece_ref[...]
    total_ref[...] = couple_slots(padded[...], weight_ref, mats_ref, range(EARLY))


def forward_kernel(masks, count, place, f_ref, class_ref, weight_ref, mats_ref, total_ref, padded, *refs):
    (near, across), out_ref = split_pieces(refs[:-1]), refs[-1]
    rows, width = f_ref.shape
    mats = count * rows
    coupled = couple_slots(
        padded[...], weight_ref, mats_ref, range(EARLY, SLOTS), total_ref[...]
    ).astype(BF16)
    applied = jnp.zeros((rows, width), F32)
    labels = class_ref[...]
    for piece in range(len(masks)):
        ref, spot = near[piece]
        product = jnp.dot(ref[spot, :mats, :], coupled, preferred_element_type=F32)
        for local_class in range(count):
            hit = labels == (place[0] ^ masks[piece]) * count + local_class
            applied = jnp.where(hit, product[local_class * rows : (local_class + 1) * rows, :], applied)
    out_ref[...] = (f_ref[...].astype(F32) - applied).astype(BF16)


def local(fields, adjoints, couple, tmatrices, neighbours, classes):
    tiles, coefs = lax.axis_size("tiles"), lax.axis_size("coef")
    rows, width = fields.shape
    count, unused, depth = tmatrices.shape

    def swap(cells, tile_mask, coef_mask):
        pairs = [
            (i * coefs + j, (i ^ tile_mask) * coefs + (j ^ coef_mask))
            for i in range(tiles)
            for j in range(coefs)
        ]
        return lax.ppermute(cells, ("tiles", "coef"), pairs)

    weights = (neighbours >= 0).astype(BF16).T
    labels = classes.reshape(1, width)
    mats = count * rows
    near_rows = mats + rows + 16
    far_rows = near_rows + 2 * rows * (width // depth)
    place, near_own, far_own, fields, adjoints, labels = pl.pallas_call(
        pack_kernel,
        out_shape=(
            jax.ShapeDtypeStruct((3,), jnp.int32),
            jax.ShapeDtypeStruct((near_rows, depth), BF16),
            jax.ShapeDtypeStruct((far_rows, depth), BF16),
            jax.ShapeDtypeStruct(fields.shape, BF16),
            jax.ShapeDtypeStruct(adjoints.shape, BF16),
            jax.ShapeDtypeStruct(labels.shape, jnp.int32),
        ),
        in_specs=[HBM] * 4,
        out_specs=(SMEM,) + (VMEM,) * 5,
        scratch_shapes=[pltpu.VMEM(tmatrices.shape, BF16), pltpu.SemaphoreType.DMA((4,))],
        compiler_params=PARAMS,
    )(*[in_hbm(cells) for cells in (tmatrices, fields, adjoints, labels)])
    mats_plain, mats_turned = pl.pallas_call(
        prepare_kernel,
        out_shape=(jax.ShapeDtypeStruct(couple.shape, BF16),) * 2,
        in_specs=[HBM, SMEM],
        out_specs=(VMEM, VMEM),
        scratch_shapes=[pltpu.SemaphoreType.DMA((SLOTS // CHUNK,))],
        cost_estimate=pl.CostEstimate(flops=0, bytes_accessed=4 * couple.size, transcendentals=0),
        compiler_params=PARAMS,
    )(in_hbm(couple), place)

    top = tiles // 2
    far = swap(far_own, 0, 1)
    first = pl.pallas_call(
        relay_kernel,
        out_shape=jax.ShapeDtypeStruct((4, near_rows, depth), BF16),
        in_specs=[VMEM] * 5,
        out_specs=VMEM,
        compiler_params=PARAMS,
    )(near_own, swap(near_own, top, 0), far, swap(near_own, top, 1), mats_turned)
    held, lows = [first], [0]
    bit = top // 2
    while bit >= 1:
        held += [swap(block, bit, 0) for block in held]
        lows += [low ^ bit for low in lows]
        bit //= 2
    masks = [low ^ high for low in lows for high in (0, top)]

    padded_fields = pl.pallas_call(
        functools.partial(fields_kernel, masks, count),
        out_shape=jax.ShapeDtypeStruct((2 * rows, width + EDGE), BF16),
        in_specs=[SMEM] + [VMEM] * (2 + len(held)),
        out_specs=VMEM,
        compiler_params=PARAMS,
    )(place, fields, far, *held)

    groups = coefs // 2
    gathered = {0: padded_fields}
    for rel in range(1, groups):
        gathered[rel] = swap(padded_fields, 0, 2 * rel)
    rels = sorted(gathered)

    steps = groups // 2
    total_rows = couple.shape[1]

    def work(slots):
        size = slots * total_rows * total_rows
        return pl.CostEstimate(flops=2 * size * width, bytes_accessed=2 * size, transcendentals=0)

    send, keep = pl.pallas_call(
        functools.partial(adjoint_kernel, masks, count),
        out_shape=(
            jax.ShapeDtypeStruct((steps, rows, width), BF16),
            jax.ShapeDtypeStruct((steps, rows, width), F32),
        ),
        in_specs=[SMEM] + [VMEM] * 5 + [ANY] + [VMEM] * len(held),
        out_specs=(VMEM, VMEM),
        scratch_shapes=[
            pltpu.VMEM((total_rows, width), F32),
            pltpu.VMEM((2 * len(masks) * mats, width + EDGE), BF16),
            pltpu.VMEM((2 * len(masks) * mats, depth), BF16),
        ],
        cost_estimate=work(SLOTS + 8),
        compiler_params=PARAMS,
    )(place, adjoints, far, labels, weights, mats_turned, padded_fields, *held)

    partial, all_fields = pl.pallas_call(
        functools.partial(gather_kernel, rels),
        out_shape=(
            jax.ShapeDtypeStruct((total_rows, width), F32),
            jax.ShapeDtypeStruct((total_rows, width + EDGE), BF16),
        ),
        in_specs=[SMEM] + [VMEM] * (2 + len(rels)),
        out_specs=(VMEM, VMEM),
        cost_estimate=work(EARLY),
        compiler_params=PARAMS,
    )(place, weights, mats_plain, *[gathered[rel] for rel in rels])
    bit = groups // 2
    arrived = swap(send, 0, 2 * bit)
    while bit > 1:
        bit //= 2
        keep, send = pl.pallas_call(
            merge_kernel,
            out_shape=(
                jax.ShapeDtypeStruct((bit, rows, width), F32),
                jax.ShapeDtypeStruct((bit, rows, width), BF16),
            ),
            in_specs=[VMEM] * 3,
            out_specs=(VMEM, VMEM),
            compiler_params=PARAMS,
        )(keep, arrived, partial)
        arrived = swap(send, 0, 2 * bit)
    returned = keep[0] + arrived[0].astype(F32)
    adjoint_out = (adjoints.astype(F32) - returned).astype(BF16)

    forward_out = pl.pallas_call(
        functools.partial(forward_kernel, masks, count),
        out_shape=jax.ShapeDtypeStruct((rows, width), BF16),
        in_specs=[SMEM] + [VMEM] * (6 + len(held)),
        out_specs=VMEM,
        cost_estimate=work(SLOTS - EARLY + 8),
        compiler_params=PARAMS,
    )(place, fields, labels, weights, mats_plain, partial, all_fields, *held)
    return (forward_out, adjoint_out)


def solution(mesh):
    placed = (
        P("coef", "tiles"),
        P("coef", "tiles"),
        P(),
        P("tiles", "coef", None),
        P("tiles", None),
        P("tiles"),
    )
    return jax.shard_map(
        local,
        mesh=mesh,
        in_specs=placed,
        out_specs=(P("coef", "tiles"), P("coef", "tiles")),
        check_vma=False,
    )
```

```python
import functools

import jax
import jax.numpy as jnp
from jax import lax
from jax.experimental import pallas as pl
from jax.experimental.pallas import tpu as pltpu
from jax.sharding import PartitionSpec as P

SLOTS = 30
HW = 15
EDGE = 128
CHUNK = 5
EARLY = 22
LEAD = 16
A_SHIFT = 32
C_SHIFT = 64
OFFSETS = [slot - HW + (1 if slot >= HW else 0) for slot in range(SLOTS)]
BF16 = jnp.bfloat16
F32 = jnp.float32
VMEM = pl.BlockSpec(memory_space=pltpu.VMEM)
SMEM = pl.BlockSpec(memory_space=pltpu.SMEM)
ANY = pl.BlockSpec(memory_space=pl.ANY)
HBM = pl.BlockSpec(memory_space=pltpu.HBM)
PARAMS = pltpu.CompilerParams(vmem_limit_bytes=24 * 1024 * 1024)


def in_hbm(cells):
    return pltpu.with_memory_space_constraint(cells, pltpu.HBM)


def edges_of(cells):
    width = cells.shape[1]
    head, tail = cells[:, :EDGE], cells[:, width - EDGE :]
    lane = lax.broadcasted_iota(jnp.int32, head.shape, 1)
    return jnp.where(lane < EDGE // 2, head, tail)


def edge_parts(rows):
    return 2 if rows % 32 == 0 else 1


def pack_kernel(
    t_any, f_any, a_any, class_any, place, near_ref, far_ref, f_ref, a_ref, class_ref, t_ref, sems
):
    coef = lax.axis_index("coef")
    place[0] = lax.axis_index("tiles")
    place[1] = coef & 1
    place[2] = coef >> 1
    copies = [
        pltpu.make_async_copy(source, target, sems.at[at])
        for at, (source, target) in enumerate(
            ((t_any, t_ref), (f_any, f_ref), (a_any, a_ref), (class_any, class_ref))
        )
    ]
    for copy in copies:
        copy.start()
    for copy in copies:
        copy.wait()
    count, rows, depth = t_ref.shape
    mats = count * rows
    width = f_ref.shape[1]
    fields, adjoints = f_ref[...], a_ref[...]
    own = edges_of(fields).astype(F32)
    turned = pltpu.roll(edges_of(adjoints).astype(F32), A_SHIFT, 1)
    class_edge = pltpu.roll(
        jnp.broadcast_to(edges_of(class_ref[...]).astype(F32), (rows, EDGE)), C_SHIFT, 1
    )
    lane = lax.broadcasted_iota(jnp.int32, own.shape, 1)
    edge = jnp.where(
        (lane < HW) | (lane >= EDGE - HW),
        own,
        jnp.where((lane >= A_SHIFT - HW) & (lane < A_SHIFT + HW), turned, class_edge),
    ).astype(BF16)
    parts = edge_parts(rows)
    base = mats + rows // parts
    for out_ref in (near_ref, far_ref):
        out_ref[:mats, :] = t_ref[...].reshape(mats, depth)
        for part in range(parts):
            band = edge[part * (rows // parts) : (part + 1) * (rows // parts), :]
            out_ref[mats:base, part * EDGE : (part + 1) * EDGE] = band
        for part in range(parts, depth // EDGE):
            out_ref[mats:base, part * EDGE : (part + 1) * EDGE] = edge[: base - mats, :]
    for part in range(width // depth):
        lanes = slice(part * depth, (part + 1) * depth)
        far_ref[base + 2 * part * rows : base + (2 * part + 1) * rows, :] = fields[:, lanes]
        far_ref[base + (2 * part + 1) * rows : base + (2 * part + 2) * rows, :] = adjoints[:, lanes]


def relay_kernel(near_ref, top_ref, far_ref, cross_ref, after_ref, out_ref):
    rows = near_ref.shape[0]
    out_ref[0] = near_ref[...]
    out_ref[1] = top_ref[...]
    out_ref[2] = far_ref[:rows, :]
    out_ref[3] = cross_ref[...]


def merge_kernel(keep_ref, arrived_ref, after_ref, kept_ref, send_ref):
    half = kept_ref.shape[0]
    kept_ref[...] = keep_ref[:half] + arrived_ref[:half].astype(F32)
    send_ref[...] = (keep_ref[half:] + arrived_ref[half:].astype(F32)).astype(BF16)


def pick_halo(place, pieces, masks, mats, rows):
    tile = place[0]
    parts = edge_parts(rows)
    lane = lax.broadcasted_iota(jnp.int32, (rows, EDGE), 1)
    above = jnp.zeros((rows, EDGE), F32)
    below = jnp.zeros((rows, EDGE), F32)
    for (piece_ref, at), mask in zip(pieces, masks):
        bands = [
            piece_ref[at, mats : mats + rows // parts, part * EDGE : (part + 1) * EDGE]
            for part in range(parts)
        ]
        cells = jnp.concatenate(bands, axis=0).astype(F32)
        owner = tile ^ mask
        above = jnp.where(owner == tile + 1, cells, above)
        below = jnp.where(owner == tile - 1, cells, below)
    return above, below


def join_halo(halo, shift):
    above, below = halo
    lane = lax.broadcasted_iota(jnp.int32, above.shape, 1)
    back = (EDGE - shift) % EDGE
    if back:
        above, below = pltpu.roll(above, back, 1), pltpu.roll(below, back, 1)
    return jnp.where(lane < EDGE // 2, above, below)


def split_pieces(refs):
    near = [(ref, at) for ref in refs for at in (0, 1)]
    across = [(ref, at) for ref in refs for at in (2, 3)]
    return near, across


def fields_kernel(masks, count, place, f_ref, far_ref, *refs):
    (near, across), out_ref = split_pieces(refs[:-1]), refs[-1]
    rows, width = f_ref.shape
    depth = far_ref.shape[1]
    mats = count * rows
    base = mats + rows // edge_parts(rows)
    first = pl.multiple_of(place[1] * rows, rows)
    second = pl.multiple_of((1 - place[1]) * rows, rows)
    out_ref[pl.ds(first, rows), :width] = f_ref[...]
    halo = join_halo(pick_halo(place, near, masks, mats, rows), 0)
    out_ref[pl.ds(first, rows), width:] = halo.astype(BF16)
    for part in range(width // depth):
        out_ref[pl.ds(second, rows), part * depth : (part + 1) * depth] = far_ref[
            base + 2 * part * rows : base + (2 * part + 1) * rows, :
        ]
    halo = join_halo(pick_halo(place, across, masks, mats, rows), 0)
    out_ref[pl.ds(second, rows), width:] = halo.astype(BF16)


def prepare_kernel(couple_ref, weight_ref, after_ref, mats_ref, spread_ref, sems):
    copies = []
    for chunk in range(SLOTS // CHUNK):
        span = pl.ds(chunk * CHUNK, CHUNK)
        copies.append(pltpu.make_async_copy(couple_ref.at[span], mats_ref.at[span], sems.at[chunk]))
    for copy in copies:
        copy.start()
    weights = weight_ref[...].astype(F32).astype(BF16)
    row = lax.broadcasted_iota(jnp.int32, (weights.shape[0], 2 * EDGE), 0)
    lane = lax.broadcasted_iota(jnp.int32, (weights.shape[0], 2 * EDGE), 1)
    for pair in range(SLOTS // 2):
        chosen = row == 2 * pair + (lane >= EDGE).astype(jnp.int32)
        unit = jnp.where(chosen, 1.0, 0.0).astype(BF16)
        spread = lax.dot_general(
            weights, unit, (((0,), (0,)), ((), ())), preferred_element_type=F32
        ).astype(BF16)
        spread_ref[2 * pair] = spread[:, :EDGE]
        spread_ref[2 * pair + 1] = spread[:, EDGE:]
    for copy in copies:
        copy.wait()


def stand_up(cells, upright):
    width = cells.shape[1] - EDGE
    turned = cells.astype(F32).T
    for half in range(upright.shape[0]):
        lanes = slice(half * EDGE, (half + 1) * EDGE)
        upright[half, LEAD : LEAD + width, :] = turned[:width, lanes]
        upright[half, LEAD + width :, :] = turned[width : width + LEAD, lanes]
        upright[half, :LEAD, :] = turned[width + EDGE - LEAD :, lanes]


def couple_slots(upright, spread_ref, mats_ref, slots, adjoint_mode, total=None):
    width = spread_ref.shape[1]
    for slot in slots:
        start = LEAD + OFFSETS[slot]
        weight = spread_ref[slot]
        selected = jnp.concatenate(
            [
                upright[half, start : start + width, :].astype(BF16) * weight
                for half in range(upright.shape[0])
            ],
            axis=1,
        )
        mat = mats_ref[SLOTS - 1 - slot if adjoint_mode else slot]
        dims = (((1,), (0 if adjoint_mode else 1,)), ((), ()))
        product = lax.dot_general(selected, mat, dims, preferred_element_type=F32)
        total = product if total is None else total + product
    return total


def adjoint_kernel(
    masks, count, place, a_ref, far_ref, class_ref, spread_ref, mats_ref, after_ref, *refs
):
    half = len(masks)
    near, across = split_pieces(refs[:-6])
    send_ref, keep_ref, total_ref, expanded, stacked, upright = refs[-6:]
    rows, width = a_ref.shape
    depth = far_ref.shape[1]
    mats = count * rows
    base = mats + rows // edge_parts(rows)
    far_own = jnp.concatenate(
        [
            far_ref[base + (2 * part + 1) * rows : base + (2 * part + 2) * rows, :]
            for part in range(width // depth)
        ],
        axis=1,
    )
    halos = [pick_halo(place, pieces, masks, mats, rows) for pieces in (near, across)]
    padded = [
        jnp.concatenate([own, join_halo(halo, A_SHIFT).astype(BF16)], axis=1)
        for own, halo in ((a_ref[...], halos[0]), (far_own, halos[1]))
    ]
    class_halo = join_halo(tuple(cells[0:8, :] for cells in halos[0]), C_SHIFT)
    labels = jnp.concatenate([class_ref[...], class_halo[0:1, :].astype(jnp.int32)], axis=1)
    at = 0
    for piece in range(half):
        for which, pieces in ((0, near), (1, across)):
            ref, spot = pieces[piece]
            stacked[at : at + mats, :] = ref[spot, :mats, :]
            for local_class in range(count):
                hit = labels == (place[0] ^ masks[piece]) * count + local_class
                factor = jnp.where(hit, 1.0, 0.0).astype(BF16)
                expanded[at : at + rows, :] = padded[which] * factor
                at += rows
    scattered = lax.dot_general(
        stacked[...], expanded[...], (((0,), (0,)), ((), ())), preferred_element_type=F32
    )
    stand_up(scattered.astype(BF16), upright)
    total_ref[...] = couple_slots(upright, spread_ref, mats_ref, range(SLOTS), True).T
    steps = keep_ref.shape[0]
    for rel in range(steps):
        start = pl.multiple_of(((place[2] ^ rel) * 2 + place[1]) * rows, rows)
        keep_ref[rel] = total_ref[pl.ds(start, rows), :]
        start = pl.multiple_of(((place[2] ^ (rel + steps)) * 2 + place[1]) * rows, rows)
        send_ref[rel] = total_ref[pl.ds(start, rows), :].astype(BF16)


def gather_kernel(rels, place, spread_ref, mats_ref, *refs):
    pieces, total_ref, upright, padded = refs[:-3], refs[-3], refs[-2], refs[-1]
    block = pieces[0].shape[0]
    for rel, piece_ref in zip(rels, pieces):
        start = pl.multiple_of((place[2] ^ rel) * block, block)
        padded[pl.ds(start, block), :] = piece_ref[...]
    stand_up(padded[...], upright)
    total_ref[...] = couple_slots(upright, spread_ref, mats_ref, range(EARLY), False)


def forward_kernel(masks, count, place, f_ref, class_ref, spread_ref, mats_ref, total_ref, upright, *refs):
    (near, across), out_ref = split_pieces(refs[:-1]), refs[-1]
    rows, width = f_ref.shape
    mats = count * rows
    coupled = couple_slots(
        upright, spread_ref, mats_ref, range(EARLY, SLOTS), False, total_ref[...]
    ).astype(BF16)
    applied = jnp.zeros((rows, width), F32)
    labels = class_ref[...]
    for piece in range(len(masks)):
        ref, spot = near[piece]
        product = lax.dot_general(
            ref[spot, :mats, :], coupled, (((1,), (1,)), ((), ())), preferred_element_type=F32
        )
        for local_class in range(count):
            hit = labels == (place[0] ^ masks[piece]) * count + local_class
            applied = jnp.where(hit, product[local_class * rows : (local_class + 1) * rows, :], applied)
    out_ref[...] = (f_ref[...].astype(F32) - applied).astype(BF16)


def local(fields, adjoints, couple, tmatrices, neighbours, classes):
    tiles, coefs = lax.axis_size("tiles"), lax.axis_size("coef")
    rows, width = fields.shape
    count, unused, depth = tmatrices.shape

    def swap(cells, tile_mask, coef_mask):
        pairs = [
            (i * coefs + j, (i ^ tile_mask) * coefs + (j ^ coef_mask))
            for i in range(tiles)
            for j in range(coefs)
        ]
        return lax.ppermute(cells, ("tiles", "coef"), pairs)

    weights = (neighbours >= 0).astype(BF16).T
    weights = jnp.pad(weights, ((0, -SLOTS % 16), (0, 0)))
    labels = classes.reshape(1, width)
    mats = count * rows
    near_rows = mats + rows // edge_parts(rows)
    far_rows = near_rows + 2 * rows * (width // depth)
    place, near_own, far_own, fields, adjoints, labels = pl.pallas_call(
        pack_kernel,
        out_shape=(
            jax.ShapeDtypeStruct((3,), jnp.int32),
            jax.ShapeDtypeStruct((near_rows, depth), BF16),
            jax.ShapeDtypeStruct((far_rows, depth), BF16),
            jax.ShapeDtypeStruct(fields.shape, BF16),
            jax.ShapeDtypeStruct(adjoints.shape, BF16),
            jax.ShapeDtypeStruct(labels.shape, jnp.int32),
        ),
        in_specs=[HBM] * 4,
        out_specs=(SMEM,) + (VMEM,) * 5,
        scratch_shapes=[pltpu.VMEM(tmatrices.shape, BF16), pltpu.SemaphoreType.DMA((4,))],
        compiler_params=PARAMS,
    )(*[in_hbm(cells) for cells in (tmatrices, fields, adjoints, labels)])
    mats_held, spread = pl.pallas_call(
        prepare_kernel,
        out_shape=(
            jax.ShapeDtypeStruct(couple.shape, BF16),
            jax.ShapeDtypeStruct((SLOTS, width, EDGE), BF16),
        ),
        in_specs=[HBM, VMEM, SMEM],
        out_specs=(VMEM, VMEM),
        scratch_shapes=[pltpu.SemaphoreType.DMA((SLOTS // CHUNK,))],
        cost_estimate=pl.CostEstimate(flops=0, bytes_accessed=4 * couple.size, transcendentals=0),
        compiler_params=PARAMS,
    )(in_hbm(couple), weights, place)

    top = tiles // 2
    far = swap(far_own, 0, 1)
    first = pl.pallas_call(
        relay_kernel,
        out_shape=jax.ShapeDtypeStruct((4, near_rows, depth), BF16),
        in_specs=[VMEM] * 5,
        out_specs=VMEM,
        compiler_params=PARAMS,
    )(near_own, swap(near_own, top, 0), far, swap(near_own, top, 1), mats_held)
    held, lows = [first], [0]
    bit = top // 2
    while bit >= 1:
        held += [swap(block, bit, 0) for block in held]
        lows += [low ^ bit for low in lows]
        bit //= 2
    masks = [low ^ high for low in lows for high in (0, top)]

    padded_fields = pl.pallas_call(
        functools.partial(fields_kernel, masks, count),
        out_shape=jax.ShapeDtypeStruct((2 * rows, width + EDGE), BF16),
        in_specs=[SMEM] + [VMEM] * (2 + len(held)),
        out_specs=VMEM,
        compiler_params=PARAMS,
    )(place, fields, far, *held)

    groups = coefs // 2
    gathered = {0: padded_fields}
    for rel in range(1, groups):
        gathered[rel] = swap(padded_fields, 0, 2 * rel)
    rels = sorted(gathered)

    steps = groups // 2
    total_rows = couple.shape[1]

    def work(slots):
        size = slots * total_rows * total_rows
        return pl.CostEstimate(flops=2 * size * width, bytes_accessed=2 * size, transcendentals=0)

    send, keep = pl.pallas_call(
        functools.partial(adjoint_kernel, masks, count),
        out_shape=(
            jax.ShapeDtypeStruct((steps, rows, width), BF16),
            jax.ShapeDtypeStruct((steps, rows, width), F32),
        ),
        in_specs=[SMEM] + [VMEM] * 5 + [ANY] + [VMEM] * len(held),
        out_specs=(VMEM, VMEM),
        scratch_shapes=[
            pltpu.VMEM((total_rows, width), F32),
            pltpu.VMEM((2 * len(masks) * mats, width + EDGE), BF16),
            pltpu.VMEM((2 * len(masks) * mats, depth), BF16),
            pltpu.VMEM((total_rows // EDGE, width + 2 * LEAD, EDGE), F32),
        ],
        cost_estimate=work(SLOTS + 8),
        compiler_params=PARAMS,
    )(place, adjoints, far, labels, spread, mats_held, padded_fields, *held)

    partial, all_fields = pl.pallas_call(
        functools.partial(gather_kernel, rels),
        out_shape=(
            jax.ShapeDtypeStruct((width, total_rows), F32),
            jax.ShapeDtypeStruct((total_rows // EDGE, width + 2 * LEAD, EDGE), F32),
        ),
        in_specs=[SMEM] + [VMEM] * (2 + len(rels)),
        out_specs=(VMEM, VMEM),
        scratch_shapes=[pltpu.VMEM((total_rows, width + EDGE), BF16)],
        cost_estimate=work(EARLY),
        compiler_params=PARAMS,
    )(place, spread, mats_held, *[gathered[rel] for rel in rels])
    bit = groups // 2
    arrived = swap(send, 0, 2 * bit)
    while bit > 1:
        bit //= 2
        keep, send = pl.pallas_call(
            merge_kernel,
            out_shape=(
                jax.ShapeDtypeStruct((bit, rows, width), F32),
                jax.ShapeDtypeStruct((bit, rows, width), BF16),
            ),
            in_specs=[VMEM] * 3,
            out_specs=(VMEM, VMEM),
            compiler_params=PARAMS,
        )(keep, arrived, partial)
        arrived = swap(send, 0, 2 * bit)
    returned = keep[0] + arrived[0].astype(F32)
    adjoint_out = (adjoints.astype(F32) - returned).astype(BF16)

    forward_out = pl.pallas_call(
        functools.partial(forward_kernel, masks, count),
        out_shape=jax.ShapeDtypeStruct((rows, width), BF16),
        in_specs=[SMEM] + [VMEM] * (6 + len(held)),
        out_specs=VMEM,
        cost_estimate=work(SLOTS - EARLY + 8),
        compiler_params=PARAMS,
    )(place, fields, labels, spread, mats_held, partial, all_fields, *held)
    return (forward_out, adjoint_out)


def solution(mesh):
    placed = (
        P("coef", "tiles"),
        P("coef", "tiles"),
        P(),
        P("tiles", "coef", None),
        P("tiles", None),
        P("tiles"),
    )
    return jax.shard_map(
        local,
        mesh=mesh,
        in_specs=placed,
        out_specs=(P("coef", "tiles"), P("coef", "tiles")),
        check_vma=False,
    )
```

```python
import functools

import jax
import jax.numpy as jnp
from jax import lax
from jax.experimental import pallas as pl
from jax.experimental.pallas import tpu as pltpu
from jax.sharding import PartitionSpec as P

SLOTS = 30
HW = 15
EDGE = 128
CHUNK = 5
EARLY = 22
LEAD = 16
A_SHIFT = 32
C_SHIFT = 64
OFFSETS = [slot - HW + (1 if slot >= HW else 0) for slot in range(SLOTS)]
BF16 = jnp.bfloat16
F32 = jnp.float32
VMEM = pl.BlockSpec(memory_space=pltpu.VMEM)
SMEM = pl.BlockSpec(memory_space=pltpu.SMEM)
ANY = pl.BlockSpec(memory_space=pl.ANY)
HBM = pl.BlockSpec(memory_space=pltpu.HBM)
PARAMS = pltpu.CompilerParams(vmem_limit_bytes=24 * 1024 * 1024)


def in_hbm(cells):
    return pltpu.with_memory_space_constraint(cells, pltpu.HBM)


def edges_of(cells):
    width = cells.shape[1]
    head, tail = cells[:, :EDGE], cells[:, width - EDGE :]
    lane = lax.broadcasted_iota(jnp.int32, head.shape, 1)
    return jnp.where(lane < EDGE // 2, head, tail)


def edge_parts(rows):
    return 2 if rows % 32 == 0 else 1


def pack_kernel(
    t_any, f_any, a_any, class_any, place, near_ref, far_ref, f_ref, a_ref, class_ref, t_ref, sems
):
    coef = lax.axis_index("coef")
    place[0] = lax.axis_index("tiles")
    place[1] = coef & 1
    place[2] = coef >> 1
    copies = [
        pltpu.make_async_copy(source, target, sems.at[at])
        for at, (source, target) in enumerate(
            ((t_any, t_ref), (f_any, f_ref), (a_any, a_ref), (class_any, class_ref))
        )
    ]
    for copy in copies:
        copy.start()
    for copy in copies:
        copy.wait()
    count, rows, depth = t_ref.shape
    mats = count * rows
    width = f_ref.shape[1]
    fields, adjoints = f_ref[...], a_ref[...]
    own = edges_of(fields).astype(F32)
    turned = pltpu.roll(edges_of(adjoints).astype(F32), A_SHIFT, 1)
    class_edge = pltpu.roll(
        jnp.broadcast_to(edges_of(class_ref[...]).astype(F32), (rows, EDGE)), C_SHIFT, 1
    )
    lane = lax.broadcasted_iota(jnp.int32, own.shape, 1)
    edge = jnp.where(
        (lane < HW) | (lane >= EDGE - HW),
        own,
        jnp.where((lane >= A_SHIFT - HW) & (lane < A_SHIFT + HW), turned, class_edge),
    ).astype(BF16)
    parts = edge_parts(rows)
    base = mats + rows // parts
    for out_ref in (near_ref, far_ref):
        out_ref[:mats, :] = t_ref[...].reshape(mats, depth)
        for part in range(parts):
            band = edge[part * (rows // parts) : (part + 1) * (rows // parts), :]
            out_ref[mats:base, part * EDGE : (part + 1) * EDGE] = band
        for part in range(parts, depth // EDGE):
            out_ref[mats:base, part * EDGE : (part + 1) * EDGE] = edge[: base - mats, :]
    for part in range(width // depth):
        lanes = slice(part * depth, (part + 1) * depth)
        far_ref[base + 2 * part * rows : base + (2 * part + 1) * rows, :] = fields[:, lanes]
        far_ref[base + (2 * part + 1) * rows : base + (2 * part + 2) * rows, :] = adjoints[:, lanes]


def relay_kernel(far_ref, cross_ref, top_ref, near_ref, after_ref, out_ref):
    rows = near_ref.shape[0]
    out_ref[0] = near_ref[...]
    out_ref[1] = top_ref[...]
    out_ref[2] = far_ref[:rows, :]
    out_ref[3] = cross_ref[...]


def merge_kernel(keep_ref, arrived_ref, after_ref, kept_ref, send_ref):
    half = kept_ref.shape[0]
    kept_ref[...] = keep_ref[:half] + arrived_ref[:half].astype(F32)
    send_ref[...] = (keep_ref[half:] + arrived_ref[half:].astype(F32)).astype(BF16)


def pick_halo(place, pieces, masks, mats, rows):
    tile = place[0]
    parts = edge_parts(rows)
    lane = lax.broadcasted_iota(jnp.int32, (rows, EDGE), 1)
    above = jnp.zeros((rows, EDGE), F32)
    below = jnp.zeros((rows, EDGE), F32)
    for (piece_ref, at), mask in zip(pieces, masks):
        bands = [
            piece_ref[at, mats : mats + rows // parts, part * EDGE : (part + 1) * EDGE]
            for part in range(parts)
        ]
        cells = jnp.concatenate(bands, axis=0).astype(F32)
        owner = tile ^ mask
        above = jnp.where(owner == tile + 1, cells, above)
        below = jnp.where(owner == tile - 1, cells, below)
    return above, below


def join_halo(halo, shift):
    above, below = halo
    lane = lax.broadcasted_iota(jnp.int32, above.shape, 1)
    back = (EDGE - shift) % EDGE
    if back:
        above, below = pltpu.roll(above, back, 1), pltpu.roll(below, back, 1)
    return jnp.where(lane < EDGE // 2, above, below)


def split_pieces(refs):
    near = [(ref, at) for ref in refs for at in (0, 1)]
    across = [(ref, at) for ref in refs for at in (2, 3)]
    return near, across


def fields_kernel(masks, count, place, f_ref, *refs):
    (near, across), far_ref, out_ref = split_pieces(refs[:-2]), refs[-2], refs[-1]
    rows, width = f_ref.shape
    depth = far_ref.shape[1]
    mats = count * rows
    base = mats + rows // edge_parts(rows)
    first = pl.multiple_of(place[1] * rows, rows)
    second = pl.multiple_of((1 - place[1]) * rows, rows)
    out_ref[pl.ds(first, rows), :width] = f_ref[...]
    halo = join_halo(pick_halo(place, near, masks, mats, rows), 0)
    out_ref[pl.ds(first, rows), width:] = halo.astype(BF16)
    for part in range(width // depth):
        out_ref[pl.ds(second, rows), part * depth : (part + 1) * depth] = far_ref[
            base + 2 * part * rows : base + (2 * part + 1) * rows, :
        ]
    halo = join_halo(pick_halo(place, across, masks, mats, rows), 0)
    out_ref[pl.ds(second, rows), width:] = halo.astype(BF16)


def prepare_kernel(couple_ref, weight_ref, after_ref, mats_ref, spread_ref, sems):
    copies = []
    for chunk in range(SLOTS // CHUNK):
        span = pl.ds(chunk * CHUNK, CHUNK)
        copies.append(pltpu.make_async_copy(couple_ref.at[span], mats_ref.at[span], sems.at[chunk]))
    for copy in copies:
        copy.start()
    weights = weight_ref[...].astype(F32).astype(BF16)
    row = lax.broadcasted_iota(jnp.int32, (weights.shape[0], 2 * EDGE), 0)
    lane = lax.broadcasted_iota(jnp.int32, (weights.shape[0], 2 * EDGE), 1)
    for pair in range(SLOTS // 2):
        chosen = row == 2 * pair + (lane >= EDGE).astype(jnp.int32)
        unit = jnp.where(chosen, 1.0, 0.0).astype(BF16)
        spread = lax.dot_general(
            weights, unit, (((0,), (0,)), ((), ())), preferred_element_type=F32
        ).astype(BF16)
        spread_ref[2 * pair] = spread[:, :EDGE]
        spread_ref[2 * pair + 1] = spread[:, EDGE:]
    for copy in copies:
        copy.wait()


def stand_up(cells, upright):
    width = cells.shape[1] - EDGE
    turned = cells.astype(F32).T
    for half in range(upright.shape[0]):
        lanes = slice(half * EDGE, (half + 1) * EDGE)
        upright[half, LEAD : LEAD + width, :] = turned[:width, lanes]
        upright[half, LEAD + width :, :] = turned[width : width + LEAD, lanes]
        upright[half, :LEAD, :] = turned[width + EDGE - LEAD :, lanes]


def couple_slots(upright, spread_ref, mats_ref, slots, adjoint_mode, total=None):
    width = spread_ref.shape[1]
    for slot in slots:
        start = LEAD + OFFSETS[slot]
        weight = spread_ref[slot]
        selected = jnp.concatenate(
            [
                upright[half, start : start + width, :].astype(BF16) * weight
                for half in range(upright.shape[0])
            ],
            axis=1,
        )
        mat = mats_ref[SLOTS - 1 - slot if adjoint_mode else slot]
        dims = (((1,), (0 if adjoint_mode else 1,)), ((), ()))
        product = lax.dot_general(selected, mat, dims, preferred_element_type=F32)
        total = product if total is None else total + product
    return total


def adjoint_kernel(
    masks, count, place, a_ref, far_ref, class_ref, spread_ref, mats_ref, after_ref, *refs
):
    half = len(masks)
    near, across = split_pieces(refs[:-6])
    send_ref, keep_ref, total_ref, expanded, stacked, upright = refs[-6:]
    rows, width = a_ref.shape
    depth = far_ref.shape[1]
    mats = count * rows
    base = mats + rows // edge_parts(rows)
    far_own = jnp.concatenate(
        [
            far_ref[base + (2 * part + 1) * rows : base + (2 * part + 2) * rows, :]
            for part in range(width // depth)
        ],
        axis=1,
    )
    halos = [pick_halo(place, pieces, masks, mats, rows) for pieces in (near, across)]
    padded = [
        jnp.concatenate([own, join_halo(halo, A_SHIFT).astype(BF16)], axis=1)
        for own, halo in ((a_ref[...], halos[0]), (far_own, halos[1]))
    ]
    class_halo = join_halo(tuple(cells[0:8, :] for cells in halos[0]), C_SHIFT)
    labels = jnp.concatenate([class_ref[...], class_halo[0:1, :].astype(jnp.int32)], axis=1)
    at = 0
    for piece in range(half):
        for which, pieces in ((0, near), (1, across)):
            ref, spot = pieces[piece]
            stacked[at : at + mats, :] = ref[spot, :mats, :]
            for local_class in range(count):
                hit = labels == (place[0] ^ masks[piece]) * count + local_class
                factor = jnp.where(hit, 1.0, 0.0).astype(BF16)
                expanded[at : at + rows, :] = padded[which] * factor
                at += rows
    scattered = lax.dot_general(
        stacked[...], expanded[...], (((0,), (0,)), ((), ())), preferred_element_type=F32
    )
    stand_up(scattered.astype(BF16), upright)
    total_ref[...] = couple_slots(upright, spread_ref, mats_ref, range(SLOTS), True).T
    steps = keep_ref.shape[0]
    for rel in range(steps):
        start = pl.multiple_of(((place[2] ^ rel) * 2 + place[1]) * rows, rows)
        keep_ref[rel] = total_ref[pl.ds(start, rows), :]
        start = pl.multiple_of(((place[2] ^ (rel + steps)) * 2 + place[1]) * rows, rows)
        send_ref[rel] = total_ref[pl.ds(start, rows), :].astype(BF16)


def gather_kernel(rels, place, spread_ref, mats_ref, *refs):
    pieces, total_ref, upright, padded = refs[:-3], refs[-3], refs[-2], refs[-1]
    block = pieces[0].shape[0]
    for rel, piece_ref in zip(rels, pieces):
        start = pl.multiple_of((place[2] ^ rel) * block, block)
        padded[pl.ds(start, block), :] = piece_ref[...]
    stand_up(padded[...], upright)
    total_ref[...] = couple_slots(upright, spread_ref, mats_ref, range(EARLY), False)


def forward_kernel(masks, count, place, f_ref, class_ref, spread_ref, mats_ref, total_ref, upright, *refs):
    (near, across), out_ref = split_pieces(refs[:-1]), refs[-1]
    rows, width = f_ref.shape
    mats = count * rows
    coupled = couple_slots(
        upright, spread_ref, mats_ref, range(EARLY, SLOTS), False, total_ref[...]
    ).astype(BF16)
    applied = jnp.zeros((rows, width), F32)
    labels = class_ref[...]
    for piece in range(len(masks)):
        ref, spot = near[piece]
        product = lax.dot_general(
            ref[spot, :mats, :], coupled, (((1,), (1,)), ((), ())), preferred_element_type=F32
        )
        for local_class in range(count):
            hit = labels == (place[0] ^ masks[piece]) * count + local_class
            applied = jnp.where(hit, product[local_class * rows : (local_class + 1) * rows, :], applied)
    out_ref[...] = (f_ref[...].astype(F32) - applied).astype(BF16)


def local(fields, adjoints, couple, tmatrices, neighbours, classes):
    tiles, coefs = lax.axis_size("tiles"), lax.axis_size("coef")
    rows, width = fields.shape
    count, unused, depth = tmatrices.shape

    def swap(cells, tile_mask, coef_mask):
        pairs = [
            (i * coefs + j, (i ^ tile_mask) * coefs + (j ^ coef_mask))
            for i in range(tiles)
            for j in range(coefs)
        ]
        return lax.ppermute(cells, ("tiles", "coef"), pairs)

    weights = (neighbours >= 0).astype(BF16).T
    weights = jnp.pad(weights, ((0, -SLOTS % 16), (0, 0)))
    labels = classes.reshape(1, width)
    mats = count * rows
    near_rows = mats + rows // edge_parts(rows)
    far_rows = near_rows + 2 * rows * (width // depth)
    place, near_own, far_own, fields, adjoints, labels = pl.pallas_call(
        pack_kernel,
        out_shape=(
            jax.ShapeDtypeStruct((3,), jnp.int32),
            jax.ShapeDtypeStruct((near_rows, depth), BF16),
            jax.ShapeDtypeStruct((far_rows, depth), BF16),
            jax.ShapeDtypeStruct(fields.shape, BF16),
            jax.ShapeDtypeStruct(adjoints.shape, BF16),
            jax.ShapeDtypeStruct(labels.shape, jnp.int32),
        ),
        in_specs=[HBM] * 4,
        out_specs=(SMEM,) + (VMEM,) * 5,
        scratch_shapes=[pltpu.VMEM(tmatrices.shape, BF16), pltpu.SemaphoreType.DMA((4,))],
        compiler_params=PARAMS,
    )(*[in_hbm(cells) for cells in (tmatrices, fields, adjoints, labels)])
    mats_held, spread = pl.pallas_call(
        prepare_kernel,
        out_shape=(
            jax.ShapeDtypeStruct(couple.shape, BF16),
            jax.ShapeDtypeStruct((SLOTS, width, EDGE), BF16),
        ),
        in_specs=[HBM, VMEM, SMEM],
        out_specs=(VMEM, VMEM),
        scratch_shapes=[pltpu.SemaphoreType.DMA((SLOTS // CHUNK,))],
        cost_estimate=pl.CostEstimate(flops=0, bytes_accessed=4 * couple.size, transcendentals=0),
        compiler_params=PARAMS,
    )(in_hbm(couple), weights, place)

    top = tiles // 2
    far = swap(far_own, 0, 1)
    first = pl.pallas_call(
        relay_kernel,
        out_shape=jax.ShapeDtypeStruct((4, near_rows, depth), BF16),
        in_specs=[VMEM] * 5,
        out_specs=VMEM,
        compiler_params=PARAMS,
    )(far, swap(near_own, top, 1), swap(near_own, top, 0), near_own, mats_held)
    held, lows = [first], [0]
    bit = top // 2
    while bit >= 1:
        held += [swap(block, bit, 0) for block in held]
        lows += [low ^ bit for low in lows]
        bit //= 2
    masks = [low ^ high for low in lows for high in (0, top)]

    padded_fields = pl.pallas_call(
        functools.partial(fields_kernel, masks, count),
        out_shape=jax.ShapeDtypeStruct((2 * rows, width + EDGE), BF16),
        in_specs=[SMEM] + [VMEM] * (2 + len(held)),
        out_specs=VMEM,
        compiler_params=PARAMS,
    )(place, fields, *held, far)

    groups = coefs // 2
    gathered = {0: padded_fields}
    for rel in range(1, groups):
        gathered[rel] = swap(padded_fields, 0, 2 * rel)
    rels = sorted(gathered, reverse=True)

    steps = groups // 2
    total_rows = couple.shape[1]

    def work(slots):
        size = slots * total_rows * total_rows
        return pl.CostEstimate(flops=2 * size * width, bytes_accessed=2 * size, transcendentals=0)

    send, keep = pl.pallas_call(
        functools.partial(adjoint_kernel, masks, count),
        out_shape=(
            jax.ShapeDtypeStruct((steps, rows, width), BF16),
            jax.ShapeDtypeStruct((steps, rows, width), F32),
        ),
        in_specs=[SMEM] + [VMEM] * 5 + [ANY] + [VMEM] * len(held),
        out_specs=(VMEM, VMEM),
        scratch_shapes=[
            pltpu.VMEM((total_rows, width), F32),
            pltpu.VMEM((2 * len(masks) * mats, width + EDGE), BF16),
            pltpu.VMEM((2 * len(masks) * mats, depth), BF16),
            pltpu.VMEM((total_rows // EDGE, width + 2 * LEAD, EDGE), F32),
        ],
        cost_estimate=work(SLOTS + 8),
        compiler_params=PARAMS,
    )(place, adjoints, far, labels, spread, mats_held, padded_fields, *held)

    partial, all_fields = pl.pallas_call(
        functools.partial(gather_kernel, rels),
        out_shape=(
            jax.ShapeDtypeStruct((width, total_rows), F32),
            jax.ShapeDtypeStruct((total_rows // EDGE, width + 2 * LEAD, EDGE), F32),
        ),
        in_specs=[SMEM] + [VMEM] * (2 + len(rels)),
        out_specs=(VMEM, VMEM),
        scratch_shapes=[pltpu.VMEM((total_rows, width + EDGE), BF16)],
        cost_estimate=work(EARLY),
        compiler_params=PARAMS,
    )(place, spread, mats_held, *[gathered[rel] for rel in rels])
    bit = groups // 2
    arrived = swap(send, 0, 2 * bit)
    while bit > 1:
        bit //= 2
        keep, send = pl.pallas_call(
            merge_kernel,
            out_shape=(
                jax.ShapeDtypeStruct((bit, rows, width), F32),
                jax.ShapeDtypeStruct((bit, rows, width), BF16),
            ),
            in_specs=[VMEM] * 3,
            out_specs=(VMEM, VMEM),
            compiler_params=PARAMS,
        )(keep, arrived, partial)
        arrived = swap(send, 0, 2 * bit)
    returned = keep[0] + arrived[0].astype(F32)
    adjoint_out = (adjoints.astype(F32) - returned).astype(BF16)

    forward_out = pl.pallas_call(
        functools.partial(forward_kernel, masks, count),
        out_shape=jax.ShapeDtypeStruct((rows, width), BF16),
        in_specs=[SMEM] + [VMEM] * (6 + len(held)),
        out_specs=VMEM,
        cost_estimate=work(SLOTS - EARLY + 8),
        compiler_params=PARAMS,
    )(place, fields, labels, spread, mats_held, partial, all_fields, *held)
    return (forward_out, adjoint_out)


def solution(mesh):
    placed = (
        P("coef", "tiles"),
        P("coef", "tiles"),
        P(),
        P("tiles", "coef", None),
        P("tiles", None),
        P("tiles"),
    )
    return jax.shard_map(
        local,
        mesh=mesh,
        in_specs=placed,
        out_specs=(P("coef", "tiles"), P("coef", "tiles")),
        check_vma=False,
    )
```

```python
import functools

import jax
import jax.numpy as jnp
from jax import lax
from jax.experimental import pallas as pl
from jax.experimental.pallas import tpu as pltpu
from jax.sharding import PartitionSpec as P

SLOTS = 30
HW = 15
EDGE = 128
CHUNK = 5
LEAD = 16
BAND = 128
A_SHIFT = 32
C_SHIFT = 64
OFFSETS = [slot - HW + (1 if slot >= HW else 0) for slot in range(SLOTS)]
BF16 = jnp.bfloat16
F32 = jnp.float32
VMEM = pl.BlockSpec(memory_space=pltpu.VMEM)
SMEM = pl.BlockSpec(memory_space=pltpu.SMEM)
ANY = pl.BlockSpec(memory_space=pl.ANY)
HBM = pl.BlockSpec(memory_space=pltpu.HBM)
PARAMS = pltpu.CompilerParams(vmem_limit_bytes=24 * 1024 * 1024)


def in_hbm(cells):
    return pltpu.with_memory_space_constraint(cells, pltpu.HBM)


def edges_of(cells):
    width = cells.shape[1]
    head, tail = cells[:, :EDGE], cells[:, width - EDGE :]
    lane = lax.broadcasted_iota(jnp.int32, head.shape, 1)
    return jnp.where(lane < EDGE // 2, head, tail)


def edge_parts(rows):
    return 2 if rows % 32 == 0 else 1


def far_spans(base, rows, width, depth, which):
    starts = [base + (2 * part + which) * rows for part in range(width // depth)]
    return [slice(start, start + rows) for start in starts]


def far_cells(far_ref, base, rows, width, which):
    spans = far_spans(base, rows, width, far_ref.shape[1], which)
    return jnp.concatenate([far_ref[span, :] for span in spans], axis=1)


def pack_kernel(
    t_any, f_any, a_any, class_any, place, near_ref, far_ref, both_ref, class_ref, t_ref, sems
):
    coef = lax.axis_index("coef")
    place[0] = lax.axis_index("tiles")
    place[1] = coef & 1
    place[2] = coef >> 1
    copies = [
        pltpu.make_async_copy(source, target, sems.at[at])
        for at, (source, target) in enumerate(
            (
                (t_any, t_ref),
                (f_any, both_ref.at[0]),
                (a_any, both_ref.at[1]),
                (class_any, class_ref),
            )
        )
    ]
    for copy in copies:
        copy.start()
    for copy in copies:
        copy.wait()
    count, rows, depth = t_ref.shape
    mats = count * rows
    fields, adjoints = both_ref[0], both_ref[1]
    own = edges_of(fields).astype(F32)
    turned = pltpu.roll(edges_of(adjoints).astype(F32), A_SHIFT, 1)
    class_edge = pltpu.roll(
        jnp.broadcast_to(edges_of(class_ref[...]).astype(F32), (rows, EDGE)), C_SHIFT, 1
    )
    lane = lax.broadcasted_iota(jnp.int32, own.shape, 1)
    edge = jnp.where(
        (lane < HW) | (lane >= EDGE - HW),
        own,
        jnp.where((lane >= A_SHIFT - HW) & (lane < A_SHIFT + HW), turned, class_edge),
    ).astype(BF16)
    parts = edge_parts(rows)
    base = mats + rows // parts
    near_ref[:mats, :] = t_ref[...].reshape(mats, depth)
    for part in range(depth // EDGE):
        start = part * (rows // parts) if part < parts else 0
        near_ref[mats:base, part * EDGE : (part + 1) * EDGE] = edge[start : start + base - mats, :]
    far_ref[:base, :] = near_ref[...]
    for which, cells in enumerate((fields, adjoints)):
        for part, span in enumerate(far_spans(base, rows, cells.shape[1], depth, which)):
            far_ref[span, :] = cells[:, part * depth : (part + 1) * depth]


def relay_kernel(far_ref, cross_ref, top_ref, near_ref, after_ref, out_ref):
    out_ref[0] = near_ref[...]
    out_ref[1] = top_ref[...]
    out_ref[2] = far_ref[: near_ref.shape[0], :]
    out_ref[3] = cross_ref[...]


def pick_halo(place, pieces, masks, mats, rows):
    tile = place[0]
    parts = edge_parts(rows)
    lane = lax.broadcasted_iota(jnp.int32, (rows, EDGE), 1)
    above = jnp.zeros((rows, EDGE), F32)
    below = jnp.zeros((rows, EDGE), F32)
    for (piece_ref, at), mask in zip(pieces, masks):
        bands = [
            piece_ref[at, mats : mats + rows // parts, part * EDGE : (part + 1) * EDGE]
            for part in range(parts)
        ]
        cells = jnp.concatenate(bands, axis=0).astype(F32)
        owner = tile ^ mask
        above = jnp.where(owner == tile + 1, cells, above)
        below = jnp.where(owner == tile - 1, cells, below)
    return above, below


def join_halo(halo, shift):
    above, below = halo
    lane = lax.broadcasted_iota(jnp.int32, above.shape, 1)
    back = (EDGE - shift) % EDGE
    if back:
        above, below = pltpu.roll(above, back, 1), pltpu.roll(below, back, 1)
    return jnp.where(lane < EDGE // 2, above, below)


def split_pieces(refs):
    near = [(ref, at) for ref in refs for at in (0, 1)]
    across = [(ref, at) for ref in refs for at in (2, 3)]
    return near, across


def fields_kernel(masks, count, place, both_ref, *refs):
    (near, across), far_ref, out_ref = split_pieces(refs[:-2]), refs[-2], refs[-1]
    unused, rows, width = both_ref.shape
    mats = count * rows
    far_own = far_cells(far_ref, mats + rows // edge_parts(rows), rows, width, 0)
    for start, source, pieces in ((place[1], both_ref[0], near), (1 - place[1], far_own, across)):
        start = pl.multiple_of(start * rows, rows)
        out_ref[pl.ds(start, rows), :width] = source
        halo = join_halo(pick_halo(place, pieces, masks, mats, rows), 0)
        out_ref[pl.ds(start, rows), width:] = halo.astype(BF16)


def prepare_kernel(rows, couple_ref, links_ref, place, mats_ref, own_ref, spread_ref, links, weights, sems):
    copies = []
    for chunk in range(SLOTS // CHUNK):
        span = pl.ds(chunk * CHUNK, CHUNK)
        copies.append(pltpu.make_async_copy(couple_ref.at[span], mats_ref.at[span], sems.at[chunk]))
    linked = pltpu.make_async_copy(links_ref, links, sems.at[len(copies)])
    linked.start()
    for copy in copies:
        copy.start()
    linked.wait()
    weights[...] = jnp.zeros_like(weights)
    weights[:SLOTS, :] = jnp.where(links[...] >= 0, 1.0, 0.0)
    filled = weights[...].astype(BF16)
    row = lax.broadcasted_iota(jnp.int32, (filled.shape[0], 2 * EDGE), 0)
    lane = lax.broadcasted_iota(jnp.int32, (filled.shape[0], 2 * EDGE), 1)
    for pair in range(SLOTS // 2):
        chosen = row == 2 * pair + (lane >= EDGE).astype(jnp.int32)
        unit = jnp.where(chosen, 1.0, 0.0).astype(BF16)
        spread = lax.dot_general(
            filled, unit, (((0,), (0,)), ((), ())), preferred_element_type=F32
        ).astype(BF16)
        spread_ref[2 * pair] = spread[:, :EDGE]
        spread_ref[2 * pair + 1] = spread[:, EDGE:]
    depth = mats_ref.shape[1]
    odd = place[1]
    lane = lax.broadcasted_iota(jnp.int32, (depth, EDGE), 1)
    first = jnp.where((lane // rows) % 2 == odd, 1.0, 0.0).astype(BF16)
    second = (1.0 - first).astype(BF16)
    shift = jnp.where(odd == 1, EDGE - rows, rows)
    for chunk, copy in enumerate(copies):
        copy.wait()
        for mat in range(chunk * CHUNK, (chunk + 1) * CHUNK):
            moved = pltpu.roll(mats_ref[mat, :, EDGE : 2 * EDGE], shift, 1)
            chosen = mats_ref[mat, :, :EDGE] * first + moved * second
            slot = SLOTS - 1 - mat
            side = (slot % 2) * EDGE
            own_ref[slot // 2, :, side : side + EDGE] = chosen


def stand_up(cells, upright):
    width = cells.shape[1] - EDGE
    turned = cells.astype(F32).T
    for half in range(upright.shape[0]):
        lanes = slice(half * EDGE, (half + 1) * EDGE)
        upright[half, LEAD : LEAD + width, :] = turned[:width, lanes]
        upright[half, LEAD + width :, :] = turned[width : width + LEAD, lanes]
        upright[half, :LEAD, :] = turned[width + EDGE - LEAD :, lanes]


def couple_slots(upright, spread_ref, mats_ref, slots, total=None):
    width = spread_ref.shape[1]
    for slot in slots:
        start = LEAD + OFFSETS[slot]
        weight = spread_ref[slot]
        selected = jnp.concatenate(
            [
                upright[half, start : start + width, :].astype(BF16) * weight
                for half in range(upright.shape[0])
            ],
            axis=1,
        )
        product = lax.dot_general(
            selected, mats_ref[slot], (((1,), (1,)), ((), ())), preferred_element_type=F32
        )
        total = product if total is None else total + product
    return total


def couple_own(upright, spread_ref, own_ref, products):
    width = spread_ref.shape[1]
    for pair in range(SLOTS // 2):
        both = jnp.dot(upright, own_ref[pair], preferred_element_type=F32)
        products[2 * pair] = both[:, :EDGE]
        products[2 * pair + 1] = both[:, EDGE:]
    bands = []
    for band in range(0, width, BAND):
        total = None
        for slot in range(SLOTS):
            start = LEAD + OFFSETS[slot] + band
            term = products[slot, start : start + BAND, :] * spread_ref[slot, band : band + BAND, :].astype(F32)
            total = term if total is None else total + term
        bands.append(total)
    return jnp.concatenate(bands, axis=0)


def adjoint_kernel(
    masks, count, sends, place, both_ref, far_ref, class_ref, spread_ref, own_ref, after_ref, *refs
):
    half = len(masks)
    near, across = split_pieces(refs[: -sends - 4])
    keep_ref, *send_refs = refs[-sends - 4 : -4]
    total_ref, expanded, stacked, products = refs[-4:]
    unused, rows, width = both_ref.shape
    mats = count * rows
    far_own = far_cells(far_ref, mats + rows // edge_parts(rows), rows, width, 1)
    halos = [pick_halo(place, pieces, masks, mats, rows) for pieces in (near, across)]
    padded = [
        jnp.concatenate([own, join_halo(halo, A_SHIFT).astype(BF16)], axis=1)
        for own, halo in ((both_ref[1], halos[0]), (far_own, halos[1]))
    ]
    class_halo = join_halo(tuple(cells[0:8, :] for cells in halos[0]), C_SHIFT)
    labels = jnp.concatenate([class_ref[...], class_halo[0:1, :].astype(jnp.int32)], axis=1)
    at = 0
    for piece in range(half):
        for which, pieces in ((0, near), (1, across)):
            ref, spot = pieces[piece]
            stacked[at : at + mats, :] = ref[spot, :mats, :]
            for local_class in range(count):
                hit = labels == (place[0] ^ masks[piece]) * count + local_class
                factor = jnp.where(hit, 1.0, 0.0).astype(BF16)
                expanded[at : at + rows, :] = padded[which] * factor
                at += rows
    scattered = lax.dot_general(
        stacked[...], expanded[...], (((0,), (0,)), ((), ())), preferred_element_type=F32
    )
    turned = scattered.astype(BF16).T
    upright = jnp.concatenate(
        [turned[width + EDGE - LEAD :], turned[:width], turned[width : width + LEAD]], axis=0
    )
    total_ref[...] = couple_own(upright, spread_ref, own_ref, products).T

    def block(rel):
        start = ((place[2] ^ rel) * 2 + place[1]) * rows
        moved = start - EDGE + jnp.where(place[1] == 1, -rows, rows)
        return pl.ds(pl.multiple_of(jnp.where(start < EDGE, start, moved), rows), rows)

    keep_ref[...] = total_ref[block(0), :]
    for rel, send_ref in enumerate(send_refs, 1):
        send_ref[...] = total_ref[block(rel), :].astype(BF16)


def forward_kernel(
    masks, count, rels, place, both_ref, class_ref, spread_ref, mats_ref, *refs
):
    pieces, refs = refs[: len(rels)], refs[len(rels) :]
    (near, across), (out_ref, padded, upright, stacked) = split_pieces(refs[:-4]), refs[-4:]
    unused, rows, width = both_ref.shape
    mats = count * rows
    block = 2 * rows
    for rel, piece_ref in zip(rels, pieces):
        start = pl.multiple_of((place[2] ^ rel) * block, block)
        padded[pl.ds(start, block), :] = piece_ref[...]
    stand_up(padded[...], upright)
    coupled = couple_slots(upright, spread_ref, mats_ref, range(SLOTS)).astype(BF16)
    for piece, (ref, spot) in enumerate(near):
        stacked[piece * mats : (piece + 1) * mats, :] = ref[spot, :mats, :]
    product = lax.dot_general(
        stacked[...], coupled, (((1,), (1,)), ((), ())), preferred_element_type=F32
    )
    applied = jnp.zeros((rows, width), F32)
    labels = class_ref[...]
    for piece in range(len(masks)):
        for local_class in range(count):
            hit = labels == (place[0] ^ masks[piece]) * count + local_class
            at = piece * mats + local_class * rows
            applied = jnp.where(hit, product[at : at + rows, :], applied)
    out_ref[...] = (both_ref[0].astype(F32) - applied).astype(BF16)


def finish_kernel(both_ref, keep_ref, after_ref, *refs):
    arrived, out_ref = refs[:-1], refs[-1]
    returned = keep_ref[...]
    for ref in arrived:
        returned = returned + ref[...].astype(F32)
    out_ref[...] = (both_ref[1].astype(F32) - returned).astype(BF16)


def local(fields, adjoints, couple, tmatrices, neighbours, classes):
    tiles, coefs = lax.axis_size("tiles"), lax.axis_size("coef")
    rows, width = fields.shape
    count, unused, depth = tmatrices.shape

    def swap(cells, tile_mask, coef_mask):
        pairs = [
            (i * coefs + j, (i ^ tile_mask) * coefs + (j ^ coef_mask))
            for i in range(tiles)
            for j in range(coefs)
        ]
        return lax.ppermute(cells, ("tiles", "coef"), pairs)

    labels = classes.reshape(1, width)
    mats = count * rows
    near_rows = mats + rows // edge_parts(rows)
    total_rows = couple.shape[1]
    place, near_own, far_own, both, labels = pl.pallas_call(
        pack_kernel,
        out_shape=(
            jax.ShapeDtypeStruct((3,), jnp.int32),
            jax.ShapeDtypeStruct((near_rows, depth), BF16),
            jax.ShapeDtypeStruct((near_rows + 2 * rows * (width // depth), depth), BF16),
            jax.ShapeDtypeStruct((2, rows, width), BF16),
            jax.ShapeDtypeStruct(labels.shape, jnp.int32),
        ),
        in_specs=[HBM] * 4,
        out_specs=(SMEM,) + (VMEM,) * 4,
        scratch_shapes=[pltpu.VMEM(tmatrices.shape, BF16), pltpu.SemaphoreType.DMA((4,))],
        compiler_params=PARAMS,
    )(*[in_hbm(cells) for cells in (tmatrices, fields, adjoints, labels)])
    mats_held, mats_own, spread = pl.pallas_call(
        functools.partial(prepare_kernel, rows),
        out_shape=(
            jax.ShapeDtypeStruct(couple.shape, BF16),
            jax.ShapeDtypeStruct((SLOTS // 2, total_rows, 2 * EDGE), BF16),
            jax.ShapeDtypeStruct((SLOTS, width, EDGE), BF16),
        ),
        in_specs=[HBM, HBM, SMEM],
        out_specs=(VMEM,) * 3,
        scratch_shapes=[
            pltpu.VMEM((SLOTS, width), jnp.int32),
            pltpu.VMEM((SLOTS + -SLOTS % 16, width), F32),
            pltpu.SemaphoreType.DMA((SLOTS // CHUNK + 1,)),
        ],
        cost_estimate=pl.CostEstimate(flops=0, bytes_accessed=4 * couple.size, transcendentals=0),
        compiler_params=PARAMS,
    )(in_hbm(couple), in_hbm(neighbours.T), place)

    top = tiles // 2
    far = swap(far_own, 0, 1)
    first = pl.pallas_call(
        relay_kernel,
        out_shape=jax.ShapeDtypeStruct((4, near_rows, depth), BF16),
        in_specs=[VMEM] * 5,
        out_specs=VMEM,
        compiler_params=PARAMS,
    )(far, swap(near_own, top, 1), swap(near_own, top, 0), near_own, mats_held)
    held, lows = [first], [0]
    bit = top // 2
    while bit >= 1:
        held += [swap(block, bit, 0) for block in held]
        lows += [low ^ bit for low in lows]
        bit //= 2
    masks = [low ^ high for low in lows for high in (0, top)]

    padded_fields = pl.pallas_call(
        functools.partial(fields_kernel, masks, count),
        out_shape=jax.ShapeDtypeStruct((2 * rows, width + EDGE), BF16),
        in_specs=[SMEM] + [VMEM] * (2 + len(held)),
        out_specs=VMEM,
        compiler_params=PARAMS,
    )(place, both, *held, far)

    groups = coefs // 2
    gathered = {0: padded_fields}
    for rel in range(1, groups):
        gathered[rel] = swap(padded_fields, 0, 2 * rel)
    rels = sorted(gathered, reverse=False)


    def work(slots):
        size = slots * total_rows * total_rows
        return pl.CostEstimate(flops=2 * size * width, bytes_accessed=2 * size, transcendentals=0)

    keep, *sent = pl.pallas_call(
        functools.partial(adjoint_kernel, masks, count, groups),
        out_shape=(jax.ShapeDtypeStruct((rows, width), F32),)
        + (jax.ShapeDtypeStruct((rows, width), BF16),) * (groups - 1),
        in_specs=[SMEM] + [VMEM] * 5 + [ANY] + [VMEM] * len(held),
        out_specs=(VMEM,) * groups,
        scratch_shapes=[
            pltpu.VMEM((EDGE, width), F32),
            pltpu.VMEM((2 * len(masks) * mats, width + EDGE), BF16),
            pltpu.VMEM((2 * len(masks) * mats, depth), BF16),
            pltpu.VMEM((SLOTS, width + 2 * LEAD, EDGE), F32),
        ],
        cost_estimate=work(SLOTS + 8),
        compiler_params=PARAMS,
    )(place, both, far, labels, spread, mats_own, padded_fields, *held)
    arrived = [swap(block, 0, 2 * rel) for rel, block in enumerate(sent, 1)]

    forward_out = pl.pallas_call(
        functools.partial(forward_kernel, masks, count, rels),
        out_shape=jax.ShapeDtypeStruct((rows, width), BF16),
        in_specs=[SMEM] + [VMEM] * (4 + len(rels) + len(held)),
        out_specs=VMEM,
        scratch_shapes=[
            pltpu.VMEM((total_rows, width + EDGE), BF16),
            pltpu.VMEM((total_rows // EDGE, width + 2 * LEAD, EDGE), F32),
            pltpu.VMEM((len(masks) * mats, depth), BF16),
        ],
        cost_estimate=work(SLOTS + 8),
        compiler_params=PARAMS,
    )(place, both, labels, spread, mats_held, *[gathered[rel] for rel in rels], *held)
    adjoint_out = pl.pallas_call(
        finish_kernel,
        out_shape=jax.ShapeDtypeStruct((rows, width), BF16),
        in_specs=[VMEM] * 2 + [HBM] + [VMEM] * len(arrived),
        out_specs=VMEM,
        compiler_params=PARAMS,
    )(both, keep, in_hbm(forward_out), *arrived[::-1])
    return (forward_out, adjoint_out)


def solution(mesh):
    placed = (
        P("coef", "tiles"),
        P("coef", "tiles"),
        P(),
        P("tiles", "coef", None),
        P("tiles", None),
        P("tiles"),
    )
    return jax.shard_map(
        local,
        mesh=mesh,
        in_specs=placed,
        out_specs=(P("coef", "tiles"), P("coef", "tiles")),
        check_vma=False,
    )
```

```python
import functools

import jax
import jax.numpy as jnp
from jax import lax
from jax.experimental import pallas as pl
from jax.experimental.pallas import tpu as pltpu
from jax.sharding import PartitionSpec as P

SLOTS = 30
HW = 15
EDGE = 128
CHUNK = 5
LEAD = 16
BAND = 128
A_SHIFT = 32
C_SHIFT = 64
OFFSETS = [slot - HW + (1 if slot >= HW else 0) for slot in range(SLOTS)]
BF16 = jnp.bfloat16
F32 = jnp.float32
VMEM = pl.BlockSpec(memory_space=pltpu.VMEM)
SMEM = pl.BlockSpec(memory_space=pltpu.SMEM)
ANY = pl.BlockSpec(memory_space=pl.ANY)
HBM = pl.BlockSpec(memory_space=pltpu.HBM)
PARAMS = pltpu.CompilerParams(vmem_limit_bytes=24 * 1024 * 1024)


def in_hbm(cells):
    return pltpu.with_memory_space_constraint(cells, pltpu.HBM)


def edges_of(cells):
    width = cells.shape[1]
    head, tail = cells[:, :EDGE], cells[:, width - EDGE :]
    lane = lax.broadcasted_iota(jnp.int32, head.shape, 1)
    return jnp.where(lane < EDGE // 2, head, tail)


def edge_parts(rows):
    return 2 if rows % 32 == 0 else 1


def pack_kernel(
    t_any, f_any, a_any, class_any, place, near_ref, both_ref, class_ref, t_ref, sems
):
    coef = lax.axis_index("coef")
    place[0] = lax.axis_index("tiles")
    place[1] = coef & 1
    place[2] = coef >> 1
    copies = [
        pltpu.make_async_copy(source, target, sems.at[at])
        for at, (source, target) in enumerate(
            (
                (t_any, t_ref),
                (f_any, both_ref.at[0]),
                (a_any, both_ref.at[1]),
                (class_any, class_ref),
            )
        )
    ]
    for copy in copies:
        copy.start()
    for copy in copies:
        copy.wait()
    count, rows, depth = t_ref.shape
    mats = count * rows
    fields, adjoints = both_ref[0], both_ref[1]
    own = edges_of(fields).astype(F32)
    turned = pltpu.roll(edges_of(adjoints).astype(F32), A_SHIFT, 1)
    class_edge = pltpu.roll(
        jnp.broadcast_to(edges_of(class_ref[...]).astype(F32), (rows, EDGE)), C_SHIFT, 1
    )
    lane = lax.broadcasted_iota(jnp.int32, own.shape, 1)
    edge = jnp.where(
        (lane < HW) | (lane >= EDGE - HW),
        own,
        jnp.where((lane >= A_SHIFT - HW) & (lane < A_SHIFT + HW), turned, class_edge),
    ).astype(BF16)
    parts = edge_parts(rows)
    base = mats + rows // parts
    near_ref[:mats, :] = t_ref[...].reshape(mats, depth)
    for part in range(depth // EDGE):
        start = part * (rows // parts) if part < parts else 0
        near_ref[mats:base, part * EDGE : (part + 1) * EDGE] = edge[start : start + base - mats, :]


def relay_kernel(cross_ref, far_ref, top_ref, both_ref, beside_ref, near_ref, after_ref, out_ref):
    out_ref[0] = near_ref[...]
    out_ref[1] = top_ref[...]
    out_ref[2] = far_ref[...]
    out_ref[3] = cross_ref[...]


def pick_halo(place, pieces, mats, rows):
    tile = place[0]
    parts = edge_parts(rows)
    lane = lax.broadcasted_iota(jnp.int32, (rows, EDGE), 1)
    above = jnp.zeros((rows, EDGE), F32)
    below = jnp.zeros((rows, EDGE), F32)
    for piece_ref, at, mask in pieces:
        bands = [
            piece_ref[at, mats : mats + rows // parts, part * EDGE : (part + 1) * EDGE]
            for part in range(parts)
        ]
        cells = jnp.concatenate(bands, axis=0).astype(F32)
        owner = tile ^ mask
        above = jnp.where(owner == tile + 1, cells, above)
        below = jnp.where(owner == tile - 1, cells, below)
    return above, below


def join_halo(halo, shift):
    above, below = halo
    lane = lax.broadcasted_iota(jnp.int32, above.shape, 1)
    back = (EDGE - shift) % EDGE
    if back:
        above, below = pltpu.roll(above, back, 1), pltpu.roll(below, back, 1)
    return jnp.where(lane < EDGE // 2, above, below)


def find_pieces(spots, refs):
    return [[(refs[which], at, mask) for which, at, mask in group] for group in spots]


def fields_kernel(spots, count, place, both_ref, far_ref, *refs):
    (near, across), (out_ref, halos) = find_pieces(spots, refs[:-2]), refs[-2:]
    unused, rows, width = both_ref.shape
    mats = count * rows
    for start, source, pieces in ((place[1], both_ref[0], near), (1 - place[1], far_ref[0], across)):
        start = pl.multiple_of(start * rows, rows)
        for part in range(width // EDGE):
            lanes = slice(part * EDGE, (part + 1) * EDGE)
            out_ref[pl.ds(part * 2 * rows + start, rows), :] = source[:, lanes]
        halos[pl.ds(start, rows), :] = join_halo(pick_halo(place, pieces, mats, rows), 0)
    lane = lax.broadcasted_iota(jnp.int32, (LEAD, EDGE), 1)
    packed = jnp.zeros((LEAD, EDGE), F32)
    for group in range(2 * rows // LEAD):
        halo = halos[group * LEAD : (group + 1) * LEAD, :]
        narrow = jnp.where(lane < LEAD, halo, pltpu.roll(halo, 2 * LEAD, 1))
        first = 2 * LEAD * group
        moved = pltpu.roll(narrow, first, 1) if group else narrow
        packed = jnp.where((lane >= first) & (lane < first + 2 * LEAD), moved, packed)
    out_ref[2 * rows * (width // EDGE) :, :] = packed.astype(BF16)


def unpack_fields(piece_ref, padded, start, block):
    width = padded.shape[1] - EDGE
    for part in range(width // EDGE):
        lanes = slice(part * EDGE, (part + 1) * EDGE)
        padded[pl.ds(start, block), lanes] = piece_ref[part * block : (part + 1) * block, :]
    packed = piece_ref[block * (width // EDGE) :, :].astype(F32)
    lane = lax.broadcasted_iota(jnp.int32, (LEAD, EDGE), 1)
    for group in range(block // LEAD):
        narrow = pltpu.roll(packed, EDGE - 2 * LEAD * group, 1) if group else packed
        halo = jnp.where(lane < EDGE // 2, narrow, pltpu.roll(narrow, EDGE - 2 * LEAD, 1))
        padded[pl.ds(start + group * LEAD, LEAD), width:] = halo.astype(BF16)


def prepare_kernel(rows, couple_ref, links_ref, place, mats_ref, own_ref, spread_ref, links, weights, sems):
    copies = []
    for chunk in range(SLOTS // CHUNK):
        span = pl.ds(chunk * CHUNK, CHUNK)
        copies.append(pltpu.make_async_copy(couple_ref.at[span], mats_ref.at[span], sems.at[chunk]))
    linked = pltpu.make_async_copy(links_ref, links, sems.at[len(copies)])
    linked.start()
    for copy in copies:
        copy.start()
    linked.wait()
    weights[...] = jnp.zeros_like(weights)
    weights[:SLOTS, :] = jnp.where(links[...] >= 0, 1.0, 0.0)
    filled = weights[...].astype(BF16)
    row = lax.broadcasted_iota(jnp.int32, (filled.shape[0], 2 * EDGE), 0)
    lane = lax.broadcasted_iota(jnp.int32, (filled.shape[0], 2 * EDGE), 1)
    for pair in range(SLOTS // 2):
        chosen = row == 2 * pair + (lane >= EDGE).astype(jnp.int32)
        unit = jnp.where(chosen, 1.0, 0.0).astype(BF16)
        spread = lax.dot_general(
            filled, unit, (((0,), (0,)), ((), ())), preferred_element_type=F32
        ).astype(BF16)
        spread_ref[2 * pair] = spread[:, :EDGE]
        spread_ref[2 * pair + 1] = spread[:, EDGE:]
    depth = mats_ref.shape[1]
    odd = place[1]
    lane = lax.broadcasted_iota(jnp.int32, (depth, EDGE), 1)
    first = jnp.where((lane // rows) % 2 == odd, 1.0, 0.0).astype(BF16)
    second = (1.0 - first).astype(BF16)
    shift = jnp.where(odd == 1, EDGE - rows, rows)
    for chunk, copy in enumerate(copies):
        copy.wait()
        for mat in range(chunk * CHUNK, (chunk + 1) * CHUNK):
            moved = pltpu.roll(mats_ref[mat, :, EDGE : 2 * EDGE], shift, 1)
            chosen = mats_ref[mat, :, :EDGE] * first + moved * second
            slot = SLOTS - 1 - mat
            side = (slot % 2) * EDGE
            own_ref[slot // 2, :, side : side + EDGE] = chosen


def stand_up(cells, upright):
    width = cells.shape[1] - EDGE
    turned = cells.astype(F32).T
    for half in range(upright.shape[0]):
        lanes = slice(half * EDGE, (half + 1) * EDGE)
        upright[half, LEAD : LEAD + width, :] = turned[:width, lanes]
        upright[half, LEAD + width :, :] = turned[width : width + LEAD, lanes]
        upright[half, :LEAD, :] = turned[width + EDGE - LEAD :, lanes]


def couple_slots(upright, spread_ref, mats_ref, slots, total=None):
    width = spread_ref.shape[1]
    for slot in slots:
        start = LEAD + OFFSETS[slot]
        weight = spread_ref[slot]
        selected = jnp.concatenate(
            [
                upright[half, start : start + width, :].astype(BF16) * weight
                for half in range(upright.shape[0])
            ],
            axis=1,
        )
        product = lax.dot_general(
            selected, mats_ref[slot], (((1,), (1,)), ((), ())), preferred_element_type=F32
        )
        total = product if total is None else total + product
    return total


def couple_own(upright, spread_ref, own_ref, products):
    width = spread_ref.shape[1]
    for pair in range(SLOTS // 2):
        both = jnp.dot(upright, own_ref[pair], preferred_element_type=F32)
        products[2 * pair] = both[:, :EDGE]
        products[2 * pair + 1] = both[:, EDGE:]
    bands = []
    for band in range(0, width, BAND):
        total = None
        for slot in range(SLOTS):
            start = LEAD + OFFSETS[slot] + band
            term = products[slot, start : start + BAND, :] * spread_ref[slot, band : band + BAND, :].astype(F32)
            total = term if total is None else total + term
        bands.append(total)
    return jnp.concatenate(bands, axis=0)


def adjoint_kernel(
    spots, count, sends, place, both_ref, far_ref, class_ref, spread_ref, own_ref, after_ref, *refs
):
    near, across = find_pieces(spots, refs[: -sends - 4])
    keep_ref, *send_refs = refs[-sends - 4 : -4]
    total_ref, expanded, stacked, products = refs[-4:]
    unused, rows, width = both_ref.shape
    mats = count * rows
    halos = [pick_halo(place, pieces, mats, rows) for pieces in (near, across)]
    padded = [
        jnp.concatenate([own, join_halo(halo, A_SHIFT).astype(BF16)], axis=1)
        for own, halo in ((both_ref[1], halos[0]), (far_ref[1], halos[1]))
    ]
    class_halo = join_halo(tuple(cells[0:8, :] for cells in halos[0]), C_SHIFT)
    labels = jnp.concatenate([class_ref[...], class_halo[0:1, :].astype(jnp.int32)], axis=1)
    at = 0
    for own, pieces in zip(padded, (near, across)):
        for ref, spot, mask in pieces:
            stacked[at : at + mats, :] = ref[spot, :mats, :]
            for local_class in range(count):
                hit = labels == (place[0] ^ mask) * count + local_class
                factor = jnp.where(hit, 1.0, 0.0).astype(BF16)
                expanded[at : at + rows, :] = own * factor
                at += rows
    scattered = lax.dot_general(
        stacked[...], expanded[...], (((0,), (0,)), ((), ())), preferred_element_type=F32
    )
    turned = scattered.astype(BF16).T
    upright = jnp.concatenate(
        [turned[width + EDGE - LEAD :], turned[:width], turned[width : width + LEAD]], axis=0
    )
    total_ref[...] = couple_own(upright, spread_ref, own_ref, products).T

    def block(rel):
        start = (((place[2] + rel) & (sends - 1)) * 2 + place[1]) * rows
        moved = start - EDGE + jnp.where(place[1] == 1, -rows, rows)
        return pl.ds(pl.multiple_of(jnp.where(start < EDGE, start, moved), rows), rows)

    keep_ref[...] = total_ref[block(0), :]
    for rel, send_ref in enumerate(send_refs, 1):
        send_ref[...] = total_ref[block(rel), :].astype(BF16)


def forward_kernel(
    spots, count, rels, place, both_ref, class_ref, spread_ref, mats_ref, *refs
):
    pieces, refs = refs[: len(rels)], refs[len(rels) :]
    (near, across), (out_ref, padded, upright, stacked) = find_pieces(spots, refs[:-4]), refs[-4:]
    unused, rows, width = both_ref.shape
    mats = count * rows
    block = 2 * rows
    for rel, piece_ref in zip(rels, pieces):
        start = pl.multiple_of(((place[2] - rel) & (len(rels) - 1)) * block, block)
        unpack_fields(piece_ref, padded, start, block)
    stand_up(padded[...], upright)
    coupled = couple_slots(upright, spread_ref, mats_ref, range(SLOTS)).astype(BF16)
    for piece, (ref, spot, mask) in enumerate(near):
        stacked[piece * mats : (piece + 1) * mats, :] = ref[spot, :mats, :]
    product = lax.dot_general(
        stacked[...], coupled, (((1,), (1,)), ((), ())), preferred_element_type=F32
    )
    applied = jnp.zeros((rows, width), F32)
    labels = class_ref[...]
    for piece, (ref, spot, mask) in enumerate(near):
        for local_class in range(count):
            hit = labels == (place[0] ^ mask) * count + local_class
            at = piece * mats + local_class * rows
            applied = jnp.where(hit, product[at : at + rows, :], applied)
    out_ref[...] = (both_ref[0].astype(F32) - applied).astype(BF16)


def finish_kernel(both_ref, keep_ref, after_ref, *refs):
    arrived, out_ref = refs[:-1], refs[-1]
    returned = keep_ref[...]
    for ref in arrived:
        returned = returned + ref[...].astype(F32)
    out_ref[...] = (both_ref[1].astype(F32) - returned).astype(BF16)


def local(fields, adjoints, couple, tmatrices, neighbours, classes):
    tiles, coefs = lax.axis_size("tiles"), lax.axis_size("coef")
    rows, width = fields.shape
    count, unused, depth = tmatrices.shape

    def swap(cells, tile_mask, coef_mask):
        pairs = [
            (i * coefs + j, (i ^ tile_mask) * coefs + (j ^ coef_mask))
            for i in range(tiles)
            for j in range(coefs)
        ]
        return lax.ppermute(cells, ("tiles", "coef"), pairs)

    def shift(cells, rel):
        pairs = [
            (i * coefs + j, i * coefs + (j + 2 * rel) % coefs)
            for i in range(tiles)
            for j in range(coefs)
        ]
        return lax.ppermute(cells, ("tiles", "coef"), pairs)

    labels = classes.reshape(1, width)
    mats = count * rows
    near_rows = mats + rows // edge_parts(rows)
    total_rows = couple.shape[1]
    place, near_own, both, labels = pl.pallas_call(
        pack_kernel,
        out_shape=(
            jax.ShapeDtypeStruct((3,), jnp.int32),
            jax.ShapeDtypeStruct((near_rows, depth), BF16),
            jax.ShapeDtypeStruct((2, rows, width), BF16),
            jax.ShapeDtypeStruct(labels.shape, jnp.int32),
        ),
        in_specs=[HBM] * 4,
        out_specs=(SMEM,) + (VMEM,) * 3,
        scratch_shapes=[pltpu.VMEM(tmatrices.shape, BF16), pltpu.SemaphoreType.DMA((4,))],
        compiler_params=PARAMS,
    )(*[in_hbm(cells) for cells in (tmatrices, fields, adjoints, labels)])
    mats_held, mats_own, spread = pl.pallas_call(
        functools.partial(prepare_kernel, rows),
        out_shape=(
            jax.ShapeDtypeStruct(couple.shape, BF16),
            jax.ShapeDtypeStruct((SLOTS // 2, total_rows, 2 * EDGE), BF16),
            jax.ShapeDtypeStruct((SLOTS, width, EDGE), BF16),
        ),
        in_specs=[HBM, HBM, SMEM],
        out_specs=(VMEM,) * 3,
        scratch_shapes=[
            pltpu.VMEM((SLOTS, width), jnp.int32),
            pltpu.VMEM((SLOTS + -SLOTS % 16, width), F32),
            pltpu.SemaphoreType.DMA((SLOTS // CHUNK + 1,)),
        ],
        cost_estimate=pl.CostEstimate(flops=0, bytes_accessed=4 * couple.size, transcendentals=0),
        compiler_params=PARAMS,
    )(in_hbm(couple), in_hbm(neighbours.T), place)

    top = tiles // 2
    both_far = swap(both, 0, 1)
    beside = swap(near_own, 1, 0)
    first = pl.pallas_call(
        relay_kernel,
        out_shape=jax.ShapeDtypeStruct((4, near_rows, depth), BF16),
        in_specs=[VMEM] * 7,
        out_specs=VMEM,
        compiler_params=PARAMS,
    )(
        swap(near_own, top ^ 1, 1),
        swap(near_own, 1, 1),
        swap(near_own, top ^ 1, 0),
        both_far,
        beside,
        near_own,
        mats_held,
    )
    held, lows = [first], [0]
    bit = top // 2
    while bit >= 1:
        held += [swap(block, bit, 0) for block in held]
        lows += [low ^ bit for low in lows]
        bit //= 2
    spots = (
        [(at, slot, low ^ (0, top ^ 1)[slot]) for at, low in enumerate(lows) for slot in (0, 1)],
        [(at, slot, low ^ (1, top ^ 1)[slot - 2]) for at, low in enumerate(lows) for slot in (2, 3)],
    )
    if tiles == 4:
        sources = [first, beside[None]]
        edge_spots = ([(0, 1, 3), (1, 0, 1)], [(0, 2, 1), (0, 3, 3)])
    else:
        sources, edge_spots = held, spots

    padded_fields = pl.pallas_call(
        functools.partial(fields_kernel, edge_spots, count),
        out_shape=jax.ShapeDtypeStruct((2 * rows * (width // EDGE) + LEAD, EDGE), BF16),
        in_specs=[SMEM] + [VMEM] * (2 + len(sources)),
        out_specs=VMEM,
        scratch_shapes=[pltpu.VMEM((2 * rows, EDGE), F32)],
        compiler_params=PARAMS,
    )(place, both, both_far, *sources)

    groups = coefs // 2
    gathered = {0: padded_fields}
    for rel in range(1, groups):
        gathered[rel] = shift(padded_fields, rel)
    rels = [0, 1, 2, 3] if groups == 4 else sorted(gathered)


    def work(slots):
        size = slots * total_rows * total_rows
        return pl.CostEstimate(flops=2 * size * width, bytes_accessed=2 * size, transcendentals=0)

    keep, *sent = pl.pallas_call(
        functools.partial(adjoint_kernel, spots, count, groups),
        out_shape=(jax.ShapeDtypeStruct((rows, width), F32),)
        + (jax.ShapeDtypeStruct((rows, width), BF16),) * (groups - 1),
        in_specs=[SMEM] + [VMEM] * 5 + [ANY] + [VMEM] * len(held),
        out_specs=(VMEM,) * groups,
        scratch_shapes=[
            pltpu.VMEM((EDGE, width), F32),
            pltpu.VMEM((2 * tiles * mats, width + EDGE), BF16),
            pltpu.VMEM((2 * tiles * mats, depth), BF16),
            pltpu.VMEM((SLOTS, width + 2 * LEAD, EDGE), F32),
        ],
        cost_estimate=work(SLOTS + 8),
        compiler_params=PARAMS,
    )(place, both, both_far, labels, spread, mats_own, padded_fields, *held)
    arrived = [shift(block, rel) for rel, block in enumerate(sent, 1)]

    forward_out = pl.pallas_call(
        functools.partial(forward_kernel, spots, count, rels),
        out_shape=jax.ShapeDtypeStruct((rows, width), BF16),
        in_specs=[SMEM] + [VMEM] * (4 + len(rels) + len(held)),
        out_specs=VMEM,
        scratch_shapes=[
            pltpu.VMEM((total_rows, width + EDGE), BF16),
            pltpu.VMEM((total_rows // EDGE, width + 2 * LEAD, EDGE), F32),
            pltpu.VMEM((tiles * mats, depth), BF16),
        ],
        cost_estimate=work(SLOTS + 8),
        compiler_params=PARAMS,
    )(place, both, labels, spread, mats_held, *[gathered[rel] for rel in rels], *held)
    adjoint_out = pl.pallas_call(
        finish_kernel,
        out_shape=jax.ShapeDtypeStruct((rows, width), BF16),
        in_specs=[VMEM] * 2 + [HBM] + [VMEM] * len(arrived),
        out_specs=VMEM,
        compiler_params=PARAMS,
    )(both, keep, in_hbm(forward_out), *[arrived[k - 1] for k in ((2, 3, 1) if groups == 4 else range(1, groups))])
    return (forward_out, adjoint_out)


def solution(mesh):
    placed = (
        P("coef", "tiles"),
        P("coef", "tiles"),
        P(),
        P("tiles", "coef", None),
        P("tiles", None),
        P("tiles"),
    )
    return jax.shard_map(
        local,
        mesh=mesh,
        in_specs=placed,
        out_specs=(P("coef", "tiles"), P("coef", "tiles")),
        check_vma=False,
    )
```

```python
import functools

import jax
import jax.numpy as jnp
from jax import lax
from jax.experimental import pallas as pl
from jax.experimental.pallas import tpu as pltpu
from jax.sharding import PartitionSpec as P

SLOTS = 30
HW = 15
EDGE = 128
CHUNK = 5
LEAD = 16
BAND = 128
A_SHIFT = 32
C_SHIFT = 64
OFFSETS = [slot - HW + (1 if slot >= HW else 0) for slot in range(SLOTS)]
BF16 = jnp.bfloat16
F32 = jnp.float32
VMEM = pl.BlockSpec(memory_space=pltpu.VMEM)
ANY = pl.BlockSpec(memory_space=pl.ANY)
HBM = pl.BlockSpec(memory_space=pltpu.HBM)
PARAMS = pltpu.CompilerParams(vmem_limit_bytes=24 * 1024 * 1024)


def in_hbm(cells):
    return pltpu.with_memory_space_constraint(cells, pltpu.HBM)


def find_place():
    coef = lax.axis_index("coef")
    return lax.axis_index("tiles"), coef & 1, coef >> 1


def edges_of(cells):
    width = cells.shape[1]
    head, tail = cells[:, :EDGE], cells[:, width - EDGE :]
    lane = lax.broadcasted_iota(jnp.int32, head.shape, 1)
    return jnp.where(lane < EDGE // 2, head, tail)


def edge_parts(rows):
    return 2 if rows % 32 == 0 else 1


def pack_kernel(
    t_any, f_any, a_any, class_any, near_ref, both_ref, class_ref, t_ref, sems
):
    copies = [
        pltpu.make_async_copy(source, target, sems.at[at])
        for at, (source, target) in enumerate(
            (
                (t_any, t_ref),
                (f_any, both_ref.at[0]),
                (a_any, both_ref.at[1]),
                (class_any, class_ref),
            )
        )
    ]
    for copy in copies:
        copy.start()
    for copy in copies:
        copy.wait()
    count, rows, depth = t_ref.shape
    mats = count * rows
    fields, adjoints = both_ref[0], both_ref[1]
    own = edges_of(fields).astype(F32)
    turned = pltpu.roll(edges_of(adjoints).astype(F32), A_SHIFT, 1)
    class_edge = pltpu.roll(
        jnp.broadcast_to(edges_of(class_ref[...]).astype(F32), (rows, EDGE)), C_SHIFT, 1
    )
    lane = lax.broadcasted_iota(jnp.int32, own.shape, 1)
    edge = jnp.where(
        (lane < HW) | (lane >= EDGE - HW),
        own,
        jnp.where((lane >= A_SHIFT - HW) & (lane < A_SHIFT + HW), turned, class_edge),
    ).astype(BF16)
    parts = edge_parts(rows)
    base = mats + rows // parts
    near_ref[:mats, :] = t_ref[...].reshape(mats, depth)
    for part in range(depth // EDGE):
        start = part * (rows // parts) if part < parts else 0
        near_ref[mats:base, part * EDGE : (part + 1) * EDGE] = edge[start : start + base - mats, :]


def relay_kernel(cross_ref, far_ref, top_ref, both_ref, beside_ref, near_ref, after_ref, out_ref):
    out_ref[0] = near_ref[...]
    out_ref[1] = top_ref[...]
    out_ref[2] = far_ref[...]
    out_ref[3] = cross_ref[...]


def pick_halo(place, pieces, mats, rows):
    tile = place[0]
    parts = edge_parts(rows)
    lane = lax.broadcasted_iota(jnp.int32, (rows, EDGE), 1)
    above = jnp.zeros((rows, EDGE), F32)
    below = jnp.zeros((rows, EDGE), F32)
    for piece_ref, at, mask in pieces:
        bands = [
            piece_ref[at, mats : mats + rows // parts, part * EDGE : (part + 1) * EDGE]
            for part in range(parts)
        ]
        cells = jnp.concatenate(bands, axis=0).astype(F32)
        owner = tile ^ mask
        above = jnp.where(owner == tile + 1, cells, above)
        below = jnp.where(owner == tile - 1, cells, below)
    return above, below


def join_halo(halo, shift):
    above, below = halo
    lane = lax.broadcasted_iota(jnp.int32, above.shape, 1)
    back = (EDGE - shift) % EDGE
    if back:
        above, below = pltpu.roll(above, back, 1), pltpu.roll(below, back, 1)
    return jnp.where(lane < EDGE // 2, above, below)


def find_pieces(spots, refs):
    return [[(refs[which], at, mask) for which, at, mask in group] for group in spots]


def fields_kernel(spots, count, both_ref, far_ref, *refs):
    place = find_place()
    (near, across), (out_ref, halos) = find_pieces(spots, refs[:-2]), refs[-2:]
    unused, rows, width = both_ref.shape
    mats = count * rows
    for start, source, pieces in ((place[1], both_ref[0], near), (1 - place[1], far_ref[0], across)):
        start = pl.multiple_of(start * rows, rows)
        for part in range(width // EDGE):
            lanes = slice(part * EDGE, (part + 1) * EDGE)
            out_ref[pl.ds(part * 2 * rows + start, rows), :] = source[:, lanes]
        halos[pl.ds(start, rows), :] = join_halo(pick_halo(place, pieces, mats, rows), 0)
    lane = lax.broadcasted_iota(jnp.int32, (LEAD, EDGE), 1)
    packed = jnp.zeros((LEAD, EDGE), F32)
    for group in range(2 * rows // LEAD):
        halo = halos[group * LEAD : (group + 1) * LEAD, :]
        narrow = jnp.where(lane < LEAD, halo, pltpu.roll(halo, 2 * LEAD, 1))
        first = 2 * LEAD * group
        moved = pltpu.roll(narrow, first, 1) if group else narrow
        packed = jnp.where((lane >= first) & (lane < first + 2 * LEAD), moved, packed)
    out_ref[2 * rows * (width // EDGE) :, :] = packed.astype(BF16)


def unpack_fields(piece_ref, padded, start, block):
    width = padded.shape[1] - EDGE
    for part in range(width // EDGE):
        lanes = slice(part * EDGE, (part + 1) * EDGE)
        padded[pl.ds(start, block), lanes] = piece_ref[part * block : (part + 1) * block, :]
    packed = piece_ref[block * (width // EDGE) :, :].astype(F32)
    lane = lax.broadcasted_iota(jnp.int32, (LEAD, EDGE), 1)
    for group in range(block // LEAD):
        narrow = pltpu.roll(packed, EDGE - 2 * LEAD * group, 1) if group else packed
        halo = jnp.where(lane < EDGE // 2, narrow, pltpu.roll(narrow, EDGE - 2 * LEAD, 1))
        padded[pl.ds(start + group * LEAD, LEAD), width:] = halo.astype(BF16)


def prepare_kernel(rows, couple_ref, links_ref, after_ref, mats_ref, own_ref, spread_ref, links, weights, sems):
    copies = []
    for chunk in range(SLOTS // CHUNK):
        span = pl.ds(chunk * CHUNK, CHUNK)
        copies.append(pltpu.make_async_copy(couple_ref.at[span], mats_ref.at[span], sems.at[chunk]))
    linked = pltpu.make_async_copy(links_ref, links, sems.at[len(copies)])
    linked.start()
    for copy in copies:
        copy.start()
    linked.wait()
    weights[...] = jnp.zeros_like(weights)
    weights[:SLOTS, :] = jnp.where(links[...] >= 0, 1.0, 0.0)
    filled = weights[...].astype(BF16)
    row = lax.broadcasted_iota(jnp.int32, (filled.shape[0], 2 * EDGE), 0)
    lane = lax.broadcasted_iota(jnp.int32, (filled.shape[0], 2 * EDGE), 1)
    for pair in range(SLOTS // 2):
        chosen = row == 2 * pair + (lane >= EDGE).astype(jnp.int32)
        unit = jnp.where(chosen, 1.0, 0.0).astype(BF16)
        spread = lax.dot_general(
            filled, unit, (((0,), (0,)), ((), ())), preferred_element_type=F32
        ).astype(BF16)
        spread_ref[2 * pair] = spread[:, :EDGE]
        spread_ref[2 * pair + 1] = spread[:, EDGE:]
    depth = mats_ref.shape[1]
    odd = find_place()[1]
    lane = lax.broadcasted_iota(jnp.int32, (depth, EDGE), 1)
    first = jnp.where((lane // rows) % 2 == odd, 1.0, 0.0).astype(BF16)
    second = (1.0 - first).astype(BF16)
    shift = jnp.where(odd == 1, EDGE - rows, rows)
    for chunk, copy in enumerate(copies):
        copy.wait()
        for mat in range(chunk * CHUNK, (chunk + 1) * CHUNK):
            moved = pltpu.roll(mats_ref[mat, :, EDGE : 2 * EDGE], shift, 1)
            chosen = mats_ref[mat, :, :EDGE] * first + moved * second
            slot = SLOTS - 1 - mat
            side = (slot % 2) * EDGE
            own_ref[slot // 2, :, side : side + EDGE] = chosen


def stand_up(cells, upright):
    width = cells.shape[1] - EDGE
    turned = cells.astype(F32).T
    for half in range(upright.shape[0]):
        lanes = slice(half * EDGE, (half + 1) * EDGE)
        upright[half, LEAD : LEAD + width, :] = turned[:width, lanes]
        upright[half, LEAD + width :, :] = turned[width : width + LEAD, lanes]
        upright[half, :LEAD, :] = turned[width + EDGE - LEAD :, lanes]


def couple_slots(upright, spread_ref, mats_ref, slots, total=None):
    width = spread_ref.shape[1]
    for slot in slots:
        start = LEAD + OFFSETS[slot]
        weight = spread_ref[slot]
        selected = jnp.concatenate(
            [
                upright[half, start : start + width, :].astype(BF16) * weight
                for half in range(upright.shape[0])
            ],
            axis=1,
        )
        product = lax.dot_general(
            selected, mats_ref[slot], (((1,), (1,)), ((), ())), preferred_element_type=F32
        )
        total = product if total is None else total + product
    return total


def couple_own(upright, spread_ref, own_ref, products):
    width = spread_ref.shape[1]
    for pair in range(SLOTS // 2):
        both = jnp.dot(upright, own_ref[pair], preferred_element_type=F32)
        products[2 * pair] = both[:, :EDGE]
        products[2 * pair + 1] = both[:, EDGE:]
    bands = []
    for band in range(0, width, BAND):
        total = None
        for slot in range(SLOTS):
            start = LEAD + OFFSETS[slot] + band
            term = products[slot, start : start + BAND, :] * spread_ref[slot, band : band + BAND, :].astype(F32)
            total = term if total is None else total + term
        bands.append(total)
    return jnp.concatenate(bands, axis=0)


def adjoint_kernel(
    spots, count, sends, both_ref, far_ref, class_ref, spread_ref, own_ref, after_ref, *refs
):
    place = find_place()
    near, across = find_pieces(spots, refs[: -sends - 4])
    keep_ref, *send_refs = refs[-sends - 4 : -4]
    total_ref, expanded, stacked, products = refs[-4:]
    unused, rows, width = both_ref.shape
    mats = count * rows
    halos = [pick_halo(place, pieces, mats, rows) for pieces in (near, across)]
    padded = [
        jnp.concatenate([own, join_halo(halo, A_SHIFT).astype(BF16)], axis=1)
        for own, halo in ((both_ref[1], halos[0]), (far_ref[1], halos[1]))
    ]
    class_halo = join_halo(tuple(cells[0:8, :] for cells in halos[0]), C_SHIFT)
    labels = jnp.concatenate([class_ref[...], class_halo[0:1, :].astype(jnp.int32)], axis=1)
    at = 0
    for own, pieces in zip(padded, (near, across)):
        for ref, spot, mask in pieces:
            stacked[at : at + mats, :] = ref[spot, :mats, :]
            for local_class in range(count):
                hit = labels == (place[0] ^ mask) * count + local_class
                factor = jnp.where(hit, 1.0, 0.0).astype(BF16)
                expanded[at : at + rows, :] = own * factor
                at += rows
    scattered = lax.dot_general(
        stacked[...], expanded[...], (((0,), (0,)), ((), ())), preferred_element_type=F32
    )
    turned = scattered.astype(BF16).T
    upright = jnp.concatenate(
        [turned[width + EDGE - LEAD :], turned[:width], turned[width : width + LEAD]], axis=0
    )
    total_ref[...] = couple_own(upright, spread_ref, own_ref, products).T

    def block(rel):
        start = (((place[2] + rel) & (sends - 1)) * 2 + place[1]) * rows
        moved = start - EDGE + jnp.where(place[1] == 1, -rows, rows)
        return pl.ds(pl.multiple_of(jnp.where(start < EDGE, start, moved), rows), rows)

    keep_ref[...] = total_ref[block(0), :]
    for rel, send_ref in enumerate(send_refs, 1):
        send_ref[...] = total_ref[block(rel), :].astype(BF16)


def forward_kernel(
    spots, count, rels, both_ref, class_ref, spread_ref, mats_ref, *refs
):
    place = find_place()
    pieces, refs = refs[: len(rels)], refs[len(rels) :]
    (near, across), (out_ref, padded, upright, stacked) = find_pieces(spots, refs[:-4]), refs[-4:]
    unused, rows, width = both_ref.shape
    mats = count * rows
    block = 2 * rows
    for rel, piece_ref in zip(rels, pieces):
        start = pl.multiple_of(((place[2] - rel) & (len(rels) - 1)) * block, block)
        unpack_fields(piece_ref, padded, start, block)
    stand_up(padded[...], upright)
    coupled = couple_slots(upright, spread_ref, mats_ref, range(SLOTS)).astype(BF16)
    for piece, (ref, spot, mask) in enumerate(near):
        stacked[piece * mats : (piece + 1) * mats, :] = ref[spot, :mats, :]
    product = lax.dot_general(
        stacked[...], coupled, (((1,), (1,)), ((), ())), preferred_element_type=F32
    )
    applied = jnp.zeros((rows, width), F32)
    labels = class_ref[...]
    for piece, (ref, spot, mask) in enumerate(near):
        for local_class in range(count):
            hit = labels == (place[0] ^ mask) * count + local_class
            at = piece * mats + local_class * rows
            applied = jnp.where(hit, product[at : at + rows, :], applied)
    out_ref[...] = (both_ref[0].astype(F32) - applied).astype(BF16)


def finish_kernel(both_ref, keep_ref, after_ref, *refs):
    arrived, out_ref = refs[:-1], refs[-1]
    returned = keep_ref[...]
    for ref in arrived:
        returned = returned + ref[...].astype(F32)
    out_ref[...] = (both_ref[1].astype(F32) - returned).astype(BF16)


def local(fields, adjoints, couple, tmatrices, neighbours, classes):
    tiles, coefs = lax.axis_size("tiles"), lax.axis_size("coef")
    rows, width = fields.shape
    count, unused, depth = tmatrices.shape

    def swap(cells, tile_mask, coef_mask):
        pairs = [
            (i * coefs + j, (i ^ tile_mask) * coefs + (j ^ coef_mask))
            for i in range(tiles)
            for j in range(coefs)
        ]
        return lax.ppermute(cells, ("tiles", "coef"), pairs)

    def shift(cells, rel):
        pairs = [
            (i * coefs + j, i * coefs + (j + 2 * rel) % coefs)
            for i in range(tiles)
            for j in range(coefs)
        ]
        return lax.ppermute(cells, ("tiles", "coef"), pairs)

    labels = classes.reshape(1, width)
    mats = count * rows
    near_rows = mats + rows // edge_parts(rows)
    total_rows = couple.shape[1]
    near_own, both, labels = pl.pallas_call(
        pack_kernel,
        out_shape=(
            jax.ShapeDtypeStruct((near_rows, depth), BF16),
            jax.ShapeDtypeStruct((2, rows, width), BF16),
            jax.ShapeDtypeStruct(labels.shape, jnp.int32),
        ),
        in_specs=[HBM] * 4,
        out_specs=(VMEM,) * 3,
        scratch_shapes=[pltpu.VMEM(tmatrices.shape, BF16), pltpu.SemaphoreType.DMA((4,))],
        compiler_params=PARAMS,
    )(*[in_hbm(cells) for cells in (tmatrices, fields, adjoints, labels)])
    mats_held, mats_own, spread = pl.pallas_call(
        functools.partial(prepare_kernel, rows),
        out_shape=(
            jax.ShapeDtypeStruct(couple.shape, BF16),
            jax.ShapeDtypeStruct((SLOTS // 2, total_rows, 2 * EDGE), BF16),
            jax.ShapeDtypeStruct((SLOTS, width, EDGE), BF16),
        ),
        in_specs=[HBM, HBM, VMEM],
        out_specs=(VMEM,) * 3,
        scratch_shapes=[
            pltpu.VMEM((SLOTS, width), jnp.int32),
            pltpu.VMEM((SLOTS + -SLOTS % 16, width), F32),
            pltpu.SemaphoreType.DMA((SLOTS // CHUNK + 1,)),
        ],
        cost_estimate=pl.CostEstimate(flops=0, bytes_accessed=4 * couple.size, transcendentals=0),
        compiler_params=PARAMS,
    )(in_hbm(couple), in_hbm(neighbours.T), labels)

    top = tiles // 2
    both_far = swap(both, 0, 1)
    beside = swap(near_own, 1, 0)
    first = pl.pallas_call(
        relay_kernel,
        out_shape=jax.ShapeDtypeStruct((4, near_rows, depth), BF16),
        in_specs=[VMEM] * 7,
        out_specs=VMEM,
        compiler_params=PARAMS,
    )(
        swap(near_own, top ^ 1, 1),
        swap(near_own, 1, 1),
        swap(near_own, top ^ 1, 0),
        both_far,
        beside,
        near_own,
        mats_held,
    )
    held, lows = [first], [0]
    bit = top // 2
    while bit >= 1:
        held += [swap(block, bit, 0) for block in held]
        lows += [low ^ bit for low in lows]
        bit //= 2
    spots = (
        [(at, slot, low ^ (0, top ^ 1)[slot]) for at, low in enumerate(lows) for slot in (0, 1)],
        [(at, slot, low ^ (1, top ^ 1)[slot - 2]) for at, low in enumerate(lows) for slot in (2, 3)],
    )
    if tiles == 4:
        sources = [first, beside[None]]
        edge_spots = ([(0, 1, 3), (1, 0, 1)], [(0, 2, 1), (0, 3, 3)])
    else:
        sources, edge_spots = held, spots

    padded_fields = pl.pallas_call(
        functools.partial(fields_kernel, edge_spots, count),
        out_shape=jax.ShapeDtypeStruct((2 * rows * (width // EDGE) + LEAD, EDGE), BF16),
        in_specs=[VMEM] * (2 + len(sources)),
        out_specs=VMEM,
        scratch_shapes=[pltpu.VMEM((2 * rows, EDGE), F32)],
        compiler_params=PARAMS,
    )(both, both_far, *sources)

    groups = coefs // 2
    gathered = {0: padded_fields}
    for rel in range(1, groups):
        gathered[rel] = shift(padded_fields, rel)
    rels = [0, 1, 2, 3] if groups == 4 else sorted(gathered)


    def work(slots):
        size = slots * total_rows * total_rows
        return pl.CostEstimate(flops=2 * size * width, bytes_accessed=2 * size, transcendentals=0)

    keep, *sent = pl.pallas_call(
        functools.partial(adjoint_kernel, spots, count, groups),
        out_shape=(jax.ShapeDtypeStruct((rows, width), F32),)
        + (jax.ShapeDtypeStruct((rows, width), BF16),) * (groups - 1),
        in_specs=[VMEM] * 5 + [ANY] + [VMEM] * len(held),
        out_specs=(VMEM,) * groups,
        scratch_shapes=[
            pltpu.VMEM((EDGE, width), F32),
            pltpu.VMEM((2 * tiles * mats, width + EDGE), BF16),
            pltpu.VMEM((2 * tiles * mats, depth), BF16),
            pltpu.VMEM((SLOTS, width + 2 * LEAD, EDGE), F32),
        ],
        cost_estimate=work(SLOTS + 8),
        compiler_params=PARAMS,
    )(both, both_far, labels, spread, mats_own, padded_fields, *held)
    arrived = [shift(block, rel) for rel, block in enumerate(sent, 1)]

    forward_out = pl.pallas_call(
        functools.partial(forward_kernel, spots, count, rels),
        out_shape=jax.ShapeDtypeStruct((rows, width), BF16),
        in_specs=[VMEM] * (4 + len(rels) + len(held)),
        out_specs=VMEM,
        scratch_shapes=[
            pltpu.VMEM((total_rows, width + EDGE), BF16),
            pltpu.VMEM((total_rows // EDGE, width + 2 * LEAD, EDGE), F32),
            pltpu.VMEM((tiles * mats, depth), BF16),
        ],
        cost_estimate=work(SLOTS + 8),
        compiler_params=PARAMS,
    )(both, labels, spread, mats_held, *[gathered[rel] for rel in rels], *held)
    adjoint_out = pl.pallas_call(
        finish_kernel,
        out_shape=jax.ShapeDtypeStruct((rows, width), BF16),
        in_specs=[VMEM] * 2 + [HBM] + [VMEM] * len(arrived),
        out_specs=VMEM,
        compiler_params=PARAMS,
    )(both, keep, in_hbm(forward_out), *[arrived[k - 1] for k in ((2, 3, 1) if groups == 4 else range(1, groups))])
    return (forward_out, adjoint_out)


def solution(mesh):
    placed = (
        P("coef", "tiles"),
        P("coef", "tiles"),
        P(),
        P("tiles", "coef", None),
        P("tiles", None),
        P("tiles"),
    )
    return jax.shard_map(
        local,
        mesh=mesh,
        in_specs=placed,
        out_specs=(P("coef", "tiles"), P("coef", "tiles")),
        check_vma=False,
    )
```

```python
import functools

import jax
import jax.numpy as jnp
from jax import lax
from jax.experimental import pallas as pl
from jax.experimental.pallas import tpu as pltpu
from jax.sharding import PartitionSpec as P

SLOTS = 30
HW = 15
EDGE = 128
CHUNK = 5
LEAD = 16
BAND = 128
A_SHIFT = 32
C_SHIFT = 64
OFFSETS = [slot - HW + (1 if slot >= HW else 0) for slot in range(SLOTS)]
BF16 = jnp.bfloat16
F32 = jnp.float32
VMEM = pl.BlockSpec(memory_space=pltpu.VMEM)
ANY = pl.BlockSpec(memory_space=pl.ANY)
HBM = pl.BlockSpec(memory_space=pltpu.HBM)
PARAMS = pltpu.CompilerParams(vmem_limit_bytes=24 * 1024 * 1024)


def in_hbm(cells):
    return pltpu.with_memory_space_constraint(cells, pltpu.HBM)


def find_place():
    coef = lax.axis_index("coef")
    return lax.axis_index("tiles"), coef & 1, coef >> 1


def edges_of(cells):
    width = cells.shape[1]
    head, tail = cells[:, :EDGE], cells[:, width - EDGE :]
    lane = lax.broadcasted_iota(jnp.int32, head.shape, 1)
    return jnp.where(lane < EDGE // 2, head, tail)


def edge_parts(rows):
    return 2 if rows % 32 == 0 else 1


def pack_kernel(
    t_any, f_any, a_any, class_any, near_ref, both_ref, sent_ref, class_ref, t_ref, sems
):
    copies = [
        pltpu.make_async_copy(source, target, sems.at[at])
        for at, (source, target) in enumerate(
            (
                (t_any, t_ref),
                (f_any, both_ref.at[0]),
                (a_any, both_ref.at[1]),
                (class_any, class_ref),
            )
        )
    ]
    for copy in copies:
        copy.start()
    for copy in copies:
        copy.wait()
    count, rows, depth = t_ref.shape
    mats = count * rows
    fields, adjoints = both_ref[0], both_ref[1]
    own = edges_of(fields).astype(F32)
    turned = pltpu.roll(edges_of(adjoints).astype(F32), A_SHIFT, 1)
    class_edge = pltpu.roll(
        jnp.broadcast_to(edges_of(class_ref[...]).astype(F32), (rows, EDGE)), C_SHIFT, 1
    )
    lane = lax.broadcasted_iota(jnp.int32, own.shape, 1)
    edge = jnp.where(
        (lane < HW) | (lane >= EDGE - HW),
        own,
        jnp.where((lane >= A_SHIFT - HW) & (lane < A_SHIFT + HW), turned, class_edge),
    ).astype(BF16)
    parts = edge_parts(rows)
    base = mats + rows // parts
    near_ref[:mats, :] = t_ref[...].reshape(mats, depth)
    for part in range(depth // EDGE):
        start = part * (rows // parts) if part < parts else 0
        near_ref[mats:base, part * EDGE : (part + 1) * EDGE] = edge[start : start + base - mats, :]
    sent_ref[:rows, :] = fields
    sent_ref[rows : 2 * rows, :] = adjoints
    sent_ref[2 * rows :, :] = jnp.zeros_like(sent_ref[2 * rows :, :])


def relay_kernel(cross_ref, far_ref, top_ref, both_ref, beside_ref, near_ref, after_ref, out_ref):
    out_ref[0] = near_ref[...]
    out_ref[1] = top_ref[...]
    out_ref[2] = far_ref[...]
    out_ref[3] = cross_ref[...]


def pick_halo(place, pieces, mats, rows):
    tile = place[0]
    parts = edge_parts(rows)
    lane = lax.broadcasted_iota(jnp.int32, (rows, EDGE), 1)
    above = jnp.zeros((rows, EDGE), F32)
    below = jnp.zeros((rows, EDGE), F32)
    for piece_ref, at, mask in pieces:
        bands = [
            piece_ref[at, mats : mats + rows // parts, part * EDGE : (part + 1) * EDGE]
            for part in range(parts)
        ]
        cells = jnp.concatenate(bands, axis=0).astype(F32)
        owner = tile ^ mask
        above = jnp.where(owner == tile + 1, cells, above)
        below = jnp.where(owner == tile - 1, cells, below)
    return above, below


def join_halo(halo, shift):
    above, below = halo
    lane = lax.broadcasted_iota(jnp.int32, above.shape, 1)
    back = (EDGE - shift) % EDGE
    if back:
        above, below = pltpu.roll(above, back, 1), pltpu.roll(below, back, 1)
    return jnp.where(lane < EDGE // 2, above, below)


def find_pieces(spots, refs):
    return [[(refs[which], at, mask) for which, at, mask in group] for group in spots]


def fields_kernel(spots, count, both_ref, far_ref, *refs):
    place = find_place()
    (near, across), (out_ref, halos) = find_pieces(spots, refs[:-2]), refs[-2:]
    unused, rows, width = both_ref.shape
    mats = count * rows
    for start, source, pieces in ((place[1], both_ref[0], near), (1 - place[1], far_ref[:rows, :], across)):
        start = pl.multiple_of(start * rows, rows)
        for part in range(width // EDGE):
            lanes = slice(part * EDGE, (part + 1) * EDGE)
            out_ref[pl.ds(part * 2 * rows + start, rows), :] = source[:, lanes]
        halos[pl.ds(start, rows), :] = join_halo(pick_halo(place, pieces, mats, rows), 0)
    lane = lax.broadcasted_iota(jnp.int32, (LEAD, EDGE), 1)
    packed = jnp.zeros((LEAD, EDGE), F32)
    for group in range(2 * rows // LEAD):
        halo = halos[group * LEAD : (group + 1) * LEAD, :]
        narrow = jnp.where(lane < LEAD, halo, pltpu.roll(halo, 2 * LEAD, 1))
        first = 2 * LEAD * group
        moved = pltpu.roll(narrow, first, 1) if group else narrow
        packed = jnp.where((lane >= first) & (lane < first + 2 * LEAD), moved, packed)
    out_ref[2 * rows * (width // EDGE) :, :] = packed.astype(BF16)


def unpack_fields(piece_ref, padded, start, block):
    width = padded.shape[1] - EDGE
    for part in range(width // EDGE):
        lanes = slice(part * EDGE, (part + 1) * EDGE)
        padded[pl.ds(start, block), lanes] = piece_ref[part * block : (part + 1) * block, :]
    packed = piece_ref[block * (width // EDGE) :, :].astype(F32)
    lane = lax.broadcasted_iota(jnp.int32, (LEAD, EDGE), 1)
    for group in range(block // LEAD):
        narrow = pltpu.roll(packed, EDGE - 2 * LEAD * group, 1) if group else packed
        halo = jnp.where(lane < EDGE // 2, narrow, pltpu.roll(narrow, EDGE - 2 * LEAD, 1))
        padded[pl.ds(start + group * LEAD, LEAD), width:] = halo.astype(BF16)


def prepare_kernel(rows, couple_ref, links_ref, after_ref, mats_ref, own_ref, spread_ref, links, weights, sems):
    copies = []
    for chunk in range(SLOTS // CHUNK):
        span = pl.ds(chunk * CHUNK, CHUNK)
        copies.append(pltpu.make_async_copy(couple_ref.at[span], mats_ref.at[span], sems.at[chunk]))
    linked = pltpu.make_async_copy(links_ref, links, sems.at[len(copies)])
    linked.start()
    for copy in copies:
        copy.start()
    linked.wait()
    weights[...] = jnp.zeros_like(weights)
    weights[:SLOTS, :] = jnp.where(links[...] >= 0, 1.0, 0.0)
    filled = weights[...].astype(BF16)
    row = lax.broadcasted_iota(jnp.int32, (filled.shape[0], 2 * EDGE), 0)
    lane = lax.broadcasted_iota(jnp.int32, (filled.shape[0], 2 * EDGE), 1)
    for pair in range(SLOTS // 2):
        chosen = row == 2 * pair + (lane >= EDGE).astype(jnp.int32)
        unit = jnp.where(chosen, 1.0, 0.0).astype(BF16)
        spread = lax.dot_general(
            filled, unit, (((0,), (0,)), ((), ())), preferred_element_type=F32
        ).astype(BF16)
        spread_ref[2 * pair] = spread[:, :EDGE]
        spread_ref[2 * pair + 1] = spread[:, EDGE:]
    depth = mats_ref.shape[1]
    odd = find_place()[1]
    lane = lax.broadcasted_iota(jnp.int32, (depth, EDGE), 1)
    first = jnp.where((lane // rows) % 2 == odd, 1.0, 0.0).astype(BF16)
    second = (1.0 - first).astype(BF16)
    shift = jnp.where(odd == 1, EDGE - rows, rows)
    for chunk, copy in enumerate(copies):
        copy.wait()
        for mat in range(chunk * CHUNK, (chunk + 1) * CHUNK):
            moved = pltpu.roll(mats_ref[mat, :, EDGE : 2 * EDGE], shift, 1)
            chosen = mats_ref[mat, :, :EDGE] * first + moved * second
            slot = SLOTS - 1 - mat
            side = (slot % 2) * EDGE
            own_ref[slot // 2, :, side : side + EDGE] = chosen


def stand_up(cells, upright):
    width = cells.shape[1] - EDGE
    turned = cells.astype(F32).T
    for half in range(upright.shape[0]):
        lanes = slice(half * EDGE, (half + 1) * EDGE)
        upright[half, LEAD : LEAD + width, :] = turned[:width, lanes]
        upright[half, LEAD + width :, :] = turned[width : width + LEAD, lanes]
        upright[half, :LEAD, :] = turned[width + EDGE - LEAD :, lanes]


def couple_slots(upright, spread_ref, mats_ref, slots, total=None):
    width = spread_ref.shape[1]
    for slot in slots:
        start = LEAD + OFFSETS[slot]
        weight = spread_ref[slot]
        selected = jnp.concatenate(
            [
                upright[half, start : start + width, :].astype(BF16) * weight
                for half in range(upright.shape[0])
            ],
            axis=1,
        )
        product = lax.dot_general(
            selected, mats_ref[slot], (((1,), (1,)), ((), ())), preferred_element_type=F32
        )
        total = product if total is None else total + product
    return total


def couple_own(upright, spread_ref, own_ref, products):
    width = spread_ref.shape[1]
    for pair in range(SLOTS // 2):
        both = jnp.dot(upright, own_ref[pair], preferred_element_type=F32)
        products[2 * pair] = both[:, :EDGE]
        products[2 * pair + 1] = both[:, EDGE:]
    bands = []
    for band in range(0, width, BAND):
        total = None
        for slot in range(SLOTS):
            start = LEAD + OFFSETS[slot] + band
            term = products[slot, start : start + BAND, :] * spread_ref[slot, band : band + BAND, :].astype(F32)
            total = term if total is None else total + term
        bands.append(total)
    return jnp.concatenate(bands, axis=0)


def adjoint_kernel(
    spots, count, sends, both_ref, far_ref, class_ref, spread_ref, own_ref, after_ref, *refs
):
    place = find_place()
    near, across = find_pieces(spots, refs[: -sends - 4])
    keep_ref, *send_refs = refs[-sends - 4 : -4]
    total_ref, expanded, stacked, products = refs[-4:]
    unused, rows, width = both_ref.shape
    mats = count * rows
    halos = [pick_halo(place, pieces, mats, rows) for pieces in (near, across)]
    padded = [
        jnp.concatenate([own, join_halo(halo, A_SHIFT).astype(BF16)], axis=1)
        for own, halo in ((both_ref[1], halos[0]), (far_ref[rows : 2 * rows, :], halos[1]))
    ]
    class_halo = join_halo(tuple(cells[0:8, :] for cells in halos[0]), C_SHIFT)
    labels = jnp.concatenate([class_ref[...], class_halo[0:1, :].astype(jnp.int32)], axis=1)
    at = 0
    for own, pieces in zip(padded, (near, across)):
        for ref, spot, mask in pieces:
            stacked[at : at + mats, :] = ref[spot, :mats, :]
            for local_class in range(count):
                hit = labels == (place[0] ^ mask) * count + local_class
                factor = jnp.where(hit, 1.0, 0.0).astype(BF16)
                expanded[at : at + rows, :] = own * factor
                at += rows
    scattered = lax.dot_general(
        stacked[...], expanded[...], (((0,), (0,)), ((), ())), preferred_element_type=F32
    )
    turned = scattered.astype(BF16).T
    upright = jnp.concatenate(
        [turned[width + EDGE - LEAD :], turned[:width], turned[width : width + LEAD]], axis=0
    )
    total_ref[...] = couple_own(upright, spread_ref, own_ref, products).T

    def block(rel):
        start = ((place[2] ^ rel) * 2 + place[1]) * rows
        moved = start - EDGE + jnp.where(place[1] == 1, -rows, rows)
        return pl.ds(pl.multiple_of(jnp.where(start < EDGE, start, moved), rows), rows)

    keep_ref[...] = total_ref[block(0), :]
    for rel, send_ref in enumerate(send_refs, 1):
        send_ref[...] = total_ref[block(rel), :].astype(BF16)


def forward_kernel(
    spots, count, rels, both_ref, class_ref, spread_ref, mats_ref, *refs
):
    place = find_place()
    pieces, refs = refs[: len(rels)], refs[len(rels) :]
    (near, across), (out_ref, padded, upright, stacked) = find_pieces(spots, refs[:-4]), refs[-4:]
    unused, rows, width = both_ref.shape
    mats = count * rows
    block = 2 * rows
    for rel, piece_ref in zip(rels, pieces):
        start = pl.multiple_of((place[2] ^ rel) * block, block)
        unpack_fields(piece_ref, padded, start, block)
    stand_up(padded[...], upright)
    coupled = couple_slots(upright, spread_ref, mats_ref, range(SLOTS)).astype(BF16)
    for piece, (ref, spot, mask) in enumerate(near):
        stacked[piece * mats : (piece + 1) * mats, :] = ref[spot, :mats, :]
    product = lax.dot_general(
        stacked[...], coupled, (((1,), (1,)), ((), ())), preferred_element_type=F32
    )
    applied = jnp.zeros((rows, width), F32)
    labels = class_ref[...]
    for piece, (ref, spot, mask) in enumerate(near):
        for local_class in range(count):
            hit = labels == (place[0] ^ mask) * count + local_class
            at = piece * mats + local_class * rows
            applied = jnp.where(hit, product[at : at + rows, :], applied)
    out_ref[...] = (both_ref[0].astype(F32) - applied).astype(BF16)


def finish_kernel(both_ref, keep_ref, forward_ref, *refs):
    arrived, (out_ref, adjoint_ref) = refs[:-2], refs[-2:]
    out_ref[...] = forward_ref[...]
    returned = keep_ref[...]
    for ref in arrived:
        returned = returned + ref[...].astype(F32)
    adjoint_ref[...] = (both_ref[1].astype(F32) - returned).astype(BF16)


def local(fields, adjoints, couple, tmatrices, neighbours, classes):
    tiles, coefs = lax.axis_size("tiles"), lax.axis_size("coef")
    rows, width = fields.shape
    count, unused, depth = tmatrices.shape

    def swap(cells, tile_mask, coef_mask):
        pairs = [
            (i * coefs + j, (i ^ tile_mask) * coefs + (j ^ coef_mask))
            for i in range(tiles)
            for j in range(coefs)
        ]
        return lax.ppermute(cells, ("tiles", "coef"), pairs)

    labels = classes.reshape(1, width)
    mats = count * rows
    near_rows = mats + rows // edge_parts(rows)
    total_rows = couple.shape[1]
    near_own, both, sent_far, labels = pl.pallas_call(
        pack_kernel,
        out_shape=(
            jax.ShapeDtypeStruct((near_rows, depth), BF16),
            jax.ShapeDtypeStruct((2, rows, width), BF16),
            jax.ShapeDtypeStruct((2 * rows + LEAD, width), BF16),
            jax.ShapeDtypeStruct(labels.shape, jnp.int32),
        ),
        in_specs=[HBM] * 4,
        out_specs=(VMEM,) * 4,
        scratch_shapes=[pltpu.VMEM(tmatrices.shape, BF16), pltpu.SemaphoreType.DMA((4,))],
        compiler_params=PARAMS,
    )(*[in_hbm(cells) for cells in (tmatrices, fields, adjoints, labels)])
    mats_held, mats_own, spread = pl.pallas_call(
        functools.partial(prepare_kernel, rows),
        out_shape=(
            jax.ShapeDtypeStruct(couple.shape, BF16),
            jax.ShapeDtypeStruct((SLOTS // 2, total_rows, 2 * EDGE), BF16),
            jax.ShapeDtypeStruct((SLOTS, width, EDGE), BF16),
        ),
        in_specs=[HBM, HBM, VMEM],
        out_specs=(VMEM,) * 3,
        scratch_shapes=[
            pltpu.VMEM((SLOTS, width), jnp.int32),
            pltpu.VMEM((SLOTS + -SLOTS % 16, width), F32),
            pltpu.SemaphoreType.DMA((SLOTS // CHUNK + 1,)),
        ],
        cost_estimate=pl.CostEstimate(flops=0, bytes_accessed=4 * couple.size, transcendentals=0),
        compiler_params=PARAMS,
    )(in_hbm(couple), in_hbm(neighbours.T), labels)

    top = tiles // 2
    both_far = swap(sent_far, 0, 1)
    beside = swap(near_own, 1, 0)
    first = pl.pallas_call(
        relay_kernel,
        out_shape=jax.ShapeDtypeStruct((4, near_rows, depth), BF16),
        in_specs=[VMEM] * 7,
        out_specs=VMEM,
        compiler_params=PARAMS,
    )(
        swap(near_own, top ^ 1, 1),
        swap(near_own, 1, 1),
        swap(near_own, top ^ 1, 0),
        both_far,
        beside,
        near_own,
        mats_held,
    )
    held, lows = [first], [0]
    bit = top // 2
    while bit >= 1:
        held += [swap(block, bit, 0) for block in held]
        lows += [low ^ bit for low in lows]
        bit //= 2
    spots = (
        [(at, slot, low ^ (0, top ^ 1)[slot]) for at, low in enumerate(lows) for slot in (0, 1)],
        [(at, slot, low ^ (1, top ^ 1)[slot - 2]) for at, low in enumerate(lows) for slot in (2, 3)],
    )
    if tiles == 4:
        sources = [first, beside[None]]
        edge_spots = ([(0, 1, 3), (1, 0, 1)], [(0, 2, 1), (0, 3, 3)])
    else:
        sources, edge_spots = held, spots

    padded_fields = pl.pallas_call(
        functools.partial(fields_kernel, edge_spots, count),
        out_shape=jax.ShapeDtypeStruct((2 * rows * (width // EDGE) + LEAD, EDGE), BF16),
        in_specs=[VMEM] * (2 + len(sources)),
        out_specs=VMEM,
        scratch_shapes=[pltpu.VMEM((2 * rows, EDGE), F32)],
        compiler_params=PARAMS,
    )(both, both_far, *sources)

    groups = coefs // 2
    gathered = {0: padded_fields}
    for rel in range(1, groups):
        gathered[rel] = swap(padded_fields, 0, 2 * rel)
    rels = [0, 1, 3, 2] if groups == 4 else sorted(gathered)


    def work(slots):
        size = slots * total_rows * total_rows
        return pl.CostEstimate(flops=2 * size * width, bytes_accessed=2 * size, transcendentals=0)

    keep, *sent = pl.pallas_call(
        functools.partial(adjoint_kernel, spots, count, groups),
        out_shape=(jax.ShapeDtypeStruct((rows, width), F32),)
        + (jax.ShapeDtypeStruct((rows, width), BF16),) * (groups - 1),
        in_specs=[VMEM] * 5 + [ANY] + [VMEM] * len(held),
        out_specs=(VMEM,) * groups,
        scratch_shapes=[
            pltpu.VMEM((EDGE, width), F32),
            pltpu.VMEM((2 * tiles * mats, width + EDGE), BF16),
            pltpu.VMEM((2 * tiles * mats, depth), BF16),
            pltpu.VMEM((SLOTS, width + 2 * LEAD, EDGE), F32),
        ],
        cost_estimate=work(SLOTS + 8),
        compiler_params=PARAMS,
    )(both, both_far, labels, spread, mats_own, padded_fields, *held)
    arrived = [swap(block, 0, 2 * rel) for rel, block in enumerate(sent, 1)]

    forward = pl.pallas_call(
        functools.partial(forward_kernel, spots, count, rels),
        out_shape=jax.ShapeDtypeStruct((rows, width), BF16),
        in_specs=[VMEM] * (4 + len(rels) + len(held)),
        out_specs=VMEM,
        scratch_shapes=[
            pltpu.VMEM((total_rows, width + EDGE), BF16),
            pltpu.VMEM((total_rows // EDGE, width + 2 * LEAD, EDGE), F32),
            pltpu.VMEM((tiles * mats, depth), BF16),
        ],
        cost_estimate=work(SLOTS + 8),
        compiler_params=PARAMS,
    )(both, labels, spread, mats_held, *[gathered[rel] for rel in rels], *held)
    return pl.pallas_call(
        finish_kernel,
        out_shape=(jax.ShapeDtypeStruct((rows, width), BF16),) * 2,
        in_specs=[VMEM] * (3 + len(arrived)),
        out_specs=(VMEM, VMEM),
        compiler_params=PARAMS,
    )(both, keep, forward, *[arrived[k - 1] for k in ((3, 2, 1) if groups == 4 else range(1, groups))])


def solution(mesh):
    placed = (
        P("coef", "tiles"),
        P("coef", "tiles"),
        P(),
        P("tiles", "coef", None),
        P("tiles", None),
        P("tiles"),
    )
    return jax.shard_map(
        local,
        mesh=mesh,
        in_specs=placed,
        out_specs=(P("coef", "tiles"), P("coef", "tiles")),
        check_vma=False,
    )
```

```python
import functools

import jax
import jax.numpy as jnp
from jax import lax
from jax.experimental import pallas as pl
from jax.experimental.pallas import tpu as pltpu
from jax.sharding import PartitionSpec as P

SLOTS = 30
HW = 15
EDGE = 128
CHUNK = 5
LEAD = 16
BAND = 128
A_SHIFT = 32
C_SHIFT = 64
OFFSETS = [slot - HW + (1 if slot >= HW else 0) for slot in range(SLOTS)]
BF16 = jnp.bfloat16
F32 = jnp.float32
VMEM = pl.BlockSpec(memory_space=pltpu.VMEM)
ANY = pl.BlockSpec(memory_space=pl.ANY)
HBM = pl.BlockSpec(memory_space=pltpu.HBM)
PARAMS = pltpu.CompilerParams(vmem_limit_bytes=24 * 1024 * 1024)


def in_hbm(cells):
    return pltpu.with_memory_space_constraint(cells, pltpu.HBM)


def find_place():
    coef = lax.axis_index("coef")
    return lax.axis_index("tiles"), coef & 1, coef >> 1


def edges_of(cells):
    width = cells.shape[1]
    head, tail = cells[:, :EDGE], cells[:, width - EDGE :]
    lane = lax.broadcasted_iota(jnp.int32, head.shape, 1)
    return jnp.where(lane < EDGE // 2, head, tail)


def edge_parts(rows):
    return 2 if rows % 32 == 0 else 1


def pack_kernel(
    t_any, f_any, a_any, class_any, near_ref, both_ref, sent_ref, class_ref, t_ref, sems
):
    copies = [
        pltpu.make_async_copy(source, target, sems.at[at])
        for at, (source, target) in enumerate(
            (
                (t_any, t_ref),
                (f_any, both_ref.at[0]),
                (a_any, both_ref.at[1]),
                (class_any, class_ref),
            )
        )
    ]
    for copy in copies:
        copy.start()
    for copy in copies:
        copy.wait()
    count, rows, depth = t_ref.shape
    mats = count * rows
    fields, adjoints = both_ref[0], both_ref[1]
    own = edges_of(fields).astype(F32)
    turned = pltpu.roll(edges_of(adjoints).astype(F32), A_SHIFT, 1)
    class_edge = pltpu.roll(
        jnp.broadcast_to(edges_of(class_ref[...]).astype(F32), (rows, EDGE)), C_SHIFT, 1
    )
    lane = lax.broadcasted_iota(jnp.int32, own.shape, 1)
    edge = jnp.where(
        (lane < HW) | (lane >= EDGE - HW),
        own,
        jnp.where((lane >= A_SHIFT - HW) & (lane < A_SHIFT + HW), turned, class_edge),
    ).astype(BF16)
    parts = edge_parts(rows)
    base = mats + rows // parts
    near_ref[:mats, :] = t_ref[...].reshape(mats, depth)
    for part in range(depth // EDGE):
        start = part * (rows // parts) if part < parts else 0
        near_ref[mats:base, part * EDGE : (part + 1) * EDGE] = edge[start : start + base - mats, :]
    sent_ref[:rows, :] = fields
    sent_ref[rows : 2 * rows, :] = adjoints
    sent_ref[2 * rows :, :] = jnp.zeros_like(sent_ref[2 * rows :, :])


def relay_kernel(cross_ref, top_ref, far_ref, both_ref, beside_ref, near_ref, after_ref, out_ref):
    out_ref[0] = near_ref[...]
    out_ref[1] = top_ref[...]
    out_ref[2] = far_ref[...]
    out_ref[3] = cross_ref[...]


def pick_halo(place, pieces, mats, rows):
    tile = place[0]
    parts = edge_parts(rows)
    lane = lax.broadcasted_iota(jnp.int32, (rows, EDGE), 1)
    above = jnp.zeros((rows, EDGE), F32)
    below = jnp.zeros((rows, EDGE), F32)
    for piece_ref, at, mask in pieces:
        bands = [
            piece_ref[at, mats : mats + rows // parts, part * EDGE : (part + 1) * EDGE]
            for part in range(parts)
        ]
        cells = jnp.concatenate(bands, axis=0).astype(F32)
        owner = tile ^ mask
        above = jnp.where(owner == tile + 1, cells, above)
        below = jnp.where(owner == tile - 1, cells, below)
    return above, below


def join_halo(halo, shift):
    above, below = halo
    lane = lax.broadcasted_iota(jnp.int32, above.shape, 1)
    back = (EDGE - shift) % EDGE
    if back:
        above, below = pltpu.roll(above, back, 1), pltpu.roll(below, back, 1)
    return jnp.where(lane < EDGE // 2, above, below)


def find_pieces(spots, refs):
    return [[(refs[which], at, mask) for which, at, mask in group] for group in spots]


def fields_kernel(spots, count, both_ref, far_ref, *refs):
    place = find_place()
    (near, across), (out_ref, halos) = find_pieces(spots, refs[:-2]), refs[-2:]
    unused, rows, width = both_ref.shape
    mats = count * rows
    for start, source, pieces in ((place[1], both_ref[0], near), (1 - place[1], far_ref[:rows, :], across)):
        start = pl.multiple_of(start * rows, rows)
        for part in range(width // EDGE):
            lanes = slice(part * EDGE, (part + 1) * EDGE)
            out_ref[pl.ds(part * 2 * rows + start, rows), :] = source[:, lanes]
        halos[pl.ds(start, rows), :] = join_halo(pick_halo(place, pieces, mats, rows), 0)
    lane = lax.broadcasted_iota(jnp.int32, (LEAD, EDGE), 1)
    packed = jnp.zeros((LEAD, EDGE), F32)
    for group in range(2 * rows // LEAD):
        halo = halos[group * LEAD : (group + 1) * LEAD, :]
        narrow = jnp.where(lane < LEAD, halo, pltpu.roll(halo, 2 * LEAD, 1))
        first = 2 * LEAD * group
        moved = pltpu.roll(narrow, first, 1) if group else narrow
        packed = jnp.where((lane >= first) & (lane < first + 2 * LEAD), moved, packed)
    out_ref[2 * rows * (width // EDGE) :, :] = packed.astype(BF16)


def unpack_fields(piece_ref, padded, start, block):
    width = padded.shape[1] - EDGE
    for part in range(width // EDGE):
        lanes = slice(part * EDGE, (part + 1) * EDGE)
        padded[pl.ds(start, block), lanes] = piece_ref[part * block : (part + 1) * block, :]
    packed = piece_ref[block * (width // EDGE) :, :].astype(F32)
    lane = lax.broadcasted_iota(jnp.int32, (LEAD, EDGE), 1)
    for group in range(block // LEAD):
        narrow = pltpu.roll(packed, EDGE - 2 * LEAD * group, 1) if group else packed
        halo = jnp.where(lane < EDGE // 2, narrow, pltpu.roll(narrow, EDGE - 2 * LEAD, 1))
        padded[pl.ds(start + group * LEAD, LEAD), width:] = halo.astype(BF16)


def prepare_kernel(rows, couple_ref, links_ref, after_ref, mats_ref, own_ref, spread_ref, links, weights, sems):
    copies = []
    for chunk in range(SLOTS // CHUNK):
        span = pl.ds(chunk * CHUNK, CHUNK)
        copies.append(pltpu.make_async_copy(couple_ref.at[span], mats_ref.at[span], sems.at[chunk]))
    linked = pltpu.make_async_copy(links_ref, links, sems.at[len(copies)])
    linked.start()
    for copy in copies:
        copy.start()
    linked.wait()
    weights[...] = jnp.zeros_like(weights)
    weights[:SLOTS, :] = jnp.where(links[...] >= 0, 1.0, 0.0)
    filled = weights[...].astype(BF16)
    row = lax.broadcasted_iota(jnp.int32, (filled.shape[0], 2 * EDGE), 0)
    lane = lax.broadcasted_iota(jnp.int32, (filled.shape[0], 2 * EDGE), 1)
    for pair in range(SLOTS // 2):
        chosen = row == 2 * pair + (lane >= EDGE).astype(jnp.int32)
        unit = jnp.where(chosen, 1.0, 0.0).astype(BF16)
        spread = lax.dot_general(
            filled, unit, (((0,), (0,)), ((), ())), preferred_element_type=F32
        ).astype(BF16)
        spread_ref[2 * pair] = spread[:, :EDGE]
        spread_ref[2 * pair + 1] = spread[:, EDGE:]
    depth = mats_ref.shape[1]
    odd = find_place()[1]
    lane = lax.broadcasted_iota(jnp.int32, (depth, EDGE), 1)
    first = jnp.where((lane // rows) % 2 == odd, 1.0, 0.0).astype(BF16)
    second = (1.0 - first).astype(BF16)
    shift = jnp.where(odd == 1, EDGE - rows, rows)
    for chunk, copy in enumerate(copies):
        copy.wait()
        for mat in range(chunk * CHUNK, (chunk + 1) * CHUNK):
            moved = pltpu.roll(mats_ref[mat, :, EDGE : 2 * EDGE], shift, 1)
            chosen = mats_ref[mat, :, :EDGE] * first + moved * second
            slot = SLOTS - 1 - mat
            side = (slot % 2) * EDGE
            own_ref[slot // 2, :, side : side + EDGE] = chosen


def stand_up(cells, upright):
    width = cells.shape[1] - EDGE
    turned = cells.astype(F32).T
    for half in range(upright.shape[0]):
        lanes = slice(half * EDGE, (half + 1) * EDGE)
        upright[half, LEAD : LEAD + width, :] = turned[:width, lanes]
        upright[half, LEAD + width :, :] = turned[width : width + LEAD, lanes]
        upright[half, :LEAD, :] = turned[width + EDGE - LEAD :, lanes]


def couple_slots(upright, spread_ref, mats_ref, slots, total=None):
    width = spread_ref.shape[1]
    for slot in slots:
        start = LEAD + OFFSETS[slot]
        weight = spread_ref[slot]
        selected = jnp.concatenate(
            [
                upright[half, start : start + width, :].astype(BF16) * weight
                for half in range(upright.shape[0])
            ],
            axis=1,
        )
        product = lax.dot_general(
            selected, mats_ref[slot], (((1,), (1,)), ((), ())), preferred_element_type=F32
        )
        total = product if total is None else total + product
    return total


def couple_own(upright, spread_ref, own_ref, products):
    width = spread_ref.shape[1]
    for pair in range(SLOTS // 2):
        both = jnp.dot(upright, own_ref[pair], preferred_element_type=F32)
        products[2 * pair] = both[:, :EDGE]
        products[2 * pair + 1] = both[:, EDGE:]
    bands = []
    for band in range(0, width, BAND):
        total = None
        for slot in range(SLOTS):
            start = LEAD + OFFSETS[slot] + band
            term = products[slot, start : start + BAND, :] * spread_ref[slot, band : band + BAND, :].astype(F32)
            total = term if total is None else total + term
        bands.append(total)
    return jnp.concatenate(bands, axis=0)


def adjoint_kernel(
    spots, count, sends, both_ref, far_ref, class_ref, spread_ref, own_ref, after_ref, *refs
):
    place = find_place()
    near, across = find_pieces(spots, refs[: -sends - 4])
    keep_ref, *send_refs = refs[-sends - 4 : -4]
    total_ref, expanded, stacked, products = refs[-4:]
    unused, rows, width = both_ref.shape
    mats = count * rows
    halos = [pick_halo(place, pieces, mats, rows) for pieces in (near, across)]
    padded = [
        jnp.concatenate([own, join_halo(halo, A_SHIFT).astype(BF16)], axis=1)
        for own, halo in ((both_ref[1], halos[0]), (far_ref[rows : 2 * rows, :], halos[1]))
    ]
    class_halo = join_halo(tuple(cells[0:8, :] for cells in halos[0]), C_SHIFT)
    labels = jnp.concatenate([class_ref[...], class_halo[0:1, :].astype(jnp.int32)], axis=1)
    at = 0
    for own, pieces in zip(padded, (near, across)):
        for ref, spot, mask in pieces:
            stacked[at : at + mats, :] = ref[spot, :mats, :]
            for local_class in range(count):
                hit = labels == (place[0] ^ mask) * count + local_class
                factor = jnp.where(hit, 1.0, 0.0).astype(BF16)
                expanded[at : at + rows, :] = own * factor
                at += rows
    scattered = lax.dot_general(
        stacked[...], expanded[...], (((0,), (0,)), ((), ())), preferred_element_type=F32
    )
    turned = scattered.astype(BF16).T
    upright = jnp.concatenate(
        [turned[width + EDGE - LEAD :], turned[:width], turned[width : width + LEAD]], axis=0
    )
    total_ref[...] = couple_own(upright, spread_ref, own_ref, products).T

    def block(rel):
        start = ((place[2] ^ rel) * 2 + place[1]) * rows
        moved = start - EDGE + jnp.where(place[1] == 1, -rows, rows)
        return pl.ds(pl.multiple_of(jnp.where(start < EDGE, start, moved), rows), rows)

    keep_ref[...] = total_ref[block(0), :]
    for rel, send_ref in enumerate(send_refs, 1):
        send_ref[...] = total_ref[block(rel), :].astype(BF16)


def forward_kernel(
    spots, count, rels, both_ref, class_ref, spread_ref, mats_ref, *refs
):
    place = find_place()
    pieces, refs = refs[: len(rels)], refs[len(rels) :]
    (near, across), (out_ref, padded, upright, stacked) = find_pieces(spots, refs[:-4]), refs[-4:]
    unused, rows, width = both_ref.shape
    mats = count * rows
    block = 2 * rows
    for rel, piece_ref in zip(rels, pieces):
        start = pl.multiple_of((place[2] ^ rel) * block, block)
        unpack_fields(piece_ref, padded, start, block)
    stand_up(padded[...], upright)
    coupled = couple_slots(upright, spread_ref, mats_ref, range(SLOTS)).astype(BF16)
    for piece, (ref, spot, mask) in enumerate(near):
        stacked[piece * mats : (piece + 1) * mats, :] = ref[spot, :mats, :]
    product = lax.dot_general(
        stacked[...], coupled, (((1,), (1,)), ((), ())), preferred_element_type=F32
    )
    applied = jnp.zeros((rows, width), F32)
    labels = class_ref[...]
    for piece, (ref, spot, mask) in enumerate(near):
        for local_class in range(count):
            hit = labels == (place[0] ^ mask) * count + local_class
            at = piece * mats + local_class * rows
            applied = jnp.where(hit, product[at : at + rows, :], applied)
    out_ref[...] = (both_ref[0].astype(F32) - applied).astype(BF16)


def finish_kernel(both_ref, keep_ref, forward_ref, *refs):
    arrived, (out_ref, adjoint_ref) = refs[:-2], refs[-2:]
    out_ref[...] = forward_ref[...]
    returned = keep_ref[...]
    for ref in arrived:
        returned = returned + ref[...].astype(F32)
    adjoint_ref[...] = (both_ref[1].astype(F32) - returned).astype(BF16)


def local(fields, adjoints, couple, tmatrices, neighbours, classes):
    tiles, coefs = lax.axis_size("tiles"), lax.axis_size("coef")
    rows, width = fields.shape
    count, unused, depth = tmatrices.shape

    def swap(cells, tile_mask, coef_mask):
        pairs = [
            (i * coefs + j, (i ^ tile_mask) * coefs + (j ^ coef_mask))
            for i in range(tiles)
            for j in range(coefs)
        ]
        return lax.ppermute(cells, ("tiles", "coef"), pairs)

    labels = classes.reshape(1, width)
    mats = count * rows
    near_rows = mats + rows // edge_parts(rows)
    total_rows = couple.shape[1]
    near_own, both, sent_far, labels = pl.pallas_call(
        pack_kernel,
        out_shape=(
            jax.ShapeDtypeStruct((near_rows, depth), BF16),
            jax.ShapeDtypeStruct((2, rows, width), BF16),
            jax.ShapeDtypeStruct((2 * rows + LEAD, width), BF16),
            jax.ShapeDtypeStruct(labels.shape, jnp.int32),
        ),
        in_specs=[HBM] * 4,
        out_specs=(VMEM,) * 4,
        scratch_shapes=[pltpu.VMEM(tmatrices.shape, BF16), pltpu.SemaphoreType.DMA((4,))],
        compiler_params=PARAMS,
    )(*[in_hbm(cells) for cells in (tmatrices, fields, adjoints, labels)])
    mats_held, mats_own, spread = pl.pallas_call(
        functools.partial(prepare_kernel, rows),
        out_shape=(
            jax.ShapeDtypeStruct(couple.shape, BF16),
            jax.ShapeDtypeStruct((SLOTS // 2, total_rows, 2 * EDGE), BF16),
            jax.ShapeDtypeStruct((SLOTS, width, EDGE), BF16),
        ),
        in_specs=[HBM, HBM, VMEM],
        out_specs=(VMEM,) * 3,
        scratch_shapes=[
            pltpu.VMEM((SLOTS, width), jnp.int32),
            pltpu.VMEM((SLOTS + -SLOTS % 16, width), F32),
            pltpu.SemaphoreType.DMA((SLOTS // CHUNK + 1,)),
        ],
        cost_estimate=pl.CostEstimate(flops=0, bytes_accessed=4 * couple.size, transcendentals=0),
        compiler_params=PARAMS,
    )(in_hbm(couple), in_hbm(neighbours.T), labels)

    top = tiles // 2
    both_far = swap(sent_far, 0, 1)
    beside = swap(near_own, 1, 0)
    first = pl.pallas_call(
        relay_kernel,
        out_shape=jax.ShapeDtypeStruct((4, near_rows, depth), BF16),
        in_specs=[VMEM] * 7,
        out_specs=VMEM,
        compiler_params=PARAMS,
    )(
        swap(near_own, top ^ 1, 1),
        swap(near_own, top ^ 1, 0),
        swap(near_own, 1, 1),
        both_far,
        beside,
        near_own,
        mats_held,
    )
    held, lows = [first], [0]
    bit = top // 2
    while bit >= 1:
        held += [swap(block, bit, 0) for block in held]
        lows += [low ^ bit for low in lows]
        bit //= 2
    spots = (
        [(at, slot, low ^ (0, top ^ 1)[slot]) for at, low in enumerate(lows) for slot in (0, 1)],
        [(at, slot, low ^ (1, top ^ 1)[slot - 2]) for at, low in enumerate(lows) for slot in (2, 3)],
    )
    if tiles == 4:
        sources = [first, beside[None]]
        edge_spots = ([(0, 1, 3), (1, 0, 1)], [(0, 2, 1), (0, 3, 3)])
    else:
        sources, edge_spots = held, spots

    padded_fields = pl.pallas_call(
        functools.partial(fields_kernel, edge_spots, count),
        out_shape=jax.ShapeDtypeStruct((2 * rows * (width // EDGE) + LEAD, EDGE), BF16),
        in_specs=[VMEM] * (2 + len(sources)),
        out_specs=VMEM,
        scratch_shapes=[pltpu.VMEM((2 * rows, EDGE), F32)],
        compiler_params=PARAMS,
    )(both, both_far, *sources)

    groups = coefs // 2
    gathered = {0: padded_fields}
    for rel in range(1, groups):
        gathered[rel] = swap(padded_fields, 0, 2 * rel)
    rels = [0, 1, 3, 2] if groups == 4 else sorted(gathered)


    def work(slots):
        size = slots * total_rows * total_rows
        return pl.CostEstimate(flops=2 * size * width, bytes_accessed=2 * size, transcendentals=0)

    keep, *sent = pl.pallas_call(
        functools.partial(adjoint_kernel, spots, count, groups),
        out_shape=(jax.ShapeDtypeStruct((rows, width), F32),)
        + (jax.ShapeDtypeStruct((rows, width), BF16),) * (groups - 1),
        in_specs=[VMEM] * 5 + [ANY] + [VMEM] * len(held),
        out_specs=(VMEM,) * groups,
        scratch_shapes=[
            pltpu.VMEM((EDGE, width), F32),
            pltpu.VMEM((2 * tiles * mats, width + EDGE), BF16),
            pltpu.VMEM((2 * tiles * mats, depth), BF16),
            pltpu.VMEM((SLOTS, width + 2 * LEAD, EDGE), F32),
        ],
        cost_estimate=work(SLOTS + 8),
        compiler_params=PARAMS,
    )(both, both_far, labels, spread, mats_own, padded_fields, *held)
    arrived = [swap(block, 0, 2 * rel) for rel, block in enumerate(sent, 1)]

    forward = pl.pallas_call(
        functools.partial(forward_kernel, spots, count, rels),
        out_shape=jax.ShapeDtypeStruct((rows, width), BF16),
        in_specs=[VMEM] * (4 + len(rels) + len(held)),
        out_specs=VMEM,
        scratch_shapes=[
            pltpu.VMEM((total_rows, width + EDGE), BF16),
            pltpu.VMEM((total_rows // EDGE, width + 2 * LEAD, EDGE), F32),
            pltpu.VMEM((tiles * mats, depth), BF16),
        ],
        cost_estimate=work(SLOTS + 8),
        compiler_params=PARAMS,
    )(both, labels, spread, mats_held, *[gathered[rel] for rel in rels], *held)
    return pl.pallas_call(
        finish_kernel,
        out_shape=(jax.ShapeDtypeStruct((rows, width), BF16),) * 2,
        in_specs=[VMEM] * (3 + len(arrived)),
        out_specs=(VMEM, VMEM),
        compiler_params=PARAMS,
    )(both, keep, forward, *[arrived[k - 1] for k in ((3, 2, 1) if groups == 4 else range(1, groups))])


def solution(mesh):
    placed = (
        P("coef", "tiles"),
        P("coef", "tiles"),
        P(),
        P("tiles", "coef", None),
        P("tiles", None),
        P("tiles"),
    )
    return jax.shard_map(
        local,
        mesh=mesh,
        in_specs=placed,
        out_specs=(P("coef", "tiles"), P("coef", "tiles")),
        check_vma=False,
    )
```

```python
import functools

import jax
import jax.numpy as jnp
from jax import lax
from jax.experimental import pallas as pl
from jax.experimental.pallas import tpu as pltpu
from jax.sharding import PartitionSpec as P

SLOTS = 30
HW = 15
EDGE = 128
CHUNK = 5
LEAD = 16
BAND = 128
A_SHIFT = 32
C_SHIFT = 64
OFFSETS = [slot - HW + (1 if slot >= HW else 0) for slot in range(SLOTS)]
BF16 = jnp.bfloat16
F32 = jnp.float32
VMEM = pl.BlockSpec(memory_space=pltpu.VMEM)
ANY = pl.BlockSpec(memory_space=pl.ANY)
HBM = pl.BlockSpec(memory_space=pltpu.HBM)
PARAMS = pltpu.CompilerParams(vmem_limit_bytes=24 * 1024 * 1024)


def in_hbm(cells):
    return pltpu.with_memory_space_constraint(cells, pltpu.HBM)


def find_place():
    coef = lax.axis_index("coef")
    return lax.axis_index("tiles"), coef & 1, coef >> 1


def edges_of(cells):
    width = cells.shape[1]
    head, tail = cells[:, :EDGE], cells[:, width - EDGE :]
    lane = lax.broadcasted_iota(jnp.int32, head.shape, 1)
    return jnp.where(lane < EDGE // 2, head, tail)


def edge_parts(rows):
    return 2 if rows % 32 == 0 else 1


def pack_kernel(
    t_any, f_any, a_any, class_any, near_ref, both_ref, sent_ref, class_ref, t_ref, sems
):
    copies = [
        pltpu.make_async_copy(source, target, sems.at[at])
        for at, (source, target) in enumerate(
            (
                (t_any, t_ref),
                (f_any, both_ref.at[0]),
                (a_any, both_ref.at[1]),
                (class_any, class_ref),
            )
        )
    ]
    for copy in copies:
        copy.start()
    for copy in copies:
        copy.wait()
    count, rows, depth = t_ref.shape
    mats = count * rows
    fields, adjoints = both_ref[0], both_ref[1]
    own = edges_of(fields).astype(F32)
    turned = pltpu.roll(edges_of(adjoints).astype(F32), A_SHIFT, 1)
    class_edge = pltpu.roll(
        jnp.broadcast_to(edges_of(class_ref[...]).astype(F32), (rows, EDGE)), C_SHIFT, 1
    )
    lane = lax.broadcasted_iota(jnp.int32, own.shape, 1)
    edge = jnp.where(
        (lane < HW) | (lane >= EDGE - HW),
        own,
        jnp.where((lane >= A_SHIFT - HW) & (lane < A_SHIFT + HW), turned, class_edge),
    ).astype(BF16)
    parts = edge_parts(rows)
    base = mats + rows // parts
    near_ref[:mats, :] = t_ref[...].reshape(mats, depth)
    for part in range(depth // EDGE):
        start = part * (rows // parts) if part < parts else 0
        near_ref[mats:base, part * EDGE : (part + 1) * EDGE] = edge[start : start + base - mats, :]
    sent_ref[:rows, :] = fields
    sent_ref[rows : 2 * rows, :] = adjoints
    sent_ref[2 * rows :, :] = jnp.zeros_like(sent_ref[2 * rows :, :])


def relay_kernel(cross_ref, top_ref, far_ref, both_ref, beside_ref, near_ref, after_ref, out_ref):
    out_ref[0] = near_ref[...]
    out_ref[1] = top_ref[...]
    out_ref[2] = far_ref[...]
    out_ref[3] = cross_ref[...]


def pick_halo(place, pieces, mats, rows):
    tile = place[0]
    parts = edge_parts(rows)
    lane = lax.broadcasted_iota(jnp.int32, (rows, EDGE), 1)
    above = jnp.zeros((rows, EDGE), F32)
    below = jnp.zeros((rows, EDGE), F32)
    for piece_ref, at, mask in pieces:
        bands = [
            piece_ref[at, mats : mats + rows // parts, part * EDGE : (part + 1) * EDGE]
            for part in range(parts)
        ]
        cells = jnp.concatenate(bands, axis=0).astype(F32)
        owner = tile ^ mask
        above = jnp.where(owner == tile + 1, cells, above)
        below = jnp.where(owner == tile - 1, cells, below)
    return above, below


def join_halo(halo, shift):
    above, below = halo
    lane = lax.broadcasted_iota(jnp.int32, above.shape, 1)
    back = (EDGE - shift) % EDGE
    if back:
        above, below = pltpu.roll(above, back, 1), pltpu.roll(below, back, 1)
    return jnp.where(lane < EDGE // 2, above, below)


def find_pieces(spots, refs):
    return [[(refs[which], at, mask) for which, at, mask in group] for group in spots]


def fields_kernel(spots, count, both_ref, far_ref, *refs):
    place = find_place()
    (near, across), (out_ref, halos) = find_pieces(spots, refs[:-2]), refs[-2:]
    unused, rows, width = both_ref.shape
    mats = count * rows
    for start, source, pieces in ((place[1], both_ref[0], near), (1 - place[1], far_ref[:rows, :], across)):
        start = pl.multiple_of(start * rows, rows)
        for part in range(width // EDGE):
            lanes = slice(part * EDGE, (part + 1) * EDGE)
            out_ref[pl.ds(part * 2 * rows + start, rows), :] = source[:, lanes]
        halos[pl.ds(start, rows), :] = join_halo(pick_halo(place, pieces, mats, rows), 0)
    lane = lax.broadcasted_iota(jnp.int32, (LEAD, EDGE), 1)
    packed = jnp.zeros((LEAD, EDGE), F32)
    for group in range(2 * rows // LEAD):
        halo = halos[group * LEAD : (group + 1) * LEAD, :]
        narrow = jnp.where(lane < LEAD, halo, pltpu.roll(halo, 2 * LEAD, 1))
        first = 2 * LEAD * group
        moved = pltpu.roll(narrow, first, 1) if group else narrow
        packed = jnp.where((lane >= first) & (lane < first + 2 * LEAD), moved, packed)
    out_ref[2 * rows * (width // EDGE) :, :] = packed.astype(BF16)


def unpack_fields(piece_ref, padded, start, block):
    width = padded.shape[1] - EDGE
    for part in range(width // EDGE):
        lanes = slice(part * EDGE, (part + 1) * EDGE)
        padded[pl.ds(start, block), lanes] = piece_ref[part * block : (part + 1) * block, :]
    packed = piece_ref[block * (width // EDGE) :, :].astype(F32)
    lane = lax.broadcasted_iota(jnp.int32, (LEAD, EDGE), 1)
    for group in range(block // LEAD):
        narrow = pltpu.roll(packed, EDGE - 2 * LEAD * group, 1) if group else packed
        halo = jnp.where(lane < EDGE // 2, narrow, pltpu.roll(narrow, EDGE - 2 * LEAD, 1))
        padded[pl.ds(start + group * LEAD, LEAD), width:] = halo.astype(BF16)


def prepare_kernel(rows, couple_ref, links_ref, after_ref, mats_ref, own_ref, spread_ref, links, weights, sems):
    copies = []
    for chunk in range(SLOTS // CHUNK):
        span = pl.ds(chunk * CHUNK, CHUNK)
        copies.append(pltpu.make_async_copy(couple_ref.at[span], mats_ref.at[span], sems.at[chunk]))
    linked = pltpu.make_async_copy(links_ref, links, sems.at[len(copies)])
    linked.start()
    for copy in copies:
        copy.start()
    depth = mats_ref.shape[1]
    odd = find_place()[1]
    lane = lax.broadcasted_iota(jnp.int32, (depth, EDGE), 1)
    first = jnp.where((lane // rows) % 2 == odd, 1.0, 0.0).astype(BF16)
    second = (1.0 - first).astype(BF16)
    shift = jnp.where(odd == 1, EDGE - rows, rows)
    for chunk, copy in enumerate(copies):
        if chunk == 1:
            linked.wait()
            weights[...] = jnp.zeros_like(weights)
            weights[:SLOTS, :] = jnp.where(links[...] >= 0, 1.0, 0.0)
            filled = weights[...].astype(BF16)
            row = lax.broadcasted_iota(jnp.int32, (filled.shape[0], 2 * EDGE), 0)
            lane = lax.broadcasted_iota(jnp.int32, (filled.shape[0], 2 * EDGE), 1)
            for pair in range(SLOTS // 2):
                chosen = row == 2 * pair + (lane >= EDGE).astype(jnp.int32)
                unit = jnp.where(chosen, 1.0, 0.0).astype(BF16)
                spread = lax.dot_general(
                    filled, unit, (((0,), (0,)), ((), ())), preferred_element_type=F32
                ).astype(BF16)
                spread_ref[2 * pair] = spread[:, :EDGE]
                spread_ref[2 * pair + 1] = spread[:, EDGE:]
        copy.wait()
        for mat in range(chunk * CHUNK, (chunk + 1) * CHUNK):
            moved = pltpu.roll(mats_ref[mat, :, EDGE : 2 * EDGE], shift, 1)
            chosen = mats_ref[mat, :, :EDGE] * first + moved * second
            slot = SLOTS - 1 - mat
            side = (slot % 2) * EDGE
            own_ref[slot // 2, :, side : side + EDGE] = chosen


def stand_up(cells, upright):
    width = cells.shape[1] - EDGE
    turned = cells.astype(F32).T
    for half in range(upright.shape[0]):
        lanes = slice(half * EDGE, (half + 1) * EDGE)
        upright[half, LEAD : LEAD + width, :] = turned[:width, lanes]
        upright[half, LEAD + width :, :] = turned[width : width + LEAD, lanes]
        upright[half, :LEAD, :] = turned[width + EDGE - LEAD :, lanes]


def couple_slots(upright, spread_ref, mats_ref, slots, total=None):
    width = spread_ref.shape[1]
    for slot in slots:
        start = LEAD + OFFSETS[slot]
        weight = spread_ref[slot]
        selected = jnp.concatenate(
            [
                upright[half, start : start + width, :].astype(BF16) * weight
                for half in range(upright.shape[0])
            ],
            axis=1,
        )
        product = lax.dot_general(
            selected, mats_ref[slot], (((1,), (1,)), ((), ())), preferred_element_type=F32
        )
        total = product if total is None else total + product
    return total


def couple_own(upright, spread_ref, own_ref, products):
    width = spread_ref.shape[1]
    for pair in range(SLOTS // 2):
        both = jnp.dot(upright, own_ref[pair], preferred_element_type=F32)
        products[2 * pair] = both[:, :EDGE]
        products[2 * pair + 1] = both[:, EDGE:]
    bands = []
    for band in range(0, width, BAND):
        total = None
        for slot in range(SLOTS):
            start = LEAD + OFFSETS[slot] + band
            term = products[slot, start : start + BAND, :] * spread_ref[slot, band : band + BAND, :].astype(F32)
            total = term if total is None else total + term
        bands.append(total)
    return jnp.concatenate(bands, axis=0)


def adjoint_kernel(
    spots, count, sends, both_ref, far_ref, class_ref, spread_ref, own_ref, after_ref, *refs
):
    place = find_place()
    near, across = find_pieces(spots, refs[: -sends - 4])
    keep_ref, *send_refs = refs[-sends - 4 : -4]
    total_ref, expanded, stacked, products = refs[-4:]
    unused, rows, width = both_ref.shape
    mats = count * rows
    halos = [pick_halo(place, pieces, mats, rows) for pieces in (near, across)]
    padded = [
        jnp.concatenate([own, join_halo(halo, A_SHIFT).astype(BF16)], axis=1)
        for own, halo in ((both_ref[1], halos[0]), (far_ref[rows : 2 * rows, :], halos[1]))
    ]
    class_halo = join_halo(tuple(cells[0:8, :] for cells in halos[0]), C_SHIFT)
    labels = jnp.concatenate([class_ref[...], class_halo[0:1, :].astype(jnp.int32)], axis=1)
    at = 0
    for own, pieces in zip(padded, (near, across)):
        for ref, spot, mask in pieces:
            stacked[at : at + mats, :] = ref[spot, :mats, :]
            for local_class in range(count):
                hit = labels == (place[0] ^ mask) * count + local_class
                factor = jnp.where(hit, 1.0, 0.0).astype(BF16)
                expanded[at : at + rows, :] = own * factor
                at += rows
    scattered = lax.dot_general(
        stacked[...], expanded[...], (((0,), (0,)), ((), ())), preferred_element_type=F32
    )
    turned = scattered.astype(BF16).T
    upright = jnp.concatenate(
        [turned[width + EDGE - LEAD :], turned[:width], turned[width : width + LEAD]], axis=0
    )
    total_ref[...] = couple_own(upright, spread_ref, own_ref, products).T

    def block(rel):
        start = ((place[2] ^ rel) * 2 + place[1]) * rows
        moved = start - EDGE + jnp.where(place[1] == 1, -rows, rows)
        return pl.ds(pl.multiple_of(jnp.where(start < EDGE, start, moved), rows), rows)

    keep_ref[...] = total_ref[block(0), :]
    for rel, send_ref in enumerate(send_refs, 1):
        send_ref[...] = total_ref[block(rel), :].astype(BF16)


def forward_kernel(
    spots, count, rels, both_ref, class_ref, spread_ref, mats_ref, *refs
):
    place = find_place()
    pieces, refs = refs[: len(rels)], refs[len(rels) :]
    (near, across), (out_ref, padded, upright, stacked) = find_pieces(spots, refs[:-4]), refs[-4:]
    unused, rows, width = both_ref.shape
    mats = count * rows
    block = 2 * rows
    for rel, piece_ref in zip(rels, pieces):
        start = pl.multiple_of((place[2] ^ rel) * block, block)
        unpack_fields(piece_ref, padded, start, block)
    stand_up(padded[...], upright)
    coupled = couple_slots(upright, spread_ref, mats_ref, range(SLOTS)).astype(BF16)
    for piece, (ref, spot, mask) in enumerate(near):
        stacked[piece * mats : (piece + 1) * mats, :] = ref[spot, :mats, :]
    product = lax.dot_general(
        stacked[...], coupled, (((1,), (1,)), ((), ())), preferred_element_type=F32
    )
    applied = jnp.zeros((rows, width), F32)
    labels = class_ref[...]
    for piece, (ref, spot, mask) in enumerate(near):
        for local_class in range(count):
            hit = labels == (place[0] ^ mask) * count + local_class
            at = piece * mats + local_class * rows
            applied = jnp.where(hit, product[at : at + rows, :], applied)
    out_ref[...] = (both_ref[0].astype(F32) - applied).astype(BF16)


def finish_kernel(both_ref, keep_ref, forward_ref, *refs):
    arrived, (out_ref, adjoint_ref) = refs[:-2], refs[-2:]
    out_ref[...] = forward_ref[...]
    returned = keep_ref[...]
    for ref in arrived:
        returned = returned + ref[...].astype(F32)
    adjoint_ref[...] = (both_ref[1].astype(F32) - returned).astype(BF16)


def local(fields, adjoints, couple, tmatrices, neighbours, classes):
    tiles, coefs = lax.axis_size("tiles"), lax.axis_size("coef")
    rows, width = fields.shape
    count, unused, depth = tmatrices.shape

    def swap(cells, tile_mask, coef_mask):
        pairs = [
            (i * coefs + j, (i ^ tile_mask) * coefs + (j ^ coef_mask))
            for i in range(tiles)
            for j in range(coefs)
        ]
        return lax.ppermute(cells, ("tiles", "coef"), pairs)

    labels = classes.reshape(1, width)
    mats = count * rows
    near_rows = mats + rows // edge_parts(rows)
    total_rows = couple.shape[1]
    near_own, both, sent_far, labels = pl.pallas_call(
        pack_kernel,
        out_shape=(
            jax.ShapeDtypeStruct((near_rows, depth), BF16),
            jax.ShapeDtypeStruct((2, rows, width), BF16),
            jax.ShapeDtypeStruct((2 * rows + LEAD, width), BF16),
            jax.ShapeDtypeStruct(labels.shape, jnp.int32),
        ),
        in_specs=[HBM] * 4,
        out_specs=(VMEM,) * 4,
        scratch_shapes=[pltpu.VMEM(tmatrices.shape, BF16), pltpu.SemaphoreType.DMA((4,))],
        compiler_params=PARAMS,
    )(*[in_hbm(cells) for cells in (tmatrices, fields, adjoints, labels)])
    mats_held, mats_own, spread = pl.pallas_call(
        functools.partial(prepare_kernel, rows),
        out_shape=(
            jax.ShapeDtypeStruct(couple.shape, BF16),
            jax.ShapeDtypeStruct((SLOTS // 2, total_rows, 2 * EDGE), BF16),
            jax.ShapeDtypeStruct((SLOTS, width, EDGE), BF16),
        ),
        in_specs=[HBM, HBM, VMEM],
        out_specs=(VMEM,) * 3,
        scratch_shapes=[
            pltpu.VMEM((SLOTS, width), jnp.int32),
            pltpu.VMEM((SLOTS + -SLOTS % 16, width), F32),
            pltpu.SemaphoreType.DMA((SLOTS // CHUNK + 1,)),
        ],
        cost_estimate=pl.CostEstimate(flops=0, bytes_accessed=4 * couple.size, transcendentals=0),
        compiler_params=PARAMS,
    )(in_hbm(couple), in_hbm(neighbours.T), labels)

    top = tiles // 2
    both_far = swap(sent_far, 0, 1)
    beside = swap(near_own, 1, 0)
    first = pl.pallas_call(
        relay_kernel,
        out_shape=jax.ShapeDtypeStruct((4, near_rows, depth), BF16),
        in_specs=[VMEM] * 7,
        out_specs=VMEM,
        compiler_params=PARAMS,
    )(
        swap(near_own, top ^ 1, 1),
        swap(near_own, top ^ 1, 0),
        swap(near_own, 1, 1),
        both_far,
        beside,
        near_own,
        mats_held,
    )
    held, lows = [first], [0]
    bit = top // 2
    while bit >= 1:
        held += [swap(block, bit, 0) for block in held]
        lows += [low ^ bit for low in lows]
        bit //= 2
    spots = (
        [(at, slot, low ^ (0, top ^ 1)[slot]) for at, low in enumerate(lows) for slot in (0, 1)],
        [(at, slot, low ^ (1, top ^ 1)[slot - 2]) for at, low in enumerate(lows) for slot in (2, 3)],
    )
    if tiles == 4:
        sources = [first, beside[None]]
        edge_spots = ([(0, 1, 3), (1, 0, 1)], [(0, 2, 1), (0, 3, 3)])
    else:
        sources, edge_spots = held, spots

    padded_fields = pl.pallas_call(
        functools.partial(fields_kernel, edge_spots, count),
        out_shape=jax.ShapeDtypeStruct((2 * rows * (width // EDGE) + LEAD, EDGE), BF16),
        in_specs=[VMEM] * (2 + len(sources)),
        out_specs=VMEM,
        scratch_shapes=[pltpu.VMEM((2 * rows, EDGE), F32)],
        compiler_params=PARAMS,
    )(both, both_far, *sources)

    groups = coefs // 2
    gathered = {0: padded_fields}
    for rel in range(1, groups):
        gathered[rel] = swap(padded_fields, 0, 2 * rel)
    rels = [0, 1, 3, 2] if groups == 4 else sorted(gathered)


    def work(slots):
        size = slots * total_rows * total_rows
        return pl.CostEstimate(flops=2 * size * width, bytes_accessed=2 * size, transcendentals=0)

    keep, *sent = pl.pallas_call(
        functools.partial(adjoint_kernel, spots, count, groups),
        out_shape=(jax.ShapeDtypeStruct((rows, width), F32),)
        + (jax.ShapeDtypeStruct((rows, width), BF16),) * (groups - 1),
        in_specs=[VMEM] * 5 + [ANY] + [VMEM] * len(held),
        out_specs=(VMEM,) * groups,
        scratch_shapes=[
            pltpu.VMEM((EDGE, width), F32),
            pltpu.VMEM((2 * tiles * mats, width + EDGE), BF16),
            pltpu.VMEM((2 * tiles * mats, depth), BF16),
            pltpu.VMEM((SLOTS, width + 2 * LEAD, EDGE), F32),
        ],
        cost_estimate=work(SLOTS + 8),
        compiler_params=PARAMS,
    )(both, both_far, labels, spread, mats_own, padded_fields, *held)
    arrived = [swap(block, 0, 2 * rel) for rel, block in enumerate(sent, 1)]

    forward = pl.pallas_call(
        functools.partial(forward_kernel, spots, count, rels),
        out_shape=jax.ShapeDtypeStruct((rows, width), BF16),
        in_specs=[VMEM] * (4 + len(rels) + len(held)),
        out_specs=VMEM,
        scratch_shapes=[
            pltpu.VMEM((total_rows, width + EDGE), BF16),
            pltpu.VMEM((total_rows // EDGE, width + 2 * LEAD, EDGE), F32),
            pltpu.VMEM((tiles * mats, depth), BF16),
        ],
        cost_estimate=work(SLOTS + 8),
        compiler_params=PARAMS,
    )(both, labels, spread, mats_held, *[gathered[rel] for rel in rels], *held)
    return pl.pallas_call(
        finish_kernel,
        out_shape=(jax.ShapeDtypeStruct((rows, width), BF16),) * 2,
        in_specs=[VMEM] * (3 + len(arrived)),
        out_specs=(VMEM, VMEM),
        compiler_params=PARAMS,
    )(both, keep, forward, *[arrived[k - 1] for k in ((3, 2, 1) if groups == 4 else range(1, groups))])


def solution(mesh):
    placed = (
        P("coef", "tiles"),
        P("coef", "tiles"),
        P(),
        P("tiles", "coef", None),
        P("tiles", None),
        P("tiles"),
    )
    return jax.shard_map(
        local,
        mesh=mesh,
        in_specs=placed,
        out_specs=(P("coef", "tiles"), P("coef", "tiles")),
        check_vma=False,
    )
```

```python
import functools

import jax
import jax.numpy as jnp
from jax import lax
from jax.experimental import pallas as pl
from jax.experimental.pallas import tpu as pltpu
from jax.sharding import PartitionSpec as P

SLOTS = 30
HW = 15
EDGE = 128
CHUNK = 10
LEAD = 16
BAND = 128
A_SHIFT = 32
C_SHIFT = 64
OFFSETS = [slot - HW + (1 if slot >= HW else 0) for slot in range(SLOTS)]
BF16 = jnp.bfloat16
F32 = jnp.float32
VMEM = pl.BlockSpec(memory_space=pltpu.VMEM)
ANY = pl.BlockSpec(memory_space=pl.ANY)
HBM = pl.BlockSpec(memory_space=pltpu.HBM)
PARAMS = pltpu.CompilerParams(vmem_limit_bytes=24 * 1024 * 1024)


def in_hbm(cells):
    return pltpu.with_memory_space_constraint(cells, pltpu.HBM)


def find_place():
    coef = lax.axis_index("coef")
    return lax.axis_index("tiles"), coef & 1, coef >> 1


def edges_of(cells):
    width = cells.shape[1]
    head, tail = cells[:, :EDGE], cells[:, width - EDGE :]
    lane = lax.broadcasted_iota(jnp.int32, head.shape, 1)
    return jnp.where(lane < EDGE // 2, head, tail)


def edge_parts(rows):
    return 2 if rows % 32 == 0 else 1


def pack_kernel(
    t_any, f_any, a_any, class_any, near_ref, both_ref, sent_ref, class_ref, t_ref, sems
):
    copies = [
        pltpu.make_async_copy(source, target, sems.at[at])
        for at, (source, target) in enumerate(
            (
                (t_any, t_ref),
                (f_any, both_ref.at[0]),
                (a_any, both_ref.at[1]),
                (class_any, class_ref),
            )
        )
    ]
    for copy in copies:
        copy.start()
    for copy in copies:
        copy.wait()
    count, rows, depth = t_ref.shape
    mats = count * rows
    fields, adjoints = both_ref[0], both_ref[1]
    own = edges_of(fields).astype(F32)
    turned = pltpu.roll(edges_of(adjoints).astype(F32), A_SHIFT, 1)
    class_edge = pltpu.roll(
        jnp.broadcast_to(edges_of(class_ref[...]).astype(F32), (rows, EDGE)), C_SHIFT, 1
    )
    lane = lax.broadcasted_iota(jnp.int32, own.shape, 1)
    edge = jnp.where(
        (lane < HW) | (lane >= EDGE - HW),
        own,
        jnp.where((lane >= A_SHIFT - HW) & (lane < A_SHIFT + HW), turned, class_edge),
    ).astype(BF16)
    parts = edge_parts(rows)
    base = mats + rows // parts
    near_ref[:mats, :] = t_ref[...].reshape(mats, depth)
    for part in range(depth // EDGE):
        start = part * (rows // parts) if part < parts else 0
        near_ref[mats:base, part * EDGE : (part + 1) * EDGE] = edge[start : start + base - mats, :]
    sent_ref[:rows, :] = fields
    sent_ref[rows : 2 * rows, :] = adjoints
    sent_ref[2 * rows :, :] = jnp.zeros_like(sent_ref[2 * rows :, :])


def relay_kernel(cross_ref, top_ref, far_ref, both_ref, beside_ref, near_ref, after_ref, out_ref):
    out_ref[0] = near_ref[...]
    out_ref[1] = top_ref[...]
    out_ref[2] = far_ref[...]
    out_ref[3] = cross_ref[...]


def pick_halo(place, pieces, mats, rows):
    tile = place[0]
    parts = edge_parts(rows)
    lane = lax.broadcasted_iota(jnp.int32, (rows, EDGE), 1)
    above = jnp.zeros((rows, EDGE), F32)
    below = jnp.zeros((rows, EDGE), F32)
    for piece_ref, at, mask in pieces:
        bands = [
            piece_ref[at, mats : mats + rows // parts, part * EDGE : (part + 1) * EDGE]
            for part in range(parts)
        ]
        cells = jnp.concatenate(bands, axis=0).astype(F32)
        owner = tile ^ mask
        above = jnp.where(owner == tile + 1, cells, above)
        below = jnp.where(owner == tile - 1, cells, below)
    return above, below


def join_halo(halo, shift):
    above, below = halo
    lane = lax.broadcasted_iota(jnp.int32, above.shape, 1)
    back = (EDGE - shift) % EDGE
    if back:
        above, below = pltpu.roll(above, back, 1), pltpu.roll(below, back, 1)
    return jnp.where(lane < EDGE // 2, above, below)


def find_pieces(spots, refs):
    return [[(refs[which], at, mask) for which, at, mask in group] for group in spots]


def fields_kernel(spots, count, both_ref, far_ref, *refs):
    place = find_place()
    (near, across), (out_ref, halos) = find_pieces(spots, refs[:-2]), refs[-2:]
    unused, rows, width = both_ref.shape
    mats = count * rows
    for start, source, pieces in ((place[1], both_ref[0], near), (1 - place[1], far_ref[:rows, :], across)):
        start = pl.multiple_of(start * rows, rows)
        for part in range(width // EDGE):
            lanes = slice(part * EDGE, (part + 1) * EDGE)
            out_ref[pl.ds(part * 2 * rows + start, rows), :] = source[:, lanes]
        halos[pl.ds(start, rows), :] = join_halo(pick_halo(place, pieces, mats, rows), 0)
    lane = lax.broadcasted_iota(jnp.int32, (LEAD, EDGE), 1)
    packed = jnp.zeros((LEAD, EDGE), F32)
    for group in range(2 * rows // LEAD):
        halo = halos[group * LEAD : (group + 1) * LEAD, :]
        narrow = jnp.where(lane < LEAD, halo, pltpu.roll(halo, 2 * LEAD, 1))
        first = 2 * LEAD * group
        moved = pltpu.roll(narrow, first, 1) if group else narrow
        packed = jnp.where((lane >= first) & (lane < first + 2 * LEAD), moved, packed)
    out_ref[2 * rows * (width // EDGE) :, :] = packed.astype(BF16)


def unpack_fields(piece_ref, padded, start, block):
    width = padded.shape[1] - EDGE
    for part in range(width // EDGE):
        lanes = slice(part * EDGE, (part + 1) * EDGE)
        padded[pl.ds(start, block), lanes] = piece_ref[part * block : (part + 1) * block, :]
    packed = piece_ref[block * (width // EDGE) :, :].astype(F32)
    lane = lax.broadcasted_iota(jnp.int32, (LEAD, EDGE), 1)
    for group in range(block // LEAD):
        narrow = pltpu.roll(packed, EDGE - 2 * LEAD * group, 1) if group else packed
        halo = jnp.where(lane < EDGE // 2, narrow, pltpu.roll(narrow, EDGE - 2 * LEAD, 1))
        padded[pl.ds(start + group * LEAD, LEAD), width:] = halo.astype(BF16)


def prepare_kernel(rows, couple_ref, links_ref, after_ref, mats_ref, own_ref, spread_ref, links, weights, sems):
    copies = []
    for chunk in range(SLOTS // CHUNK):
        span = pl.ds(chunk * CHUNK, CHUNK)
        copies.append(pltpu.make_async_copy(couple_ref.at[span], mats_ref.at[span], sems.at[chunk]))
    linked = pltpu.make_async_copy(links_ref, links, sems.at[len(copies)])
    linked.start()
    for copy in copies:
        copy.start()
    linked.wait()
    weights[...] = jnp.zeros_like(weights)
    weights[:SLOTS, :] = jnp.where(links[...] >= 0, 1.0, 0.0)
    filled = weights[...].astype(BF16)
    row = lax.broadcasted_iota(jnp.int32, (filled.shape[0], 2 * EDGE), 0)
    lane = lax.broadcasted_iota(jnp.int32, (filled.shape[0], 2 * EDGE), 1)
    for pair in range(SLOTS // 2):
        chosen = row == 2 * pair + (lane >= EDGE).astype(jnp.int32)
        unit = jnp.where(chosen, 1.0, 0.0).astype(BF16)
        spread = lax.dot_general(
            filled, unit, (((0,), (0,)), ((), ())), preferred_element_type=F32
        ).astype(BF16)
        spread_ref[2 * pair] = spread[:, :EDGE]
        spread_ref[2 * pair + 1] = spread[:, EDGE:]
    depth = mats_ref.shape[1]
    odd = find_place()[1]
    lane = lax.broadcasted_iota(jnp.int32, (depth, EDGE), 1)
    first = jnp.where((lane // rows) % 2 == odd, 1.0, 0.0).astype(BF16)
    second = (1.0 - first).astype(BF16)
    shift = jnp.where(odd == 1, EDGE - rows, rows)
    for chunk, copy in enumerate(copies):
        copy.wait()
        for mat in range(chunk * CHUNK, (chunk + 1) * CHUNK):
            moved = pltpu.roll(mats_ref[mat, :, EDGE : 2 * EDGE], shift, 1)
            chosen = mats_ref[mat, :, :EDGE] * first + moved * second
            slot = SLOTS - 1 - mat
            side = (slot % 2) * EDGE
            own_ref[slot // 2, :, side : side + EDGE] = chosen


def stand_up(cells, upright):
    width = cells.shape[1] - EDGE
    turned = cells.astype(F32).T
    for half in range(upright.shape[0]):
        lanes = slice(half * EDGE, (half + 1) * EDGE)
        upright[half, LEAD : LEAD + width, :] = turned[:width, lanes]
        upright[half, LEAD + width :, :] = turned[width : width + LEAD, lanes]
        upright[half, :LEAD, :] = turned[width + EDGE - LEAD :, lanes]


def couple_slots(upright, spread_ref, mats_ref, slots, total=None):
    width = spread_ref.shape[1]
    for slot in slots:
        start = LEAD + OFFSETS[slot]
        weight = spread_ref[slot]
        selected = jnp.concatenate(
            [
                upright[half, start : start + width, :].astype(BF16) * weight
                for half in range(upright.shape[0])
            ],
            axis=1,
        )
        product = lax.dot_general(
            selected, mats_ref[slot], (((1,), (1,)), ((), ())), preferred_element_type=F32
        )
        total = product if total is None else total + product
    return total


def couple_own(upright, spread_ref, own_ref, products):
    width = spread_ref.shape[1]
    for pair in range(SLOTS // 2):
        both = jnp.dot(upright, own_ref[pair], preferred_element_type=F32)
        products[2 * pair] = both[:, :EDGE]
        products[2 * pair + 1] = both[:, EDGE:]
    bands = []
    for band in range(0, width, BAND):
        total = None
        for slot in range(SLOTS):
            start = LEAD + OFFSETS[slot] + band
            term = products[slot, start : start + BAND, :] * spread_ref[slot, band : band + BAND, :].astype(F32)
            total = term if total is None else total + term
        bands.append(total)
    return jnp.concatenate(bands, axis=0)


def adjoint_kernel(
    spots, count, sends, both_ref, far_ref, class_ref, spread_ref, own_ref, after_ref, *refs
):
    place = find_place()
    near, across = find_pieces(spots, refs[: -sends - 4])
    keep_ref, *send_refs = refs[-sends - 4 : -4]
    total_ref, expanded, stacked, products = refs[-4:]
    unused, rows, width = both_ref.shape
    mats = count * rows
    halos = [pick_halo(place, pieces, mats, rows) for pieces in (near, across)]
    padded = [
        jnp.concatenate([own, join_halo(halo, A_SHIFT).astype(BF16)], axis=1)
        for own, halo in ((both_ref[1], halos[0]), (far_ref[rows : 2 * rows, :], halos[1]))
    ]
    class_halo = join_halo(tuple(cells[0:8, :] for cells in halos[0]), C_SHIFT)
    labels = jnp.concatenate([class_ref[...], class_halo[0:1, :].astype(jnp.int32)], axis=1)
    at = 0
    for own, pieces in zip(padded, (near, across)):
        for ref, spot, mask in pieces:
            stacked[at : at + mats, :] = ref[spot, :mats, :]
            for local_class in range(count):
                hit = labels == (place[0] ^ mask) * count + local_class
                factor = jnp.where(hit, 1.0, 0.0).astype(BF16)
                expanded[at : at + rows, :] = own * factor
                at += rows
    scattered = lax.dot_general(
        stacked[...], expanded[...], (((0,), (0,)), ((), ())), preferred_element_type=F32
    )
    turned = scattered.astype(BF16).T
    upright = jnp.concatenate(
        [turned[width + EDGE - LEAD :], turned[:width], turned[width : width + LEAD]], axis=0
    )
    total_ref[...] = couple_own(upright, spread_ref, own_ref, products).T

    def block(rel):
        start = ((place[2] ^ rel) * 2 + place[1]) * rows
        moved = start - EDGE + jnp.where(place[1] == 1, -rows, rows)
        return pl.ds(pl.multiple_of(jnp.where(start < EDGE, start, moved), rows), rows)

    keep_ref[...] = total_ref[block(0), :]
    for rel, send_ref in enumerate(send_refs, 1):
        send_ref[...] = total_ref[block(rel), :].astype(BF16)


def forward_kernel(
    spots, count, rels, both_ref, class_ref, spread_ref, mats_ref, *refs
):
    place = find_place()
    pieces, refs = refs[: len(rels)], refs[len(rels) :]
    (near, across), (out_ref, padded, upright, stacked) = find_pieces(spots, refs[:-4]), refs[-4:]
    unused, rows, width = both_ref.shape
    mats = count * rows
    block = 2 * rows
    for rel, piece_ref in zip(rels, pieces):
        start = pl.multiple_of((place[2] ^ rel) * block, block)
        unpack_fields(piece_ref, padded, start, block)
    stand_up(padded[...], upright)
    coupled = couple_slots(upright, spread_ref, mats_ref, range(SLOTS)).astype(BF16)
    for piece, (ref, spot, mask) in enumerate(near):
        stacked[piece * mats : (piece + 1) * mats, :] = ref[spot, :mats, :]
    product = lax.dot_general(
        stacked[...], coupled, (((1,), (1,)), ((), ())), preferred_element_type=F32
    )
    applied = jnp.zeros((rows, width), F32)
    labels = class_ref[...]
    for piece, (ref, spot, mask) in enumerate(near):
        for local_class in range(count):
            hit = labels == (place[0] ^ mask) * count + local_class
            at = piece * mats + local_class * rows
            applied = jnp.where(hit, product[at : at + rows, :], applied)
    out_ref[...] = (both_ref[0].astype(F32) - applied).astype(BF16)


def finish_kernel(both_ref, keep_ref, forward_ref, *refs):
    arrived, (out_ref, adjoint_ref) = refs[:-2], refs[-2:]
    out_ref[...] = forward_ref[...]
    returned = keep_ref[...]
    for ref in arrived:
        returned = returned + ref[...].astype(F32)
    adjoint_ref[...] = (both_ref[1].astype(F32) - returned).astype(BF16)


def local(fields, adjoints, couple, tmatrices, neighbours, classes):
    tiles, coefs = lax.axis_size("tiles"), lax.axis_size("coef")
    rows, width = fields.shape
    count, unused, depth = tmatrices.shape

    def swap(cells, tile_mask, coef_mask):
        pairs = [
            (i * coefs + j, (i ^ tile_mask) * coefs + (j ^ coef_mask))
            for i in range(tiles)
            for j in range(coefs)
        ]
        return lax.ppermute(cells, ("tiles", "coef"), pairs)

    labels = classes.reshape(1, width)
    mats = count * rows
    near_rows = mats + rows // edge_parts(rows)
    total_rows = couple.shape[1]
    near_own, both, sent_far, labels = pl.pallas_call(
        pack_kernel,
        out_shape=(
            jax.ShapeDtypeStruct((near_rows, depth), BF16),
            jax.ShapeDtypeStruct((2, rows, width), BF16),
            jax.ShapeDtypeStruct((2 * rows + LEAD, width), BF16),
            jax.ShapeDtypeStruct(labels.shape, jnp.int32),
        ),
        in_specs=[HBM] * 4,
        out_specs=(VMEM,) * 4,
        scratch_shapes=[pltpu.VMEM(tmatrices.shape, BF16), pltpu.SemaphoreType.DMA((4,))],
        compiler_params=PARAMS,
    )(*[in_hbm(cells) for cells in (tmatrices, fields, adjoints, labels)])
    mats_held, mats_own, spread = pl.pallas_call(
        functools.partial(prepare_kernel, rows),
        out_shape=(
            jax.ShapeDtypeStruct(couple.shape, BF16),
            jax.ShapeDtypeStruct((SLOTS // 2, total_rows, 2 * EDGE), BF16),
            jax.ShapeDtypeStruct((SLOTS, width, EDGE), BF16),
        ),
        in_specs=[HBM, HBM, VMEM],
        out_specs=(VMEM,) * 3,
        scratch_shapes=[
            pltpu.VMEM((SLOTS, width), jnp.int32),
            pltpu.VMEM((SLOTS + -SLOTS % 16, width), F32),
            pltpu.SemaphoreType.DMA((SLOTS // CHUNK + 1,)),
        ],
        cost_estimate=pl.CostEstimate(flops=0, bytes_accessed=4 * couple.size, transcendentals=0),
        compiler_params=PARAMS,
    )(in_hbm(couple), in_hbm(neighbours.T), labels)

    top = tiles // 2
    both_far = swap(sent_far, 0, 1)
    beside = swap(near_own, 1, 0)
    first = pl.pallas_call(
        relay_kernel,
        out_shape=jax.ShapeDtypeStruct((4, near_rows, depth), BF16),
        in_specs=[VMEM] * 7,
        out_specs=VMEM,
        compiler_params=PARAMS,
    )(
        swap(near_own, top ^ 1, 1),
        swap(near_own, top ^ 1, 0),
        swap(near_own, 1, 1),
        both_far,
        beside,
        near_own,
        mats_held,
    )
    held, lows = [first], [0]
    bit = top // 2
    while bit >= 1:
        held += [swap(block, bit, 0) for block in held]
        lows += [low ^ bit for low in lows]
        bit //= 2
    spots = (
        [(at, slot, low ^ (0, top ^ 1)[slot]) for at, low in enumerate(lows) for slot in (0, 1)],
        [(at, slot, low ^ (1, top ^ 1)[slot - 2]) for at, low in enumerate(lows) for slot in (2, 3)],
    )
    if tiles == 4:
        sources = [first, beside[None]]
        edge_spots = ([(0, 1, 3), (1, 0, 1)], [(0, 2, 1), (0, 3, 3)])
    else:
        sources, edge_spots = held, spots

    padded_fields = pl.pallas_call(
        functools.partial(fields_kernel, edge_spots, count),
        out_shape=jax.ShapeDtypeStruct((2 * rows * (width // EDGE) + LEAD, EDGE), BF16),
        in_specs=[VMEM] * (2 + len(sources)),
        out_specs=VMEM,
        scratch_shapes=[pltpu.VMEM((2 * rows, EDGE), F32)],
        compiler_params=PARAMS,
    )(both, both_far, *sources)

    groups = coefs // 2
    gathered = {0: padded_fields}
    for rel in range(1, groups):
        gathered[rel] = swap(padded_fields, 0, 2 * rel)
    rels = [0, 1, 3, 2] if groups == 4 else sorted(gathered)


    def work(slots):
        size = slots * total_rows * total_rows
        return pl.CostEstimate(flops=2 * size * width, bytes_accessed=2 * size, transcendentals=0)

    keep, *sent = pl.pallas_call(
        functools.partial(adjoint_kernel, spots, count, groups),
        out_shape=(jax.ShapeDtypeStruct((rows, width), F32),)
        + (jax.ShapeDtypeStruct((rows, width), BF16),) * (groups - 1),
        in_specs=[VMEM] * 5 + [ANY] + [VMEM] * len(held),
        out_specs=(VMEM,) * groups,
        scratch_shapes=[
            pltpu.VMEM((EDGE, width), F32),
            pltpu.VMEM((2 * tiles * mats, width + EDGE), BF16),
            pltpu.VMEM((2 * tiles * mats, depth), BF16),
            pltpu.VMEM((SLOTS, width + 2 * LEAD, EDGE), F32),
        ],
        cost_estimate=work(SLOTS + 8),
        compiler_params=PARAMS,
    )(both, both_far, labels, spread, mats_own, padded_fields, *held)
    arrived = [swap(block, 0, 2 * rel) for rel, block in enumerate(sent, 1)]

    forward = pl.pallas_call(
        functools.partial(forward_kernel, spots, count, rels),
        out_shape=jax.ShapeDtypeStruct((rows, width), BF16),
        in_specs=[VMEM] * (4 + len(rels) + len(held)),
        out_specs=VMEM,
        scratch_shapes=[
            pltpu.VMEM((total_rows, width + EDGE), BF16),
            pltpu.VMEM((total_rows // EDGE, width + 2 * LEAD, EDGE), F32),
            pltpu.VMEM((tiles * mats, depth), BF16),
        ],
        cost_estimate=work(SLOTS + 8),
        compiler_params=PARAMS,
    )(both, labels, spread, mats_held, *[gathered[rel] for rel in rels], *held)
    return pl.pallas_call(
        finish_kernel,
        out_shape=(jax.ShapeDtypeStruct((rows, width), BF16),) * 2,
        in_specs=[VMEM] * (3 + len(arrived)),
        out_specs=(VMEM, VMEM),
        compiler_params=PARAMS,
    )(both, keep, forward, *[arrived[k - 1] for k in ((3, 2, 1) if groups == 4 else range(1, groups))])


def solution(mesh):
    placed = (
        P("coef", "tiles"),
        P("coef", "tiles"),
        P(),
        P("tiles", "coef", None),
        P("tiles", None),
        P("tiles"),
    )
    return jax.shard_map(
        local,
        mesh=mesh,
        in_specs=placed,
        out_specs=(P("coef", "tiles"), P("coef", "tiles")),
        check_vma=False,
    )
```
